32 devices in a mesh: px: 8 (over y, x, core), py: 4 (over z).
Axes of the slice: x: 2, y: 2, z: 4, core: 2. Of those that a mesh axis runs over, the one named last changes fastest.
Arguments:
- currents_in: bfloat16 [16, 8, 2, 32, 512], P('px', 'py'), may hold values from -6 to 6
- rad_pattern: bfloat16 [2, 512, 512], replicated, may hold values from -0.1875 to 0.1875
- far_map: bfloat16 [512, 2048], replicated, may hold values from -0.25 to 0.25
- reflect: float32 [16, 8, 512], P('px', 'py'), may hold values from 0.2 to 0.7
- centres: float32 [3, 16, 8], P(None, 'px', 'py'), may hold values from -30 to 30
- spectral_dirs: float32 [3, 512], replicated, may hold values from -3 to 3
- receiver_dirs: float32 [3, 2048], replicated, may hold values from -3 to 3
- partners: int32 [16, 8, 12], P('px', 'py'), may hold values from 0 to 127, as said below
- partner_count: int32 [16, 8], P('px', 'py'), may hold values from 1 to 12, as said below
- pair_weight: bfloat16 [16, 8, 12], P('px', 'py'), may hold values from 0.29882812 to 1
Outputs:
- currents: bfloat16 [16, 8, 2, 32, 512], P('px', 'py')
- isar_image: float32 [32, 2048], P('py', 'px')
The draws below stay inside these ranges and needn't reach their ends.
Inputs may be any that keep to these rules, and one draw needn't show every extreme that they name: `partners`: the first partner_count entries of a patch's list are distinct patches other than itself, at most 1 patch rows away along the hull and, counting columns around the girth (column indices wrap modulo 8), at most 2 columns away; later entries are valid patch ids that are ignored. `partner_count`: some patch lists 12 partners.
All inputs are finite; a program needn't handle non-finite values.
Results may differ from the reference program's by a relative error of at most 0.019.
Values may be sent and summed in bfloat16 or wider, within the bound.
No kernel may reach another device: no remote copies, remote signals or barrier semaphores. Data moves between devices by JAX's collectives and lax.ppermute only.
A program may use at most 64 MiB of HBM per device.

```python
import math
import jax
import jax.numpy as jnp
from jax import lax

PR = 2
PC = 2
K = 32
B = 512
M = 512
R = 2048
SLOTS = 12
ROW_REACH = 1
COL_REACH = 2
NR = 16
NC = 8


def visibility(key):
    base = jax.random.fold_in(key, 4242)
    k_pick, k_band, k_low, k_high, k_row, k_col = jax.random.split(base, 6)
    offsets = [(a, b) for a in range(-ROW_REACH, ROW_REACH + 1) for b in range(-COL_REACH, COL_REACH + 1) if (a, b) != (0, 0)]
    row_shift = jnp.array([o[0] for o in offsets], jnp.int32)
    col_shift = jnp.array([o[1] for o in offsets], jnp.int32)
    n_offsets = len(offsets)
    row_ids = jnp.arange(NR, dtype=jnp.int32)[:, None, None]
    col_ids = jnp.arange(NC, dtype=jnp.int32)[None, :, None]
    target_row = row_ids + row_shift[None, None, :]
    usable = (target_row >= 0) & (target_row < NR)
    usable = jnp.broadcast_to(usable, (NR, NC, n_offsets))
    score = jax.random.randint(k_pick, (NR, NC, n_offsets), 0, 1 << 20) * 64 + jnp.arange(n_offsets, dtype=jnp.int32)
    score = jnp.where(usable, score, (1 << 27) + jnp.arange(n_offsets, dtype=jnp.int32))
    order = jnp.argsort(score, axis=-1, stable=True)[..., :SLOTS]
    pick_row = jnp.clip(jnp.take(row_shift, order) + row_ids, 0, NR - 1)
    pick_col = (jnp.take(col_shift, order) + col_ids) % NC
    partner_ids = pick_row * NC + pick_col
    blocks = jax.random.randint(k_band, (NR // PR, NC // PC), 0, 4)
    busy = jnp.repeat(jnp.repeat(blocks, PR, axis=0), PC, axis=1) == 3
    low_count = jax.random.randint(k_low, (NR, NC), 1, 6)
    high_count = jax.random.randint(k_high, (NR, NC), 8, SLOTS + 1)
    wanted = jnp.where(busy, high_count, low_count)
    wanted = jnp.minimum(wanted, jnp.sum(usable.astype(jnp.int32), axis=-1))
    force_row = jax.random.randint(k_row, (), ROW_REACH, NR - ROW_REACH)
    force_col = jax.random.randint(k_col, (), 0, NC)
    hit = (row_ids[:, :, 0] == force_row) & (col_ids[:, :, 0] == force_col)
    counts = jnp.where(hit, SLOTS, wanted)
    return (counts.astype(jnp.int32), partner_ids.astype(jnp.int32))


def draw_partners(key, part):
    return visibility(key)[1]


def draw_partner_count(key, part):
    return visibility(key)[0]


def shard_levels(own_key, extent, cuts, smallest, largest):
    gain = 1.0
    for position, shards_of in cuts:
        draws = jax.random.uniform(jax.random.fold_in(jax.random.fold_in(own_key, 6), position), (shards_of,), jnp.float32, smallest / len(cuts), largest / len(cuts))
        gain = gain * jnp.repeat(jnp.exp(draws), extent[position] // shards_of).reshape((-1,) + (1,) * (len(extent) - 1 - position))
    return gain


def noise(key, dims, width, most, cuts=(), held_as=jnp.bfloat16):
    entries = width * jax.random.normal(key, dims, jnp.float32)
    if cuts:
        entries = entries * shard_levels(key, dims, cuts, -0.22, 0.18)
    return jnp.clip(entries, -most, most).astype(held_as)


def setup_inputs(seed: int = 0) -> dict:
    arg_keys = jax.random.split(jax.random.key(seed), 11)
    currents_in = noise(arg_keys[0], (NR, NC, 2, K, B), 1.0, 6.0, ((0, 8), (1, 4)))
    rad_pattern = noise(arg_keys[1], (2, B, M), (2 * B) ** -0.5, 0.1875)
    far_map = noise(arg_keys[2], (M, R), M ** -0.5, 0.25)
    reflect = jnp.clip(0.2 + 0.5 * jax.random.uniform(arg_keys[3], (NR, NC, B), jnp.float32) ** shard_levels(arg_keys[3], (NR, NC, B), ((0, 8), (1, 4)), -0.2, 0.2), 0.2, 0.7)
    centres = jnp.clip(jax.random.uniform(arg_keys[4], (3, NR, NC), jnp.float32, -30.0, 30.0) * shard_levels(arg_keys[4], (3, NR, NC), ((1, 8), (2, 4)), -0.4, 0.0), -30.0, 30.0)
    spectral_dirs = noise(arg_keys[5], (3, M), 0.6, 3.0, (), jnp.float32)
    receiver_dirs = noise(arg_keys[6], (3, R), 0.6, 3.0, (), jnp.float32)
    partners = draw_partners(jax.random.fold_in(arg_keys[10], 71), 0)
    partner_count = draw_partner_count(jax.random.fold_in(arg_keys[10], 71), 0)
    pair_weight = jnp.clip(0.29882812 + 0.7011719 * jax.random.uniform(arg_keys[9], (NR, NC, SLOTS), jnp.float32) ** shard_levels(arg_keys[9], (NR, NC, SLOTS), ((0, 8), (1, 4)), -0.2, 0.2), 0.29882812, 1.0).astype(jnp.bfloat16)
    return dict(currents_in=currents_in, rad_pattern=rad_pattern, far_map=far_map, reflect=reflect, centres=centres, spectral_dirs=spectral_dirs, receiver_dirs=receiver_dirs, partners=partners, partner_count=partner_count, pair_weight=pair_weight)


def angles(dirs, centres):
    return jnp.einsum('dm,dab->abm', dirs, centres, precision=lax.Precision.HIGHEST)

def matmul(left, right):
    return jnp.dot(left, right, preferred_element_type=jnp.float32)

def radiate(currents, rad_pattern):
    flat_re = currents[:, :, 0].reshape(-1, B)
    flat_im = currents[:, :, 1].reshape(-1, B)
    spec_re = matmul(flat_re, rad_pattern[0]) - matmul(flat_im, rad_pattern[1])
    spec_im = matmul(flat_re, rad_pattern[1]) + matmul(flat_im, rad_pattern[0])
    return (spec_re.reshape(NR, NC, K, M), spec_im.reshape(NR, NC, K, M))

def bounce(current_now, currents_in, rad_pattern, reflect, phi, partners, partner_count, pair_weight):
    spec_re, spec_im = radiate(current_now, rad_pattern)
    cosine = jnp.cos(phi)[:, :, None, :]
    sine_part = jnp.sin(phi)[:, :, None, :]
    out_re = spec_re * cosine + spec_im * sine_part
    out_im = spec_im * cosine - spec_re * sine_part
    outgoing = jnp.stack([out_re, out_im], axis=2).astype(jnp.bfloat16)
    patch_total = NR * NC
    flat_out = outgoing.reshape(patch_total, 2 * K * M)
    list_ids = partners.reshape(patch_total, SLOTS).astype(jnp.int32)
    live = jnp.arange(SLOTS, dtype=jnp.int32)[None, :] < partner_count.reshape(patch_total, 1)
    weights = jnp.where(live, pair_weight.reshape(patch_total, SLOTS).astype(jnp.float32), jnp.float32(0.0))

    def step(running, slot_id):
        picked = jnp.take(flat_out, list_ids[:, slot_id], axis=0).astype(jnp.float32)
        return (running + weights[:, slot_id][:, None] * picked, None)
    start = jnp.zeros((patch_total, 2 * K * M), jnp.float32)
    collected, _ = lax.scan(step, start, jnp.arange(SLOTS, dtype=jnp.int32))
    collected = collected.reshape(NR, NC, 2, K, M)
    col_re, col_im = (collected[:, :, 0], collected[:, :, 1])
    arr_re = (col_re * cosine - col_im * sine_part).astype(jnp.bfloat16).reshape(-1, M)
    arr_im = (col_re * sine_part + col_im * cosine).astype(jnp.bfloat16).reshape(-1, M)
    recv_re = matmul(arr_re, rad_pattern[0].T) - matmul(arr_im, rad_pattern[1].T)
    recv_im = matmul(arr_re, rad_pattern[1].T) + matmul(arr_im, rad_pattern[0].T)
    received = jnp.stack([recv_re.reshape(NR, NC, K, B), recv_im.reshape(NR, NC, K, B)], axis=2)
    updated = currents_in.astype(jnp.float32) + reflect[:, :, None, None, :] * received
    return updated.astype(jnp.bfloat16)

def reference(currents_in, rad_pattern, far_map, reflect, centres, spectral_dirs, receiver_dirs, partners, partner_count, pair_weight):
    phi = angles(spectral_dirs, centres)
    current_now = currents_in
    for bounce_id in range(2):
        current_now = bounce(current_now, currents_in, rad_pattern, reflect, phi, partners, partner_count, pair_weight)
    spec_re, spec_im = radiate(current_now, rad_pattern)
    spec_re = spec_re.astype(jnp.bfloat16)
    spec_im = spec_im.astype(jnp.bfloat16)
    view = angles(receiver_dirs, centres)

    def row_step(running, pieces):
        row_re, row_im, row_view = pieces
        beam_re = matmul(row_re.reshape(-1, M), far_map).reshape(NC, K, R)
        beam_im = matmul(row_im.reshape(-1, M), far_map).reshape(NC, K, R)
        cos_view = jnp.cos(row_view)[:, None, :]
        sin_view = jnp.sin(row_view)[:, None, :]
        far_re = lax.optimization_barrier(jnp.sum(beam_re * cos_view - beam_im * sin_view, axis=0))
        far_im = lax.optimization_barrier(jnp.sum(beam_re * sin_view + beam_im * cos_view, axis=0))
        return ((running[0] + far_re, running[1] + far_im), None)
    start = (jnp.zeros((K, R), jnp.float32), jnp.zeros((K, R), jnp.float32))
    (far_re, far_im), _ = lax.scan(row_step, start, (spec_re, spec_im, view))
    factor = 1.0 / math.sqrt(NR * NC)
    far_re = far_re * factor
    far_im = far_im * factor
    rcv_ids = jnp.arange(R, dtype=jnp.int32)[:, None]
    bin_ids = jnp.arange(R, dtype=jnp.int32)[None, :]
    turn_angle = (rcv_ids * bin_ids % R).astype(jnp.float32) * (2.0 * math.pi / R)
    norm_factor = 1.0 / math.sqrt(R)
    cos_table = jnp.cos(turn_angle) * norm_factor
    sin_table = jnp.sin(turn_angle) * norm_factor
    high = lax.Precision.HIGHEST
    image_re = jnp.dot(far_re, cos_table, precision=high) + jnp.dot(far_im, sin_table, precision=high)
    image_im = jnp.dot(far_im, cos_table, precision=high) - jnp.dot(far_re, sin_table, precision=high)
    isar_image = 0.125 * (image_re * image_re + image_im * image_im)
    return (current_now, isar_image)
```

```python
import functools
import math

import jax
import jax.numpy as jnp
import numpy as np
from jax import lax
from jax.experimental import pallas as pl
from jax.experimental.pallas import tpu as pltpu
from jax.sharding import PartitionSpec as P

SLOTS = 12
ROW_REACH = 1
COL_REACH = 2
OFFSETS = [
    (a, b)
    for a in range(-ROW_REACH, ROW_REACH + 1)
    for b in range(-COL_REACH, COL_REACH + 1)
]
F32 = jnp.float32
BF16 = jnp.bfloat16
HIGH = lax.Precision.HIGHEST
VMEM_LIMIT = 48 * 1024 * 1024


def padded(block, sides, width, periodic):
    for axis, dim in sides:
        count = lax.axis_size(axis)
        forward = [(i, i + 1) for i in range(count - 1)]
        if periodic:
            forward.append((count - 1, 0))
        backward = [(target, source) for source, target in forward]
        low = lax.ppermute(
            lax.slice_in_dim(block, block.shape[dim] - width, None, axis=dim), axis, forward
        )
        high = lax.ppermute(lax.slice_in_dim(block, 0, width, axis=dim), axis, backward)
        block = jnp.concatenate([low, block, high], axis=dim)
    return block


def combined(rad_pattern):
    upper = jnp.concatenate([rad_pattern[0], rad_pattern[1]], axis=1)
    lower = jnp.concatenate([-rad_pattern[1], rad_pattern[0]], axis=1)
    return jnp.concatenate([upper, lower], axis=0)


def radiate(currents, rad_big):
    row_count, col_count, _, illum_count, unit_count = currents.shape
    stacked = jnp.concatenate([currents[:, :, 0], currents[:, :, 1]], axis=-1)
    flat_rows = stacked.reshape(row_count * col_count * illum_count, 2 * unit_count)
    spectra = jnp.dot(flat_rows, rad_big, preferred_element_type=F32)
    return spectra.reshape(row_count, col_count, illum_count, -1)


def receive(arriving, rad_big):
    row_count, col_count, illum_count, double = arriving.shape
    flat_rows = arriving.reshape(-1, double)
    answer = lax.dot_general(
        flat_rows, rad_big, (((1,), (1,)), ((), ())), preferred_element_type=F32
    )
    return answer.reshape(row_count, col_count, illum_count, -1)


def partner_sum(halo_flat, slot_index, weights):
    height = halo_flat.shape[0]
    onehot = slot_index[:, :, None] == jnp.arange(height, dtype=jnp.int32)[None, None, :]
    coef = jnp.sum(jnp.where(onehot, weights[:, :, None].astype(F32), 0.0), axis=1).astype(BF16)
    return jnp.dot(coef, halo_flat, preferred_element_type=F32)


def bounce(current_now, currents_in, rad_big, reflect, cosine, sine_part, plan):
    row_count, col_count, _, illum_count, unit_count = current_now.shape
    spectra = radiate(current_now, rad_big)
    half_width = spectra.shape[-1] // 2
    spec_re = spectra[..., :half_width]
    spec_im = spectra[..., half_width:]
    out_re = spec_re * cosine + spec_im * sine_part
    out_im = spec_im * cosine - spec_re * sine_part
    outgoing = jnp.stack([out_re, out_im], axis=2).astype(BF16)
    girth_block = padded(outgoing, (("py", 1),), COL_REACH, True)
    slot_index, weights = plan
    rim_block = padded(girth_block, (("px", 0),), ROW_REACH, False)
    halo_flat = rim_block.reshape(-1, 2 * illum_count * half_width)
    collected = partner_sum(halo_flat, slot_index, weights)
    collected = collected.reshape(row_count, col_count, 2, illum_count, half_width)
    col_re = collected[:, :, 0]
    col_im = collected[:, :, 1]
    arr_re = col_re * cosine - col_im * sine_part
    arr_im = col_re * sine_part + col_im * cosine
    arriving = jnp.concatenate([arr_re, -arr_im], axis=-1).astype(BF16)
    answer = receive(arriving, rad_big)
    received = jnp.stack([answer[..., :unit_count], -answer[..., unit_count:]], axis=2)
    updated = currents_in.astype(F32) + reflect[:, :, None, None, :] * received
    return updated.astype(BF16)


def patch_sharded(
    currents_in,
    rad_pattern,
    far_map,
    reflect,
    centres,
    spectral_dirs,
    receiver_dirs,
    partners,
    partner_count,
    pair_weight,
):
    row_count, col_count = partner_count.shape
    high = HIGH
    rad_big = combined(rad_pattern)
    phi = jnp.einsum("dm,dab->abm", spectral_dirs, centres, precision=high)
    cosine = jnp.cos(phi)[:, :, None, :]
    sine_part = jnp.sin(phi)[:, :, None, :]
    total_cols = col_count * lax.axis_size("py")
    total_rows = row_count * lax.axis_size("px")
    base_row = lax.axis_index("px") * row_count
    base_col = lax.axis_index("py") * col_count
    across = col_count + 2 * COL_REACH
    local_col = jnp.arange(col_count, dtype=jnp.int32)[None, :, None]
    live = jnp.arange(SLOTS, dtype=jnp.int32)[None, None, :] < partner_count[:, :, None]
    masked_weight = jnp.where(live, pair_weight, jnp.zeros_like(pair_weight))
    part_row = partners // total_cols
    part_col = partners % total_cols
    near_row = part_row - base_row
    near_col = (part_col - base_col - local_col + COL_REACH) % total_cols + local_col
    slot_index = ((near_row + ROW_REACH) * across + near_col).reshape(row_count * col_count, SLOTS)
    weights = masked_weight.reshape(row_count * col_count, SLOTS)
    plan = (slot_index, weights)
    current_now = currents_in
    for bounce_id in range(2):
        current_now = bounce(current_now, currents_in, rad_big, reflect, cosine, sine_part, plan)
    spectra = radiate(current_now, rad_big).astype(BF16)
    illum_count = spectra.shape[2]
    dir_count = far_map.shape[0]
    rcv_count = far_map.shape[1]
    beams = jnp.dot(spectra.reshape(-1, dir_count), far_map, preferred_element_type=F32)
    beams = beams.reshape(row_count, col_count, illum_count, 2, rcv_count)
    view = jnp.einsum("dr,dab->abr", receiver_dirs, centres, precision=high)
    cos_view = jnp.cos(view)[:, :, None, :]
    sin_view = jnp.sin(view)[:, :, None, :]
    beam_re = beams[:, :, :, 0]
    beam_im = beams[:, :, :, 1]
    far_re = jnp.sum(beam_re * cos_view - beam_im * sin_view, axis=(0, 1))
    far_im = jnp.sum(beam_re * sin_view + beam_im * cos_view, axis=(0, 1))
    factor = 1.0 / math.sqrt(total_rows * total_cols)
    far_part = jnp.stack([far_re, far_im]) * factor
    owned_far = lax.psum(
        lax.psum_scatter(far_part.astype(BF16), "py", scatter_dimension=1, tiled=True), "px"
    ).astype(F32)
    bin_width = rcv_count // lax.axis_size("px")
    rcv_ids = jnp.arange(rcv_count, dtype=jnp.int32)[:, None]
    bin_ids = lax.axis_index("px") * bin_width + jnp.arange(bin_width, dtype=jnp.int32)[None, :]
    turn_angle = (rcv_ids * bin_ids % rcv_count).astype(F32) * (2.0 * math.pi / rcv_count)
    norm_factor = 1.0 / math.sqrt(rcv_count)
    cos_table = jnp.cos(turn_angle) * norm_factor
    sin_table = jnp.sin(turn_angle) * norm_factor
    image_re = jnp.dot(owned_far[0], cos_table, precision=high) + jnp.dot(
        owned_far[1], sin_table, precision=high
    )
    image_im = jnp.dot(owned_far[1], cos_table, precision=high) - jnp.dot(
        owned_far[0], sin_table, precision=high
    )
    isar_image = 0.125 * (image_re * image_re + image_im * image_im)
    return (current_now, isar_image)


def turn_polynomials():
    grid = np.linspace(0.0, 0.25, 4001)
    safe = np.where(grid > 0, np.sqrt(grid), 1.0)
    sine_over = np.where(grid > 0, np.sin(2 * np.pi * safe) / safe, 2 * np.pi)
    cosine = np.cos(2 * np.pi * np.sqrt(grid))
    make = np.polynomial.chebyshev.Chebyshev.fit
    power = np.polynomial.Polynomial
    sine_fit = make(grid, sine_over, 6).convert(kind=power).coef
    cosine_fit = make(grid, cosine, 7).convert(kind=power).coef
    return [float(c) for c in sine_fit], [float(c) for c in cosine_fit]


SINE_FIT, COSINE_FIT = turn_polynomials()


def horner(coefs, x):
    value = jnp.full_like(x, coefs[-1])
    for c in coefs[-2::-1]:
        value = value * x + c
    return value


def cos_sin(turns):
    frac = turns - jnp.floor(turns + 0.5)
    square = frac * frac
    return horner(COSINE_FIT, square), frac * horner(SINE_FIT, square)


def dot(left, right):
    return jnp.dot(left, right, preferred_element_type=F32)


def dot_t(left, right):
    return lax.dot_general(left, right, (((1,), (1,)), ((), ())), preferred_element_type=F32)


def one_hot_rows(sources):
    table = np.zeros((len(sources), len(sources)), np.float32)
    table[np.arange(len(sources)), sources] = 1.0
    return table


def pack_kernel(
    rows, total_cols, base, cur, order, reflect, weight, partners, count, centres, out
):
    local_rows, local_cols, unit_count = reflect.shape
    local = local_rows * local_cols
    half = unit_count // 2
    width = unit_count + half
    out[:, :unit_count] = dot(order[...], cur[...]).astype(BF16)
    refl = reflect[...].reshape(local, unit_count)
    refl = jnp.concatenate([refl[:, :half], refl[:, half:]], axis=0)
    lane = lax.broadcasted_iota(jnp.int32, (local, 128), 1)
    row = lax.broadcasted_iota(jnp.int32, (local, 128), 0)
    patch_row = base[0] + row // local_cols
    patch_col = base[1] + row % local_cols
    target = jnp.full((local, 128), -1, jnp.int32)
    for o, (a, b) in enumerate(OFFSETS):
        col = patch_col + b
        col = jnp.where(col < 0, col + total_cols, col)
        col = jnp.where(col >= total_cols, col - total_cols, col)
        target = jnp.where(lane == o, (patch_row + a) * total_cols + col, target)
    small = jnp.zeros((local, 128), F32)
    for r in range(local_rows):
        for c in range(local_cols):
            here = row == r * local_cols + c
            for s in range(SLOTS):
                w = jnp.where(s < count[r, c], weight[r, c, s], 0.0)
                small = small + jnp.where(here & (target == partners[r, c, s]), w, 0.0)
    spot = jnp.zeros((local, 128), F32)
    first = len(OFFSETS)
    for d in range(3):
        in_place = (lane >= first + 3 * d) & (lane < first + 3 * d + 3)
        for r in range(local_rows):
            for c in range(local_cols):
                here = row == r * local_cols + c
                spot = jnp.where(in_place & here, centres[d, r, c], spot)
    top = spot.astype(BF16).astype(F32)
    rest = spot - top
    middle = rest.astype(BF16).astype(F32)
    bottom = rest - middle
    term = lane - first
    term = term - jnp.where(term >= 6, 6, jnp.where(term >= 3, 3, 0))
    parts = jnp.where(term == 0, top, jnp.where(term == 1, middle, bottom))
    small = jnp.where((lane >= first) & (lane < first + 9), parts, small)
    small = jnp.concatenate([small, jnp.zeros_like(small)], axis=0)
    tail = jnp.concatenate([refl, small], axis=1)
    tail = jnp.concatenate([tail, tail], axis=0).astype(BF16)
    step = tail.shape[0]
    for s in range(rows // step):
        out[step * s : step * (s + 1), unit_count:] = tail


def main_kernel(
    scale,
    splits,
    got,
    order,
    back,
    offset_of,
    spectral_dirs,
    receiver_dirs,
    short_cos,
    short_sin,
    twist_cos,
    twist_sin,
    long_table,
    rad_hbm,
    far_hbm,
    out,
    rad,
    far_map,
    rad_sem,
    far_sem,
):
    rad_copy = pltpu.make_async_copy(rad_hbm, rad, rad_sem)
    far_copy = pltpu.make_async_copy(far_hbm, far_map, far_sem)
    rad_copy.start()
    far_copy.start()
    unit_count = rad.shape[1]
    half = unit_count // 2
    patches = got.shape[0] // 2
    sorted_rows = dot(order[...], got[...])
    start = sorted_rows[:, :unit_count]
    reflect = jnp.concatenate(
        [
            sorted_rows[:patches, unit_count : unit_count + half],
            sorted_rows[patches:, unit_count : unit_count + half],
        ],
        axis=1,
    )
    small = sorted_rows[:patches, unit_count + half :]
    first = len(OFFSETS)
    centre = []
    for d in range(3):
        at = first + 3 * d
        value = small[:, at : at + 1] + small[:, at + 1 : at + 2] + small[:, at + 2 : at + 3]
        centre.append(value * (0.5 / math.pi))

    def turns(dirs):
        return centre[0] * dirs[0:1] + centre[1] * dirs[1:2] + centre[2] * dirs[2:3]

    coef = jnp.zeros((patches, patches), F32)
    offsets = offset_of[...]
    for o in range(len(OFFSETS)):
        coef = coef + jnp.where(offsets == o, small[:, o : o + 1], 0.0)
    coef = coef.astype(BF16)
    cosine, sine = cos_sin(turns(spectral_dirs[...]))
    rad_copy.wait()

    def spectrum(current):
        first_part = dot(current, rad[0])
        second_part = dot(current, rad[1])
        return (
            first_part[:patches] - second_part[patches:],
            second_part[:patches] + first_part[patches:],
        )

    current = start.astype(BF16)
    for _ in range(2):
        spec_re, spec_im = spectrum(current)
        outgoing = jnp.concatenate(
            [spec_re * cosine + spec_im * sine, spec_im * cosine - spec_re * sine], axis=1
        ).astype(BF16)
        collected = dot(coef, outgoing)
        width = collected.shape[1] // 2
        col_re = collected[:, :width]
        col_im = collected[:, width:]
        arriving = jnp.concatenate(
            [col_re * cosine - col_im * sine, col_re * sine + col_im * cosine], axis=0
        ).astype(BF16)
        first_part = dot_t(arriving, rad[0])
        second_part = dot_t(arriving, rad[1])
        recv_re = first_part[:patches] - second_part[patches:]
        recv_im = second_part[:patches] + first_part[patches:]
        current = jnp.concatenate(
            [start[:patches] + reflect * recv_re, start[patches:] + reflect * recv_im], axis=0
        ).astype(BF16)
    out[:, :unit_count] = dot(back[...], current).astype(BF16)

    spec_re, spec_im = spectrum(current)
    final = jnp.concatenate([spec_re, spec_im], axis=0).astype(BF16)
    far_copy.wait()
    tile = far_map.shape[1] // splits
    far_re, far_im = [], []
    for t in range(splits):
        beams = dot(final, far_map[:, tile * t : tile * (t + 1)])
        cos_view, sin_view = cos_sin(turns(receiver_dirs[:, tile * t : tile * (t + 1)]))
        beam_re = beams[:patches]
        beam_im = beams[patches:]
        far_re.append(jnp.sum(beam_re * cos_view - beam_im * sin_view, axis=0, keepdims=True))
        far_im.append(jnp.sum(beam_re * sin_view + beam_im * cos_view, axis=0, keepdims=True))
    mid_re = jnp.zeros((splits, tile), F32)
    mid_im = jnp.zeros((splits, tile), F32)
    for t in range(splits):
        c = short_cos[:, t : t + 1]
        s = short_sin[:, t : t + 1]
        mid_re = mid_re + (c * far_re[t] + s * far_im[t])
        mid_im = mid_im + (c * far_im[t] - s * far_re[t])
    tw_re = mid_re * twist_cos[...] + mid_im * twist_sin[...]
    tw_im = mid_im * twist_cos[...] - mid_re * twist_sin[...]
    both = jnp.concatenate([tw_re, tw_im], axis=0)
    answer = jnp.dot(both, long_table[...], precision=HIGH, preferred_element_type=F32)
    image_re = answer[:splits, :tile] + answer[splits:, tile:]
    image_im = answer[splits:, :tile] - answer[:splits, tile:]
    image = (scale * (image_re * image_re + image_im * image_im)).astype(BF16)
    pieces = tile // 128
    rows_each = out.shape[0] // pieces
    for p in range(pieces):
        piece = image[:, 128 * p : 128 * (p + 1)].astype(F32)
        piece = jnp.concatenate([piece, piece], axis=0).astype(BF16)
        for s in range(rows_each // piece.shape[0]):
            at = p * rows_each + s * piece.shape[0]
            out[at : at + piece.shape[0], unit_count:] = piece


def unpack_kernel(per_row, place, got, order, currents, image):
    unit_count = currents.shape[1]
    currents[...] = dot(order[...], got[:, :unit_count]).astype(BF16)
    splits = 8
    owned, bins = image.shape
    height = owned * splits
    at = pl.multiple_of(place[1] * height, height)
    block = got[pl.ds(at, height), unit_count:]
    each = bins // splits
    lane = lax.broadcasted_iota(jnp.int32, (128, bins), 0)
    column = lax.broadcasted_iota(jnp.int32, (128, bins), 1)
    pick = jnp.where(lane == place[0] * each + column // splits, 1.0, 0.0).astype(BF16)
    spread = dot(block, pick)
    row = lax.broadcasted_iota(jnp.int32, (height, bins), 0)
    column = lax.broadcasted_iota(jnp.int32, (height, bins), 1)
    spread = jnp.where(row % splits == column % splits, spread, 0.0)
    image[...] = jnp.sum(spread.reshape(owned, splits, bins), axis=1)


def params():
    return pltpu.CompilerParams(vmem_limit_bytes=VMEM_LIMIT)


def whole(memory_space):
    return pl.BlockSpec(memory_space=memory_space)


def illumination_sharded(
    currents_in,
    rad_pattern,
    far_map,
    reflect,
    centres,
    spectral_dirs,
    receiver_dirs,
    partners,
    partner_count,
    pair_weight,
):
    local_rows, local_cols, _, illum_count, unit_count = currents_in.shape
    n_px, n_py = lax.axis_size("px"), lax.axis_size("py")
    devices = n_px * n_py
    local = local_rows * local_cols
    rows = 2 * local * illum_count
    total_cols = local_cols * n_py
    total_rows = local_rows * n_px
    patches = total_rows * total_cols
    rcv_count = far_map.shape[1]
    block = 2 * local

    ids = np.arange(rows).reshape(local, 2, illum_count)
    to_send = np.ascontiguousarray(ids.transpose(2, 1, 0)).reshape(-1)
    send_table = one_hot_rows(to_send)
    ids = np.arange(rows).reshape(devices, 2, local)
    to_sort = np.ascontiguousarray(ids.transpose(1, 0, 2)).reshape(-1)
    sort_table = one_hot_rows(to_sort)

    patch = np.arange(patches)
    device, within = patch // local, patch % local
    patch_row = device // n_py * local_rows + within // local_cols
    patch_col = device % n_py * local_cols + within % local_cols
    offset_of = np.full((patches, patches), -1, np.int32)
    for o, (a, b) in enumerate(OFFSETS):
        match = (patch_row[None, :] - patch_row[:, None] == a) & (
            (patch_col[None, :] - patch_col[:, None] - b) % total_cols == 0
        )
        offset_of[match] = o

    splits = n_px
    tile = rcv_count // splits
    short = 2 * np.pi / splits * (np.arange(splits)[:, None] * np.arange(splits)[None, :] % splits)
    twist = 2 * np.pi / rcv_count * (np.arange(splits)[:, None] * np.arange(tile)[None, :])
    long = 2 * np.pi / tile * (np.arange(tile)[:, None] * np.arange(tile)[None, :] % tile)
    long_table = np.concatenate([np.cos(long), np.sin(long)], axis=1)

    vmem, smem, anywhere = pltpu.VMEM, pltpu.SMEM, pl.ANY
    base = jnp.stack([lax.axis_index("px") * local_rows, lax.axis_index("py") * local_cols])
    sent_width = unit_count + unit_count // 2 + 128
    packed = pl.pallas_call(
        functools.partial(pack_kernel, rows, total_cols),
        out_shape=jax.ShapeDtypeStruct((rows, sent_width), BF16),
        in_specs=[whole(m) for m in (smem, vmem, vmem, vmem, smem, smem, smem, smem)],
        out_specs=whole(vmem),
        compiler_params=params(),
        name="pack",
    )(
        base.astype(jnp.int32),
        currents_in.reshape(rows, unit_count),
        jnp.asarray(send_table, BF16),
        reflect,
        pair_weight.astype(F32),
        partners,
        partner_count,
        centres,
    )
    axes = ("px", "py")
    got = lax.all_to_all(packed.reshape(devices, block, sent_width), axes, 0, 0, tiled=True)

    scale = 0.125 / (patches * rcv_count)
    back_width = unit_count + 128
    answer = pl.pallas_call(
        functools.partial(main_kernel, scale, splits),
        out_shape=jax.ShapeDtypeStruct((rows, back_width), BF16),
        in_specs=[whole(vmem)] * 11 + [whole(anywhere)] * 2,
        out_specs=whole(vmem),
        scratch_shapes=[
            pltpu.VMEM(rad_pattern.shape, BF16),
            pltpu.VMEM(far_map.shape, BF16),
            pltpu.SemaphoreType.DMA,
            pltpu.SemaphoreType.DMA,
        ],
        compiler_params=params(),
        name="bounces",
    )(
        got.reshape(rows, sent_width),
        jnp.asarray(sort_table, BF16),
        jnp.asarray(sort_table.T, BF16),
        jnp.asarray(offset_of),
        spectral_dirs,
        receiver_dirs,
        jnp.asarray(np.cos(short), F32),
        jnp.asarray(np.sin(short), F32),
        jnp.asarray(np.cos(twist), F32),
        jnp.asarray(np.sin(twist), F32),
        jnp.asarray(long_table, F32),
        rad_pattern,
        far_map,
    )
    back = lax.all_to_all(answer.reshape(devices, block, back_width), axes, 0, 0, tiled=True)

    owned = illum_count // n_py
    per_row = 128 // (tile // splits)
    place = jnp.stack([lax.axis_index("px") % per_row, lax.axis_index("py")]).astype(jnp.int32)
    currents, image = pl.pallas_call(
        functools.partial(unpack_kernel, per_row),
        out_shape=(
            jax.ShapeDtypeStruct((rows, unit_count), BF16),
            jax.ShapeDtypeStruct((owned, tile), F32),
        ),
        in_specs=[whole(m) for m in (smem, vmem, vmem)],
        out_specs=(whole(vmem), whole(vmem)),
        compiler_params=params(),
        name="unpack",
    )(place, back.reshape(rows, back_width), jnp.asarray(send_table.T, BF16))
    return (currents.reshape(currents_in.shape), image)


def fits(mesh):
    def check(currents_in, far_map):
        n_px, n_py = mesh.shape["px"], mesh.shape["py"]
        total_rows, total_cols, _, illum_count, unit_count = currents_in.shape
        local = (total_rows // n_px) * (total_cols // n_py)
        return (
            illum_count == n_px * n_py
            and local == 4
            and n_px == 8
            and unit_count % 256 == 0
            and far_map.shape[1] == n_px * 256
            and illum_count % n_py == 0
            and total_cols > 2 * COL_REACH
        )

    return check


def solution(mesh):
    in_specs = (
        P("px", "py", None, None, None),
        P(),
        P(),
        P("px", "py", None),
        P(None, "px", "py"),
        P(),
        P(),
        P("px", "py", None),
        P("px", "py"),
        P("px", "py", None),
    )
    out_specs = (P("px", "py", None, None, None), P("py", "px"))
    check = fits(mesh)

    def run(*args):
        local = illumination_sharded if check(args[0], args[2]) else patch_sharded
        mapped = jax.shard_map(
            local, mesh=mesh, in_specs=in_specs, out_specs=out_specs, check_vma=False
        )
        return mapped(*args)

    return run
```

```python
import functools
import math

import jax
import jax.numpy as jnp
import numpy as np
from jax import lax
from jax.experimental import pallas as pl
from jax.experimental.pallas import tpu as pltpu
from jax.sharding import PartitionSpec as P

SLOTS = 12
ROW_REACH = 1
COL_REACH = 2
OFFSETS = [
    (a, b)
    for a in range(-ROW_REACH, ROW_REACH + 1)
    for b in range(-COL_REACH, COL_REACH + 1)
]
F32 = jnp.float32
BF16 = jnp.bfloat16
HIGH = lax.Precision.HIGHEST
VMEM_LIMIT = 62 * 1024 * 1024


def padded(block, sides, width, periodic):
    for axis, dim in sides:
        count = lax.axis_size(axis)
        forward = [(i, i + 1) for i in range(count - 1)]
        if periodic:
            forward.append((count - 1, 0))
        backward = [(target, source) for source, target in forward]
        low = lax.ppermute(
            lax.slice_in_dim(block, block.shape[dim] - width, None, axis=dim), axis, forward
        )
        high = lax.ppermute(lax.slice_in_dim(block, 0, width, axis=dim), axis, backward)
        block = jnp.concatenate([low, block, high], axis=dim)
    return block


def combined(rad_pattern):
    upper = jnp.concatenate([rad_pattern[0], rad_pattern[1]], axis=1)
    lower = jnp.concatenate([-rad_pattern[1], rad_pattern[0]], axis=1)
    return jnp.concatenate([upper, lower], axis=0)


def radiate(currents, rad_big):
    row_count, col_count, _, illum_count, unit_count = currents.shape
    stacked = jnp.concatenate([currents[:, :, 0], currents[:, :, 1]], axis=-1)
    flat_rows = stacked.reshape(row_count * col_count * illum_count, 2 * unit_count)
    spectra = jnp.dot(flat_rows, rad_big, preferred_element_type=F32)
    return spectra.reshape(row_count, col_count, illum_count, -1)


def receive(arriving, rad_big):
    row_count, col_count, illum_count, double = arriving.shape
    flat_rows = arriving.reshape(-1, double)
    answer = lax.dot_general(
        flat_rows, rad_big, (((1,), (1,)), ((), ())), preferred_element_type=F32
    )
    return answer.reshape(row_count, col_count, illum_count, -1)


def partner_sum(halo_flat, slot_index, weights):
    height = halo_flat.shape[0]
    onehot = slot_index[:, :, None] == jnp.arange(height, dtype=jnp.int32)[None, None, :]
    coef = jnp.sum(jnp.where(onehot, weights[:, :, None].astype(F32), 0.0), axis=1).astype(BF16)
    return jnp.dot(coef, halo_flat, preferred_element_type=F32)


def bounce(current_now, currents_in, rad_big, reflect, cosine, sine_part, plan):
    row_count, col_count, _, illum_count, unit_count = current_now.shape
    spectra = radiate(current_now, rad_big)
    half_width = spectra.shape[-1] // 2
    spec_re = spectra[..., :half_width]
    spec_im = spectra[..., half_width:]
    out_re = spec_re * cosine + spec_im * sine_part
    out_im = spec_im * cosine - spec_re * sine_part
    outgoing = jnp.stack([out_re, out_im], axis=2).astype(BF16)
    girth_block = padded(outgoing, (("py", 1),), COL_REACH, True)
    slot_index, weights = plan
    rim_block = padded(girth_block, (("px", 0),), ROW_REACH, False)
    halo_flat = rim_block.reshape(-1, 2 * illum_count * half_width)
    collected = partner_sum(halo_flat, slot_index, weights)
    collected = collected.reshape(row_count, col_count, 2, illum_count, half_width)
    col_re = collected[:, :, 0]
    col_im = collected[:, :, 1]
    arr_re = col_re * cosine - col_im * sine_part
    arr_im = col_re * sine_part + col_im * cosine
    arriving = jnp.concatenate([arr_re, -arr_im], axis=-1).astype(BF16)
    answer = receive(arriving, rad_big)
    received = jnp.stack([answer[..., :unit_count], -answer[..., unit_count:]], axis=2)
    updated = currents_in.astype(F32) + reflect[:, :, None, None, :] * received
    return updated.astype(BF16)


def patch_sharded(
    currents_in,
    rad_pattern,
    far_map,
    reflect,
    centres,
    spectral_dirs,
    receiver_dirs,
    partners,
    partner_count,
    pair_weight,
):
    row_count, col_count = partner_count.shape
    high = HIGH
    rad_big = combined(rad_pattern)
    phi = jnp.einsum("dm,dab->abm", spectral_dirs, centres, precision=high)
    cosine = jnp.cos(phi)[:, :, None, :]
    sine_part = jnp.sin(phi)[:, :, None, :]
    total_cols = col_count * lax.axis_size("py")
    total_rows = row_count * lax.axis_size("px")
    base_row = lax.axis_index("px") * row_count
    base_col = lax.axis_index("py") * col_count
    across = col_count + 2 * COL_REACH
    local_col = jnp.arange(col_count, dtype=jnp.int32)[None, :, None]
    live = jnp.arange(SLOTS, dtype=jnp.int32)[None, None, :] < partner_count[:, :, None]
    masked_weight = jnp.where(live, pair_weight, jnp.zeros_like(pair_weight))
    part_row = partners // total_cols
    part_col = partners % total_cols
    near_row = part_row - base_row
    near_col = (part_col - base_col - local_col + COL_REACH) % total_cols + local_col
    slot_index = ((near_row + ROW_REACH) * across + near_col).reshape(row_count * col_count, SLOTS)
    weights = masked_weight.reshape(row_count * col_count, SLOTS)
    plan = (slot_index, weights)
    current_now = currents_in
    for bounce_id in range(2):
        current_now = bounce(current_now, currents_in, rad_big, reflect, cosine, sine_part, plan)
    spectra = radiate(current_now, rad_big).astype(BF16)
    illum_count = spectra.shape[2]
    dir_count = far_map.shape[0]
    rcv_count = far_map.shape[1]
    beams = jnp.dot(spectra.reshape(-1, dir_count), far_map, preferred_element_type=F32)
    beams = beams.reshape(row_count, col_count, illum_count, 2, rcv_count)
    view = jnp.einsum("dr,dab->abr", receiver_dirs, centres, precision=high)
    cos_view = jnp.cos(view)[:, :, None, :]
    sin_view = jnp.sin(view)[:, :, None, :]
    beam_re = beams[:, :, :, 0]
    beam_im = beams[:, :, :, 1]
    far_re = jnp.sum(beam_re * cos_view - beam_im * sin_view, axis=(0, 1))
    far_im = jnp.sum(beam_re * sin_view + beam_im * cos_view, axis=(0, 1))
    factor = 1.0 / math.sqrt(total_rows * total_cols)
    far_part = jnp.stack([far_re, far_im]) * factor
    owned_far = lax.psum(
        lax.psum_scatter(far_part.astype(BF16), "py", scatter_dimension=1, tiled=True), "px"
    ).astype(F32)
    bin_width = rcv_count // lax.axis_size("px")
    rcv_ids = jnp.arange(rcv_count, dtype=jnp.int32)[:, None]
    bin_ids = lax.axis_index("px") * bin_width + jnp.arange(bin_width, dtype=jnp.int32)[None, :]
    turn_angle = (rcv_ids * bin_ids % rcv_count).astype(F32) * (2.0 * math.pi / rcv_count)
    norm_factor = 1.0 / math.sqrt(rcv_count)
    cos_table = jnp.cos(turn_angle) * norm_factor
    sin_table = jnp.sin(turn_angle) * norm_factor
    image_re = jnp.dot(owned_far[0], cos_table, precision=high) + jnp.dot(
        owned_far[1], sin_table, precision=high
    )
    image_im = jnp.dot(owned_far[1], cos_table, precision=high) - jnp.dot(
        owned_far[0], sin_table, precision=high
    )
    isar_image = 0.125 * (image_re * image_re + image_im * image_im)
    return (current_now, isar_image)


def turn_polynomials():
    grid = np.linspace(0.0, 0.25, 4001)
    safe = np.where(grid > 0, np.sqrt(grid), 1.0)
    sine_over = np.where(grid > 0, np.sin(2 * np.pi * safe) / safe, 2 * np.pi)
    cosine = np.cos(2 * np.pi * np.sqrt(grid))
    make = np.polynomial.chebyshev.Chebyshev.fit
    power = np.polynomial.Polynomial
    sine_fit = make(grid, sine_over, 6).convert(kind=power).coef
    cosine_fit = make(grid, cosine, 7).convert(kind=power).coef
    return [float(c) for c in sine_fit], [float(c) for c in cosine_fit]


SINE_FIT, COSINE_FIT = turn_polynomials()


def horner(coefs, x):
    value = jnp.full_like(x, coefs[-1])
    for c in coefs[-2::-1]:
        value = value * x + c
    return value


def cos_sin(turns):
    frac = turns - jnp.floor(turns + 0.5)
    square = frac * frac
    return horner(COSINE_FIT, square), frac * horner(SINE_FIT, square)


def dot(left, right):
    return jnp.dot(left, right, preferred_element_type=F32)


def dot_t(left, right):
    return lax.dot_general(left, right, (((1,), (1,)), ((), ())), preferred_element_type=F32)


def sorter(rows, outer, inner):
    out_id = lax.broadcasted_iota(jnp.int32, (rows, rows), 0)
    in_id = lax.broadcasted_iota(jnp.int32, (rows, rows), 1)
    i = out_id // (2 * outer)
    part = (out_id // outer) % 2
    o = out_id % outer
    return jnp.where(in_id == (o * 2 + part) * inner + i, 1.0, 0.0).astype(BF16)


def part_sorter(rows, inner, back):
    first = lax.broadcasted_iota(jnp.int32, (rows, rows), 1 if back else 0)
    second = lax.broadcasted_iota(jnp.int32, (rows, rows), 0 if back else 1)
    half = rows // 2
    part = first // half
    o = (first % half) // inner
    i = first % inner
    return jnp.where(second == (o * 2 + part) * inner + i, 1.0, 0.0).astype(BF16)


def fetch(pairs, sems):
    copies = [
        pltpu.make_async_copy(source, target, sems.at[n])
        for n, (source, target) in enumerate(pairs)
    ]
    for copy in copies:
        copy.start()
    return copies


def pack_kernel(
    total_cols,
    cur_hbm,
    reflect_hbm,
    weight_hbm,
    partners_hbm,
    count_hbm,
    centres_hbm,
    out,
    cur,
    reflect,
    weight,
    partners,
    count,
    centres,
    sems,
):
    copies = fetch(
        [
            (partners_hbm, partners),
            (weight_hbm, weight),
            (count_hbm, count),
            (centres_hbm, centres),
            (reflect_hbm, reflect),
            (cur_hbm, cur),
        ],
        sems,
    )
    rows = cur.shape[0]
    local_rows, local_cols, unit_count = reflect.shape
    local = local_rows * local_cols
    half = unit_count // 2
    base_row = lax.axis_index("px") * local_rows
    base_col = lax.axis_index("py") * local_cols
    order = sorter(rows, local, rows // (2 * local))
    lane = lax.broadcasted_iota(jnp.int32, (local, 128), 1)
    row = lax.broadcasted_iota(jnp.int32, (local, 128), 0)
    patch_row = base_row + row // local_cols
    patch_col = base_col + row % local_cols
    target = jnp.full((local, 128), -1, jnp.int32)
    for o, (a, b) in enumerate(OFFSETS):
        col = patch_col + b
        col = jnp.where(col < 0, col + total_cols, col)
        col = jnp.where(col >= total_cols, col - total_cols, col)
        target = jnp.where(lane == o, (patch_row + a) * total_cols + col, target)
    for copy in copies[:5]:
        copy.wait()
    ids = partners[...].reshape(local, SLOTS)
    weights = weight[...].astype(F32).reshape(local, SLOTS)
    spots = centres[...].reshape(local, 3)
    counts = count[...]
    live = jnp.zeros((local, 128), jnp.int32)
    for r in range(local_rows):
        for c in range(local_cols):
            live = jnp.where(row == r * local_cols + c, counts[r : r + 1, c : c + 1], live)
    small = jnp.zeros((local, 128), F32)
    for s in range(SLOTS):
        hit = (ids[:, s : s + 1] == target) & (live > s)
        small = small + jnp.where(hit, weights[:, s : s + 1], 0.0)
    first = len(OFFSETS)
    for d in range(3):
        spot = spots[:, d : d + 1]
        top = spot.astype(BF16).astype(F32)
        rest = spot - top
        middle = rest.astype(BF16).astype(F32)
        small = jnp.where(lane == first + 3 * d, top, small)
        small = jnp.where(lane == first + 3 * d + 1, middle, small)
        small = jnp.where(lane == first + 3 * d + 2, rest - middle, small)
    refl = reflect[...].reshape(local, unit_count)
    refl = jnp.concatenate([refl[:, :half], refl[:, half:]], axis=0)
    small = jnp.concatenate([small, jnp.zeros_like(small)], axis=0)
    tail = jnp.concatenate([refl, small], axis=1)
    tail = jnp.concatenate([tail, tail], axis=0).astype(BF16)
    step = tail.shape[0]
    for s in range(rows // step):
        out[step * s : step * (s + 1), unit_count:] = tail
    copies[5].wait()
    out[:, :unit_count] = dot(order, cur[...]).astype(BF16)


def table_kernel(long_table):
    tile = long_table.shape[0]
    row = lax.broadcasted_iota(jnp.int32, (tile, tile), 0)
    column = lax.broadcasted_iota(jnp.int32, (tile, tile), 1)
    cosine, sine = cos_sin(((row * column) % tile).astype(F32) * (1.0 / tile))
    long_table[:, :tile] = cosine
    long_table[:, tile:] = sine


def main_kernel(
    scale,
    grid_shape,
    local_shape,
    got,
    long_table,
    spectral_hbm,
    receiver_hbm,
    rad_hbm,
    far_hbm,
    out,
    spectral_dirs,
    receiver_dirs,
    rad,
    far_map,
    sems,
):
    copies = fetch(
        [
            (spectral_hbm, spectral_dirs),
            (rad_hbm, rad),
            (receiver_hbm, receiver_dirs),
            (far_hbm, far_map),
        ],
        sems,
    )
    unit_count = rad.shape[1]
    half = unit_count // 2
    rows = got.shape[0]
    patches = rows // 2
    local_rows, local_cols = local_shape
    local = local_rows * local_cols
    splits, n_py = grid_shape
    total_cols = n_py * local_cols
    sorted_rows = dot(part_sorter(rows, local, False), got[...])
    start = sorted_rows[:, :unit_count]
    reflect = jnp.concatenate(
        [
            sorted_rows[:patches, unit_count : unit_count + half],
            sorted_rows[patches:, unit_count : unit_count + half],
        ],
        axis=1,
    )
    small = sorted_rows[:patches, unit_count + half :]
    first = len(OFFSETS)
    centre = []
    for d in range(3):
        at = first + 3 * d
        value = small[:, at : at + 1] + small[:, at + 1 : at + 2] + small[:, at + 2 : at + 3]
        centre.append(value * (0.5 / math.pi))

    def turns(dirs):
        return centre[0] * dirs[0:1] + centre[1] * dirs[1:2] + centre[2] * dirs[2:3]

    def place(axis):
        ids = lax.broadcasted_iota(jnp.int32, (patches, patches), axis)
        device, within = ids // local, ids % local
        return (
            device // n_py * local_rows + within // local_cols,
            device % n_py * local_cols + within % local_cols,
        )

    (here_row, here_col), (there_row, there_col) = place(0), place(1)
    down = there_row - here_row
    across = there_col - here_col
    across = jnp.where(across > COL_REACH, across - total_cols, across)
    across = jnp.where(across < -COL_REACH, across + total_cols, across)
    near = (down >= -ROW_REACH) & (down <= ROW_REACH)
    near = near & (across >= -COL_REACH) & (across <= COL_REACH)
    offset = (down + ROW_REACH) * (2 * COL_REACH + 1) + across + COL_REACH
    offset = jnp.where(near, offset, -1)
    coef = jnp.zeros((patches, patches), F32)
    for o in range(len(OFFSETS)):
        coef = jnp.where(offset == o, small[:, o : o + 1], coef)
    coef = coef.astype(BF16)
    copies[0].wait()
    cosine, sine = cos_sin(turns(spectral_dirs[...]))
    copies[1].wait()

    def spectrum(current):
        first_part = dot(current, rad[0])
        second_part = dot(current, rad[1])
        return (
            first_part[:patches] - second_part[patches:],
            second_part[:patches] + first_part[patches:],
        )

    current = start.astype(BF16)
    for _ in range(2):
        spec_re, spec_im = spectrum(current)
        outgoing = jnp.concatenate(
            [spec_re * cosine + spec_im * sine, spec_im * cosine - spec_re * sine], axis=1
        ).astype(BF16)
        collected = dot(coef, outgoing)
        width = collected.shape[1] // 2
        col_re = collected[:, :width]
        col_im = collected[:, width:]
        arriving = jnp.concatenate(
            [col_re * cosine - col_im * sine, col_re * sine + col_im * cosine], axis=0
        ).astype(BF16)
        first_part = dot_t(arriving, rad[0])
        second_part = dot_t(arriving, rad[1])
        recv_re = first_part[:patches] - second_part[patches:]
        recv_im = second_part[:patches] + first_part[patches:]
        current = jnp.concatenate(
            [start[:patches] + reflect * recv_re, start[patches:] + reflect * recv_im], axis=0
        ).astype(BF16)
    out[:, :unit_count] = dot(part_sorter(rows, local, True), current).astype(BF16)

    spec_re, spec_im = spectrum(current)
    final = jnp.concatenate([spec_re, spec_im], axis=0).astype(BF16)
    copies[2].wait()
    copies[3].wait()
    tile = far_map.shape[1] // splits
    far_re, far_im = [], []
    for t in range(splits):
        beams = dot(final, far_map[:, tile * t : tile * (t + 1)])
        cos_view, sin_view = cos_sin(turns(receiver_dirs[:, tile * t : tile * (t + 1)]))
        beam_re = beams[:patches]
        beam_im = beams[patches:]
        far_re.append(jnp.sum(beam_re * cos_view - beam_im * sin_view, axis=0, keepdims=True))
        far_im.append(jnp.sum(beam_re * sin_view + beam_im * cos_view, axis=0, keepdims=True))
    row = lax.broadcasted_iota(jnp.int32, (splits, 128), 0)
    column = lax.broadcasted_iota(jnp.int32, (splits, 128), 1)
    short_cos, short_sin = cos_sin((row * column % splits).astype(F32) * (1.0 / splits))
    row = lax.broadcasted_iota(jnp.int32, (splits, tile), 0)
    column = lax.broadcasted_iota(jnp.int32, (splits, tile), 1)
    twist_cos, twist_sin = cos_sin((row * column).astype(F32) * (1.0 / (splits * tile)))
    mid_re = jnp.zeros((splits, tile), F32)
    mid_im = jnp.zeros((splits, tile), F32)
    for t in range(splits):
        c = short_cos[:, t : t + 1]
        s = short_sin[:, t : t + 1]
        mid_re = mid_re + (c * far_re[t] + s * far_im[t])
        mid_im = mid_im + (c * far_im[t] - s * far_re[t])
    tw_re = mid_re * twist_cos + mid_im * twist_sin
    tw_im = mid_im * twist_cos - mid_re * twist_sin
    both = jnp.concatenate([tw_re, tw_im], axis=0)
    answer = jnp.dot(both, long_table[...], precision=HIGH, preferred_element_type=F32)
    image_re = answer[:splits, :tile] + answer[splits:, tile:]
    image_im = answer[splits:, :tile] - answer[:splits, tile:]
    image = scale * (image_re * image_re + image_im * image_im)
    pieces = tile // 128
    rows_each = rows // pieces
    for p in range(pieces):
        piece = image[:, 128 * p : 128 * (p + 1)]
        piece = jnp.concatenate([piece, piece], axis=0).astype(BF16)
        for s in range(rows_each // piece.shape[0]):
            at = p * rows_each + s * piece.shape[0]
            out[at : at + piece.shape[0], unit_count:] = piece


def unpack_kernel(splits, local, got, currents, image):
    rows, unit_count = currents.shape
    order = sorter(rows, rows // (2 * local), local)
    currents[...] = dot(order, got[:, :unit_count]).astype(BF16)
    owned, bins = image.shape
    height = owned * splits
    each = bins // splits
    at = pl.multiple_of(lax.axis_index("py") * height, height)
    lanes_from = lax.axis_index("px") % (128 // each) * each
    block = got[pl.ds(at, height), unit_count:]
    lane = lax.broadcasted_iota(jnp.int32, (128, bins), 0)
    column = lax.broadcasted_iota(jnp.int32, (128, bins), 1)
    pick = jnp.where(lane == lanes_from + column // splits, 1.0, 0.0).astype(BF16)
    spread = dot(block, pick)
    row = lax.broadcasted_iota(jnp.int32, (height, bins), 0)
    column = lax.broadcasted_iota(jnp.int32, (height, bins), 1)
    spread = jnp.where(row % splits == column % splits, spread, 0.0)
    image[...] = jnp.sum(spread.reshape(owned, splits, bins), axis=1)


def call(kernel, name, outs, operands, spaces, scratch=(), cost=None):
    vmem = pl.BlockSpec(memory_space=pltpu.VMEM)
    return pl.pallas_call(
        kernel,
        out_shape=outs,
        in_specs=[pl.BlockSpec(memory_space=m) for m in spaces],
        out_specs=jax.tree.map(lambda _: vmem, outs),
        scratch_shapes=list(scratch),
        compiler_params=pltpu.CompilerParams(vmem_limit_bytes=VMEM_LIMIT),
        cost_estimate=cost,
        name=name,
    )(*operands)


def illumination_sharded(
    currents_in,
    rad_pattern,
    far_map,
    reflect,
    centres,
    spectral_dirs,
    receiver_dirs,
    partners,
    partner_count,
    pair_weight,
):
    local_rows, local_cols, _, illum_count, unit_count = currents_in.shape
    n_px, n_py = lax.axis_size("px"), lax.axis_size("py")
    devices = n_px * n_py
    local = local_rows * local_cols
    rows = 2 * local * illum_count
    total_cols = local_cols * n_py
    patches = local_rows * n_px * total_cols
    rcv_count = far_map.shape[1]
    tile = rcv_count // n_px
    block = 2 * local
    axes = ("px", "py")
    vmem, hbm = pltpu.VMEM, pltpu.HBM

    def like(array):
        return pltpu.VMEM(array.shape, array.dtype)

    sent_width = unit_count + unit_count // 2 + 128
    sources = (
        currents_in.reshape(rows, unit_count),
        reflect,
        pair_weight,
        partners,
        partner_count,
        jnp.transpose(centres, (1, 2, 0)),
    )
    packed = call(
        functools.partial(pack_kernel, total_cols),
        "pack",
        jax.ShapeDtypeStruct((rows, sent_width), BF16),
        sources,
        [hbm] * 6,
        [like(s) for s in sources] + [pltpu.SemaphoreType.DMA((6,))],
    )
    got = lax.all_to_all(packed.reshape(devices, block, sent_width), axes, 0, 0, tiled=True)
    long_table = call(
        table_kernel,
        "table",
        jax.ShapeDtypeStruct((tile, 2 * tile), F32),
        (),
        [],
        cost=pl.CostEstimate(flops=10**7, bytes_accessed=10**6, transcendentals=0),
    )
    scale = 0.125 / (patches * rcv_count)
    back_width = unit_count + 128
    answer = call(
        functools.partial(main_kernel, scale, (n_px, n_py), (local_rows, local_cols)),
        "bounces",
        jax.ShapeDtypeStruct((rows, back_width), BF16),
        (
            got.reshape(rows, sent_width),
            long_table,
            spectral_dirs,
            receiver_dirs,
            rad_pattern,
            far_map,
        ),
        [vmem] * 2 + [hbm] * 4,
        [like(a) for a in (spectral_dirs, receiver_dirs, rad_pattern, far_map)]
        + [pltpu.SemaphoreType.DMA((4,))],
    )
    back = lax.all_to_all(answer.reshape(devices, block, back_width), axes, 0, 0, tiled=True)
    owned = illum_count // n_py
    currents, image = call(
        functools.partial(unpack_kernel, n_px, local),
        "unpack",
        (
            jax.ShapeDtypeStruct((rows, unit_count), BF16),
            jax.ShapeDtypeStruct((owned, tile), F32),
        ),
        (back.reshape(rows, back_width),),
        [vmem],
    )
    return (currents.reshape(currents_in.shape), image)


def fits(mesh):
    def check(currents_in, far_map):
        n_px, n_py = mesh.shape["px"], mesh.shape["py"]
        total_rows, total_cols, _, illum_count, unit_count = currents_in.shape
        local = (total_rows // n_px) * (total_cols // n_py)
        return (
            illum_count == n_px * n_py
            and local == 4
            and n_px == 8
            and unit_count % 256 == 0
            and far_map.shape[1] == n_px * 256
            and illum_count % n_py == 0
            and total_cols > 2 * COL_REACH
        )

    return check


def solution(mesh):
    in_specs = (
        P("px", "py", None, None, None),
        P(),
        P(),
        P("px", "py", None),
        P(None, "px", "py"),
        P(),
        P(),
        P("px", "py", None),
        P("px", "py"),
        P("px", "py", None),
    )
    out_specs = (P("px", "py", None, None, None), P("py", "px"))
    check = fits(mesh)

    def run(*args):
        local = illumination_sharded if check(args[0], args[2]) else patch_sharded
        mapped = jax.shard_map(
            local, mesh=mesh, in_specs=in_specs, out_specs=out_specs, check_vma=False
        )
        return mapped(*args)

    return run
```

```python
import functools
import math

import jax
import jax.numpy as jnp
import numpy as np
from jax import lax
from jax.experimental import pallas as pl
from jax.experimental.pallas import tpu as pltpu
from jax.sharding import PartitionSpec as P

SLOTS = 12
ROW_REACH = 1
COL_REACH = 2
OFFSETS = [
    (a, b)
    for a in range(-ROW_REACH, ROW_REACH + 1)
    for b in range(-COL_REACH, COL_REACH + 1)
]
F32 = jnp.float32
BF16 = jnp.bfloat16
HIGH = lax.Precision.HIGHEST
MIB = 1024 * 1024


def padded(block, sides, width, periodic):
    for axis, dim in sides:
        count = lax.axis_size(axis)
        forward = [(i, i + 1) for i in range(count - 1)]
        if periodic:
            forward.append((count - 1, 0))
        backward = [(target, source) for source, target in forward]
        low = lax.ppermute(
            lax.slice_in_dim(block, block.shape[dim] - width, None, axis=dim), axis, forward
        )
        high = lax.ppermute(lax.slice_in_dim(block, 0, width, axis=dim), axis, backward)
        block = jnp.concatenate([low, block, high], axis=dim)
    return block


def combined(rad_pattern):
    upper = jnp.concatenate([rad_pattern[0], rad_pattern[1]], axis=1)
    lower = jnp.concatenate([-rad_pattern[1], rad_pattern[0]], axis=1)
    return jnp.concatenate([upper, lower], axis=0)


def radiate(currents, rad_big):
    row_count, col_count, _, illum_count, unit_count = currents.shape
    stacked = jnp.concatenate([currents[:, :, 0], currents[:, :, 1]], axis=-1)
    flat_rows = stacked.reshape(row_count * col_count * illum_count, 2 * unit_count)
    spectra = jnp.dot(flat_rows, rad_big, preferred_element_type=F32)
    return spectra.reshape(row_count, col_count, illum_count, -1)


def receive(arriving, rad_big):
    row_count, col_count, illum_count, double = arriving.shape
    flat_rows = arriving.reshape(-1, double)
    answer = lax.dot_general(
        flat_rows, rad_big, (((1,), (1,)), ((), ())), preferred_element_type=F32
    )
    return answer.reshape(row_count, col_count, illum_count, -1)


def partner_sum(halo_flat, slot_index, weights):
    height = halo_flat.shape[0]
    onehot = slot_index[:, :, None] == jnp.arange(height, dtype=jnp.int32)[None, None, :]
    coef = jnp.sum(jnp.where(onehot, weights[:, :, None].astype(F32), 0.0), axis=1).astype(BF16)
    return jnp.dot(coef, halo_flat, preferred_element_type=F32)


def bounce(current_now, currents_in, rad_big, reflect, cosine, sine_part, plan):
    row_count, col_count, _, illum_count, unit_count = current_now.shape
    spectra = radiate(current_now, rad_big)
    half_width = spectra.shape[-1] // 2
    spec_re = spectra[..., :half_width]
    spec_im = spectra[..., half_width:]
    out_re = spec_re * cosine + spec_im * sine_part
    out_im = spec_im * cosine - spec_re * sine_part
    outgoing = jnp.stack([out_re, out_im], axis=2).astype(BF16)
    girth_block = padded(outgoing, (("py", 1),), COL_REACH, True)
    slot_index, weights = plan
    rim_block = padded(girth_block, (("px", 0),), ROW_REACH, False)
    halo_flat = rim_block.reshape(-1, 2 * illum_count * half_width)
    collected = partner_sum(halo_flat, slot_index, weights)
    collected = collected.reshape(row_count, col_count, 2, illum_count, half_width)
    col_re = collected[:, :, 0]
    col_im = collected[:, :, 1]
    arr_re = col_re * cosine - col_im * sine_part
    arr_im = col_re * sine_part + col_im * cosine
    arriving = jnp.concatenate([arr_re, -arr_im], axis=-1).astype(BF16)
    answer = receive(arriving, rad_big)
    received = jnp.stack([answer[..., :unit_count], -answer[..., unit_count:]], axis=2)
    updated = currents_in.astype(F32) + reflect[:, :, None, None, :] * received
    return updated.astype(BF16)


def patch_sharded(
    currents_in,
    rad_pattern,
    far_map,
    reflect,
    centres,
    spectral_dirs,
    receiver_dirs,
    partners,
    partner_count,
    pair_weight,
):
    row_count, col_count = partner_count.shape
    high = HIGH
    rad_big = combined(rad_pattern)
    phi = jnp.einsum("dm,dab->abm", spectral_dirs, centres, precision=high)
    cosine = jnp.cos(phi)[:, :, None, :]
    sine_part = jnp.sin(phi)[:, :, None, :]
    total_cols = col_count * lax.axis_size("py")
    total_rows = row_count * lax.axis_size("px")
    base_row = lax.axis_index("px") * row_count
    base_col = lax.axis_index("py") * col_count
    across = col_count + 2 * COL_REACH
    local_col = jnp.arange(col_count, dtype=jnp.int32)[None, :, None]
    live = jnp.arange(SLOTS, dtype=jnp.int32)[None, None, :] < partner_count[:, :, None]
    masked_weight = jnp.where(live, pair_weight, jnp.zeros_like(pair_weight))
    part_row = partners // total_cols
    part_col = partners % total_cols
    near_row = part_row - base_row
    near_col = (part_col - base_col - local_col + COL_REACH) % total_cols + local_col
    slot_index = ((near_row + ROW_REACH) * across + near_col).reshape(row_count * col_count, SLOTS)
    weights = masked_weight.reshape(row_count * col_count, SLOTS)
    plan = (slot_index, weights)
    current_now = currents_in
    for bounce_id in range(2):
        current_now = bounce(current_now, currents_in, rad_big, reflect, cosine, sine_part, plan)
    spectra = radiate(current_now, rad_big).astype(BF16)
    illum_count = spectra.shape[2]
    dir_count = far_map.shape[0]
    rcv_count = far_map.shape[1]
    beams = jnp.dot(spectra.reshape(-1, dir_count), far_map, preferred_element_type=F32)
    beams = beams.reshape(row_count, col_count, illum_count, 2, rcv_count)
    view = jnp.einsum("dr,dab->abr", receiver_dirs, centres, precision=high)
    cos_view = jnp.cos(view)[:, :, None, :]
    sin_view = jnp.sin(view)[:, :, None, :]
    beam_re = beams[:, :, :, 0]
    beam_im = beams[:, :, :, 1]
    far_re = jnp.sum(beam_re * cos_view - beam_im * sin_view, axis=(0, 1))
    far_im = jnp.sum(beam_re * sin_view + beam_im * cos_view, axis=(0, 1))
    factor = 1.0 / math.sqrt(total_rows * total_cols)
    far_part = jnp.stack([far_re, far_im]) * factor
    owned_far = lax.psum(
        lax.psum_scatter(far_part.astype(BF16), "py", scatter_dimension=1, tiled=True), "px"
    ).astype(F32)
    bin_width = rcv_count // lax.axis_size("px")
    rcv_ids = jnp.arange(rcv_count, dtype=jnp.int32)[:, None]
    bin_ids = lax.axis_index("px") * bin_width + jnp.arange(bin_width, dtype=jnp.int32)[None, :]
    turn_angle = (rcv_ids * bin_ids % rcv_count).astype(F32) * (2.0 * math.pi / rcv_count)
    norm_factor = 1.0 / math.sqrt(rcv_count)
    cos_table = jnp.cos(turn_angle) * norm_factor
    sin_table = jnp.sin(turn_angle) * norm_factor
    image_re = jnp.dot(owned_far[0], cos_table, precision=high) + jnp.dot(
        owned_far[1], sin_table, precision=high
    )
    image_im = jnp.dot(owned_far[1], cos_table, precision=high) - jnp.dot(
        owned_far[0], sin_table, precision=high
    )
    isar_image = 0.125 * (image_re * image_re + image_im * image_im)
    return (current_now, isar_image)


def turn_polynomials():
    grid = np.linspace(0.0, 0.25, 4001)
    safe = np.where(grid > 0, np.sqrt(grid), 1.0)
    sine_over = np.where(grid > 0, np.sin(2 * np.pi * safe) / safe, 2 * np.pi)
    cosine = np.cos(2 * np.pi * np.sqrt(grid))
    make = np.polynomial.chebyshev.Chebyshev.fit
    power = np.polynomial.Polynomial
    sine_fit = make(grid, sine_over, 6).convert(kind=power).coef
    cosine_fit = make(grid, cosine, 7).convert(kind=power).coef
    return [float(c) for c in sine_fit], [float(c) for c in cosine_fit]


SINE_FIT, COSINE_FIT = turn_polynomials()


def horner(coefs, x):
    value = jnp.full_like(x, coefs[-1])
    for c in coefs[-2::-1]:
        value = value * x + c
    return value


def cos_sin(turns):
    frac = turns - jnp.floor(turns + 0.5)
    square = frac * frac
    return horner(COSINE_FIT, square), frac * horner(SINE_FIT, square)


def dot(left, right):
    return jnp.dot(left, right, preferred_element_type=F32)


def dot_t(left, right):
    return lax.dot_general(left, right, (((1,), (1,)), ((), ())), preferred_element_type=F32)


def sorter(rows, outer, inner):
    out_id = lax.broadcasted_iota(jnp.int32, (rows, rows), 0)
    in_id = lax.broadcasted_iota(jnp.int32, (rows, rows), 1)
    i = out_id // (2 * outer)
    part = (out_id // outer) % 2
    o = out_id % outer
    return jnp.where(in_id == (o * 2 + part) * inner + i, 1.0, 0.0).astype(BF16)


def part_sorter(rows, inner, back):
    first = lax.broadcasted_iota(jnp.int32, (rows, rows), 1 if back else 0)
    second = lax.broadcasted_iota(jnp.int32, (rows, rows), 0 if back else 1)
    half = rows // 2
    part = first // half
    o = (first % half) // inner
    i = first % inner
    return jnp.where(second == (o * 2 + part) * inner + i, 1.0, 0.0).astype(BF16)


def fetch(pairs, sems):
    copies = [
        pltpu.make_async_copy(source, target, sems.at[n])
        for n, (source, target) in enumerate(pairs)
    ]
    for copy in copies:
        copy.start()
    return copies


def pack_kernel(
    total_cols,
    cur_hbm,
    reflect_hbm,
    weight_hbm,
    partners_hbm,
    count_hbm,
    centres_hbm,
    out,
    cur,
    reflect,
    weight,
    partners,
    count,
    centres,
    sems,
):
    copies = fetch(
        [
            (partners_hbm, partners),
            (weight_hbm, weight),
            (count_hbm, count),
            (centres_hbm, centres),
            (reflect_hbm, reflect),
            (cur_hbm, cur),
        ],
        sems,
    )
    rows = cur.shape[0]
    local_rows, local_cols, unit_count = reflect.shape
    local = local_rows * local_cols
    half = unit_count // 2
    base_row = lax.axis_index("px") * local_rows
    base_col = lax.axis_index("py") * local_cols
    order = sorter(rows, local, rows // (2 * local))
    lane = lax.broadcasted_iota(jnp.int32, (local, 128), 1)
    row = lax.broadcasted_iota(jnp.int32, (local, 128), 0)
    patch_row = base_row + row // local_cols
    patch_col = base_col + row % local_cols
    target = jnp.full((local, 128), -1, jnp.int32)
    for o, (a, b) in enumerate(OFFSETS):
        col = patch_col + b
        col = jnp.where(col < 0, col + total_cols, col)
        col = jnp.where(col >= total_cols, col - total_cols, col)
        target = jnp.where(lane == o, (patch_row + a) * total_cols + col, target)
    for copy in copies[:5]:
        copy.wait()
    ids = partners[...].reshape(local, SLOTS)
    weights = weight[...].astype(F32).reshape(local, SLOTS)
    spots = centres[...].reshape(local, 3)
    counts = count[...]
    live = jnp.zeros((local, 128), jnp.int32)
    for r in range(local_rows):
        for c in range(local_cols):
            live = jnp.where(row == r * local_cols + c, counts[r : r + 1, c : c + 1], live)
    small = jnp.zeros((local, 128), F32)
    for s in range(SLOTS):
        hit = (ids[:, s : s + 1] == target) & (live > s)
        small = small + jnp.where(hit, weights[:, s : s + 1], 0.0)
    first = len(OFFSETS)
    for d in range(3):
        spot = spots[:, d : d + 1]
        top = spot.astype(BF16).astype(F32)
        rest = spot - top
        middle = rest.astype(BF16).astype(F32)
        small = jnp.where(lane == first + 3 * d, top, small)
        small = jnp.where(lane == first + 3 * d + 1, middle, small)
        small = jnp.where(lane == first + 3 * d + 2, rest - middle, small)
    refl = reflect[...].reshape(local, unit_count)
    refl = jnp.concatenate([refl[:, :half], refl[:, half:]], axis=0)
    small = jnp.concatenate([small, jnp.zeros_like(small)], axis=0)
    tail = jnp.concatenate([refl, small], axis=1)
    tail = jnp.concatenate([tail, tail], axis=0).astype(BF16)
    step = tail.shape[0]
    for s in range(rows // step):
        out[step * s : step * (s + 1), unit_count:] = tail
    copies[5].wait()
    out[:, :unit_count] = dot(order, cur[...]).astype(BF16)


def table_kernel(rad_hbm, far_hbm, rad, far_map, long_table, sems):
    copies = fetch([(rad_hbm, rad), (far_hbm, far_map)], sems)
    tile = long_table.shape[0]
    row = lax.broadcasted_iota(jnp.int32, (tile, tile), 0)
    column = lax.broadcasted_iota(jnp.int32, (tile, tile), 1)
    cosine, sine = cos_sin(((row * column) % tile).astype(F32) * (1.0 / tile))
    long_table[:, :tile] = cosine
    long_table[:, tile:] = sine
    for copy in copies:
        copy.wait()


def centres_of(small):
    first = len(OFFSETS)
    centre = []
    for d in range(3):
        at = first + 3 * d
        value = small[:, at : at + 1] + small[:, at + 1 : at + 2] + small[:, at + 2 : at + 3]
        centre.append(value * (0.5 / math.pi))
    return centre


def turns(centre, dirs):
    return centre[0] * dirs[0:1] + centre[1] * dirs[1:2] + centre[2] * dirs[2:3]


def spectrum(current, rad):
    patches = current.shape[0] // 2
    first_part = dot(current, rad[0])
    second_part = dot(current, rad[1])
    return (
        first_part[:patches] - second_part[patches:],
        second_part[:patches] + first_part[patches:],
    )


def bounce_kernel(grid_shape, local_shape, got, rad, spectral_dirs, out, last, kept):
    unit_count = rad.shape[1]
    half = unit_count // 2
    rows = got.shape[0]
    patches = rows // 2
    local_rows, local_cols = local_shape
    local = local_rows * local_cols
    n_px, n_py = grid_shape
    total_cols = n_py * local_cols
    sorted_rows = dot(part_sorter(rows, local, False), got[...])
    start = sorted_rows[:, :unit_count]
    reflect = jnp.concatenate(
        [
            sorted_rows[:patches, unit_count : unit_count + half],
            sorted_rows[patches:, unit_count : unit_count + half],
        ],
        axis=1,
    )
    small = sorted_rows[:patches, unit_count + half :]
    kept[...] = small

    def place(axis):
        ids = lax.broadcasted_iota(jnp.int32, (patches, patches), axis)
        device, within = ids // local, ids % local
        return (
            device % n_px * local_rows + within // local_cols,
            device // n_px * local_cols + within % local_cols,
        )

    (here_row, here_col), (there_row, there_col) = place(0), place(1)
    down = there_row - here_row
    across = there_col - here_col
    across = jnp.where(across > COL_REACH, across - total_cols, across)
    across = jnp.where(across < -COL_REACH, across + total_cols, across)
    near = (down >= -ROW_REACH) & (down <= ROW_REACH)
    near = near & (across >= -COL_REACH) & (across <= COL_REACH)
    offset = (down + ROW_REACH) * (2 * COL_REACH + 1) + across + COL_REACH
    offset = jnp.where(near, offset, -1)
    coef = jnp.zeros((patches, patches), F32)
    for o in range(len(OFFSETS)):
        coef = jnp.where(offset == o, small[:, o : o + 1], coef)
    coef = coef.astype(BF16)
    cosine, sine = cos_sin(turns(centres_of(small), spectral_dirs[...]))
    current = start.astype(BF16)
    for _ in range(2):
        spec_re, spec_im = spectrum(current, rad)
        outgoing = jnp.concatenate(
            [spec_re * cosine + spec_im * sine, spec_im * cosine - spec_re * sine], axis=1
        ).astype(BF16)
        collected = dot(coef, outgoing)
        width = collected.shape[1] // 2
        col_re = collected[:, :width]
        col_im = collected[:, width:]
        arriving = jnp.concatenate(
            [col_re * cosine - col_im * sine, col_re * sine + col_im * cosine], axis=0
        ).astype(BF16)
        first_part = dot_t(arriving, rad[0])
        second_part = dot_t(arriving, rad[1])
        recv_re = first_part[:patches] - second_part[patches:]
        recv_im = second_part[:patches] + first_part[patches:]
        current = jnp.concatenate(
            [start[:patches] + reflect * recv_re, start[patches:] + reflect * recv_im], axis=0
        ).astype(BF16)
    last[...] = current
    out[...] = dot(part_sorter(rows, local, True), current).astype(BF16)


def image_kernel(scale, last, kept, long_table, receiver_dirs, rad, far_map, image):
    splits, tile = image.shape
    patches = kept.shape[0]
    centre = centres_of(kept[...])
    final = jnp.concatenate(spectrum(last[...], rad), axis=0).astype(BF16)
    far_re, far_im = [], []
    for t in range(splits):
        beams = dot(final, far_map[:, tile * t : tile * (t + 1)])
        cos_view, sin_view = cos_sin(turns(centre, receiver_dirs[:, tile * t : tile * (t + 1)]))
        beam_re = beams[:patches]
        beam_im = beams[patches:]
        far_re.append(jnp.sum(beam_re * cos_view - beam_im * sin_view, axis=0, keepdims=True))
        far_im.append(jnp.sum(beam_re * sin_view + beam_im * cos_view, axis=0, keepdims=True))
    row = lax.broadcasted_iota(jnp.int32, (splits, 128), 0)
    column = lax.broadcasted_iota(jnp.int32, (splits, 128), 1)
    short_cos, short_sin = cos_sin((row * column % splits).astype(F32) * (1.0 / splits))
    row = lax.broadcasted_iota(jnp.int32, (splits, tile), 0)
    column = lax.broadcasted_iota(jnp.int32, (splits, tile), 1)
    twist_cos, twist_sin = cos_sin((row * column).astype(F32) * (1.0 / (splits * tile)))
    mid_re = jnp.zeros((splits, tile), F32)
    mid_im = jnp.zeros((splits, tile), F32)
    for t in range(splits):
        c = short_cos[:, t : t + 1]
        s = short_sin[:, t : t + 1]
        mid_re = mid_re + (c * far_re[t] + s * far_im[t])
        mid_im = mid_im + (c * far_im[t] - s * far_re[t])
    tw_re = mid_re * twist_cos + mid_im * twist_sin
    tw_im = mid_im * twist_cos - mid_re * twist_sin
    both = jnp.concatenate([tw_re, tw_im], axis=0)
    answer = jnp.dot(both, long_table[...], precision=HIGH, preferred_element_type=F32)
    image_re = answer[:splits, :tile] + answer[splits:, tile:]
    image_im = answer[splits:, :tile] - answer[:splits, tile:]
    power = scale * (image_re * image_re + image_im * image_im)
    each = tile // splits
    lane = lax.broadcasted_iota(jnp.int32, (splits, tile), 1)
    row = lax.broadcasted_iota(jnp.int32, (splits, tile), 0)
    fast = jnp.where(lane % splits == row, 1.0, 0.0)
    spread = lax.dot_general(
        power, fast, (((0,), (0,)), ((), ())), precision=HIGH, preferred_element_type=F32
    )
    row = lax.broadcasted_iota(jnp.int32, (tile, tile), 0)
    column = lax.broadcasted_iota(jnp.int32, (tile, tile), 1)
    spread = jnp.where(row % each == column // splits, spread, 0.0)
    image[...] = jnp.sum(spread.reshape(splits, each, tile), axis=1)


def unpack_kernel(local, got, currents):
    rows = currents.shape[0]
    order = sorter(rows, rows // (2 * local), local)
    currents[...] = dot(order, got[...]).astype(BF16)


def gather_kernel(*refs):
    pairs, image = refs[:-1], refs[-1]
    splits = pairs[0].shape[0] // 2
    me = lax.axis_index("px")
    row = lax.broadcasted_iota(jnp.int32, image.shape, 0)
    whole = jnp.zeros(image.shape, F32)
    for n, pair in enumerate(pairs):
        for half in range(2):
            mine = pair[pl.ds(half * splits + me, 1), :]
            whole = jnp.where(row == (me ^ (2 * n + half)), mine, whole)
    image[...] = whole


def call(kernel, name, outs, operands, spaces, scratch=(), cost=None, limit=62):
    vmem = pl.BlockSpec(memory_space=pltpu.VMEM)
    return pl.pallas_call(
        kernel,
        out_shape=outs,
        in_specs=[pl.BlockSpec(memory_space=m) for m in spaces],
        out_specs=jax.tree.map(lambda _: vmem, outs),
        scratch_shapes=list(scratch),
        compiler_params=pltpu.CompilerParams(vmem_limit_bytes=limit * MIB),
        cost_estimate=cost,
        name=name,
    )(*operands)


def illumination_sharded(
    currents_in,
    rad_pattern,
    far_map,
    reflect,
    centres,
    spectral_dirs,
    receiver_dirs,
    partners,
    partner_count,
    pair_weight,
):
    local_rows, local_cols, _, illum_count, unit_count = currents_in.shape
    n_px, n_py = lax.axis_size("px"), lax.axis_size("py")
    devices = n_px * n_py
    local = local_rows * local_cols
    rows = 2 * local * illum_count
    total_cols = local_cols * n_py
    patches = local_rows * n_px * total_cols
    rcv_count = far_map.shape[1]
    tile = rcv_count // n_px
    block = 2 * local
    axes = ("py", "px")
    vmem, hbm = pltpu.VMEM, pltpu.HBM

    def like(*arrays):
        scratch = [pltpu.VMEM(a.shape, a.dtype) for a in arrays]
        return scratch + [pltpu.SemaphoreType.DMA((len(arrays),))]

    def shape(*dims, dtype=BF16):
        return jax.ShapeDtypeStruct(dims, dtype)

    sent_width = unit_count + unit_count // 2 + 128
    sources = (
        currents_in.reshape(rows, unit_count),
        reflect,
        pair_weight,
        partners,
        partner_count,
        jnp.transpose(centres, (1, 2, 0)),
    )
    packed = call(
        functools.partial(pack_kernel, total_cols),
        "pack",
        shape(rows, sent_width),
        sources,
        [hbm] * 6,
        like(*sources),
    )
    got = lax.all_to_all(packed.reshape(devices, block, sent_width), axes, 0, 0, tiled=True)
    rad, far, long_table = call(
        table_kernel,
        "table",
        (shape(*rad_pattern.shape), shape(*far_map.shape), shape(tile, 2 * tile, dtype=F32)),
        (rad_pattern, far_map),
        [hbm] * 2,
        [pltpu.SemaphoreType.DMA((2,))],
        limit=32,
        cost=pl.CostEstimate(flops=10**7, bytes_accessed=4 * 10**6, transcendentals=0),
    )
    answer, last, kept = call(
        functools.partial(bounce_kernel, (n_px, n_py), (local_rows, local_cols)),
        "bounces",
        (shape(rows, unit_count), shape(rows, unit_count), shape(patches, 128, dtype=F32)),
        (got.reshape(rows, sent_width), rad, spectral_dirs),
        [vmem] * 3,
        limit=32,
    )
    back = lax.all_to_all(answer.reshape(devices, block, unit_count), axes, 0, 0, tiled=True)
    part = call(
        functools.partial(image_kernel, 0.125 / (patches * rcv_count)),
        "image",
        shape(n_px, tile, dtype=F32),
        (last, kept, long_table, receiver_dirs, rad, far),
        [vmem] * 6,
        cost=pl.CostEstimate(flops=2 * 10**9, bytes_accessed=4 * 10**6, transcendentals=0),
        limit=32,
    )

    def swapped(array, bits):
        return lax.ppermute(array, "px", [(i, i ^ bits) for i in range(n_px)])

    pair = jnp.concatenate([part, swapped(part, 1)], axis=0)
    pairs = [pair] + [swapped(pair, bits) for bits in range(2, n_px, 2)]
    image = call(
        gather_kernel,
        "gather",
        shape(illum_count // n_py, tile, dtype=F32),
        pairs,
        [vmem] * len(pairs),
        limit=16,
    )
    currents = call(
        functools.partial(unpack_kernel, local),
        "unpack",
        shape(rows, unit_count),
        (back.reshape(rows, unit_count),),
        [vmem],
        limit=16,
    )
    return (currents.reshape(currents_in.shape), image)


def fits(mesh):
    def check(currents_in, far_map):
        n_px, n_py = mesh.shape["px"], mesh.shape["py"]
        total_rows, total_cols, _, illum_count, unit_count = currents_in.shape
        local = (total_rows // n_px) * (total_cols // n_py)
        return (
            illum_count == n_px * n_py
            and local == 4
            and n_px == 8
            and unit_count % 256 == 0
            and far_map.shape[1] == n_px * 256
            and total_cols > 2 * COL_REACH
        )

    return check


def solution(mesh):
    in_specs = (
        P("px", "py", None, None, None),
        P(),
        P(),
        P("px", "py", None),
        P(None, "px", "py"),
        P(),
        P(),
        P("px", "py", None),
        P("px", "py"),
        P("px", "py", None),
    )
    out_specs = (P("px", "py", None, None, None), P("py", "px"))
    check = fits(mesh)

    def run(*args):
        local = illumination_sharded if check(args[0], args[2]) else patch_sharded
        mapped = jax.shard_map(
            local, mesh=mesh, in_specs=in_specs, out_specs=out_specs, check_vma=False
        )
        return mapped(*args)

    return run
```

```python
import functools
import math

import jax
import jax.numpy as jnp
import numpy as np
from jax import lax
from jax.experimental import pallas as pl
from jax.experimental.pallas import tpu as pltpu
from jax.sharding import PartitionSpec as P

SLOTS = 12
ROW_REACH = 1
COL_REACH = 2
OFFSETS = [
    (a, b)
    for a in range(-ROW_REACH, ROW_REACH + 1)
    for b in range(-COL_REACH, COL_REACH + 1)
]
F32 = jnp.float32
BF16 = jnp.bfloat16
HIGH = lax.Precision.HIGHEST
MIB = 1024 * 1024


def padded(block, sides, width, periodic):
    for axis, dim in sides:
        count = lax.axis_size(axis)
        forward = [(i, i + 1) for i in range(count - 1)]
        if periodic:
            forward.append((count - 1, 0))
        backward = [(target, source) for source, target in forward]
        low = lax.ppermute(
            lax.slice_in_dim(block, block.shape[dim] - width, None, axis=dim), axis, forward
        )
        high = lax.ppermute(lax.slice_in_dim(block, 0, width, axis=dim), axis, backward)
        block = jnp.concatenate([low, block, high], axis=dim)
    return block


def combined(rad_pattern):
    upper = jnp.concatenate([rad_pattern[0], rad_pattern[1]], axis=1)
    lower = jnp.concatenate([-rad_pattern[1], rad_pattern[0]], axis=1)
    return jnp.concatenate([upper, lower], axis=0)


def radiate(currents, rad_big):
    row_count, col_count, _, illum_count, unit_count = currents.shape
    stacked = jnp.concatenate([currents[:, :, 0], currents[:, :, 1]], axis=-1)
    flat_rows = stacked.reshape(row_count * col_count * illum_count, 2 * unit_count)
    spectra = jnp.dot(flat_rows, rad_big, preferred_element_type=F32)
    return spectra.reshape(row_count, col_count, illum_count, -1)


def receive(arriving, rad_big):
    row_count, col_count, illum_count, double = arriving.shape
    flat_rows = arriving.reshape(-1, double)
    answer = lax.dot_general(
        flat_rows, rad_big, (((1,), (1,)), ((), ())), preferred_element_type=F32
    )
    return answer.reshape(row_count, col_count, illum_count, -1)


def partner_sum(halo_flat, slot_index, weights):
    height = halo_flat.shape[0]
    onehot = slot_index[:, :, None] == jnp.arange(height, dtype=jnp.int32)[None, None, :]
    coef = jnp.sum(jnp.where(onehot, weights[:, :, None].astype(F32), 0.0), axis=1).astype(BF16)
    return jnp.dot(coef, halo_flat, preferred_element_type=F32)


def bounce(current_now, currents_in, rad_big, reflect, cosine, sine_part, plan):
    row_count, col_count, _, illum_count, unit_count = current_now.shape
    spectra = radiate(current_now, rad_big)
    half_width = spectra.shape[-1] // 2
    spec_re = spectra[..., :half_width]
    spec_im = spectra[..., half_width:]
    out_re = spec_re * cosine + spec_im * sine_part
    out_im = spec_im * cosine - spec_re * sine_part
    outgoing = jnp.stack([out_re, out_im], axis=2).astype(BF16)
    girth_block = padded(outgoing, (("py", 1),), COL_REACH, True)
    slot_index, weights = plan
    rim_block = padded(girth_block, (("px", 0),), ROW_REACH, False)
    halo_flat = rim_block.reshape(-1, 2 * illum_count * half_width)
    collected = partner_sum(halo_flat, slot_index, weights)
    collected = collected.reshape(row_count, col_count, 2, illum_count, half_width)
    col_re = collected[:, :, 0]
    col_im = collected[:, :, 1]
    arr_re = col_re * cosine - col_im * sine_part
    arr_im = col_re * sine_part + col_im * cosine
    arriving = jnp.concatenate([arr_re, -arr_im], axis=-1).astype(BF16)
    answer = receive(arriving, rad_big)
    received = jnp.stack([answer[..., :unit_count], -answer[..., unit_count:]], axis=2)
    updated = currents_in.astype(F32) + reflect[:, :, None, None, :] * received
    return updated.astype(BF16)


def patch_sharded(
    currents_in,
    rad_pattern,
    far_map,
    reflect,
    centres,
    spectral_dirs,
    receiver_dirs,
    partners,
    partner_count,
    pair_weight,
):
    row_count, col_count = partner_count.shape
    high = HIGH
    rad_big = combined(rad_pattern)
    phi = jnp.einsum("dm,dab->abm", spectral_dirs, centres, precision=high)
    cosine = jnp.cos(phi)[:, :, None, :]
    sine_part = jnp.sin(phi)[:, :, None, :]
    total_cols = col_count * lax.axis_size("py")
    total_rows = row_count * lax.axis_size("px")
    base_row = lax.axis_index("px") * row_count
    base_col = lax.axis_index("py") * col_count
    across = col_count + 2 * COL_REACH
    local_col = jnp.arange(col_count, dtype=jnp.int32)[None, :, None]
    live = jnp.arange(SLOTS, dtype=jnp.int32)[None, None, :] < partner_count[:, :, None]
    masked_weight = jnp.where(live, pair_weight, jnp.zeros_like(pair_weight))
    part_row = partners // total_cols
    part_col = partners % total_cols
    near_row = part_row - base_row
    near_col = (part_col - base_col - local_col + COL_REACH) % total_cols + local_col
    slot_index = ((near_row + ROW_REACH) * across + near_col).reshape(row_count * col_count, SLOTS)
    weights = masked_weight.reshape(row_count * col_count, SLOTS)
    plan = (slot_index, weights)
    current_now = currents_in
    for bounce_id in range(2):
        current_now = bounce(current_now, currents_in, rad_big, reflect, cosine, sine_part, plan)
    spectra = radiate(current_now, rad_big).astype(BF16)
    illum_count = spectra.shape[2]
    dir_count = far_map.shape[0]
    rcv_count = far_map.shape[1]
    beams = jnp.dot(spectra.reshape(-1, dir_count), far_map, preferred_element_type=F32)
    beams = beams.reshape(row_count, col_count, illum_count, 2, rcv_count)
    view = jnp.einsum("dr,dab->abr", receiver_dirs, centres, precision=high)
    cos_view = jnp.cos(view)[:, :, None, :]
    sin_view = jnp.sin(view)[:, :, None, :]
    beam_re = beams[:, :, :, 0]
    beam_im = beams[:, :, :, 1]
    far_re = jnp.sum(beam_re * cos_view - beam_im * sin_view, axis=(0, 1))
    far_im = jnp.sum(beam_re * sin_view + beam_im * cos_view, axis=(0, 1))
    factor = 1.0 / math.sqrt(total_rows * total_cols)
    far_part = jnp.stack([far_re, far_im]) * factor
    owned_far = lax.psum(
        lax.psum_scatter(far_part.astype(BF16), "py", scatter_dimension=1, tiled=True), "px"
    ).astype(F32)
    bin_width = rcv_count // lax.axis_size("px")
    rcv_ids = jnp.arange(rcv_count, dtype=jnp.int32)[:, None]
    bin_ids = lax.axis_index("px") * bin_width + jnp.arange(bin_width, dtype=jnp.int32)[None, :]
    turn_angle = (rcv_ids * bin_ids % rcv_count).astype(F32) * (2.0 * math.pi / rcv_count)
    norm_factor = 1.0 / math.sqrt(rcv_count)
    cos_table = jnp.cos(turn_angle) * norm_factor
    sin_table = jnp.sin(turn_angle) * norm_factor
    image_re = jnp.dot(owned_far[0], cos_table, precision=high) + jnp.dot(
        owned_far[1], sin_table, precision=high
    )
    image_im = jnp.dot(owned_far[1], cos_table, precision=high) - jnp.dot(
        owned_far[0], sin_table, precision=high
    )
    isar_image = 0.125 * (image_re * image_re + image_im * image_im)
    return (current_now, isar_image)


def turn_polynomials():
    grid = np.linspace(0.0, 0.25, 4001)
    safe = np.where(grid > 0, np.sqrt(grid), 1.0)
    sine_over = np.where(grid > 0, np.sin(2 * np.pi * safe) / safe, 2 * np.pi)
    cosine = np.cos(2 * np.pi * np.sqrt(grid))
    make = np.polynomial.chebyshev.Chebyshev.fit
    power = np.polynomial.Polynomial
    sine_fit = make(grid, sine_over, 5).convert(kind=power).coef
    cosine_fit = make(grid, cosine, 6).convert(kind=power).coef
    return [float(c) for c in sine_fit], [float(c) for c in cosine_fit]


SINE_FIT, COSINE_FIT = turn_polynomials()


def horner(coefs, x):
    value = jnp.full_like(x, coefs[-1])
    for c in coefs[-2::-1]:
        value = value * x + c
    return value


def cos_sin(turns):
    frac = turns - jnp.floor(turns + 0.5)
    square = frac * frac
    return horner(COSINE_FIT, square), frac * horner(SINE_FIT, square)


def dot(left, right):
    return jnp.dot(left, right, preferred_element_type=F32)


def dot_t(left, right):
    return lax.dot_general(left, right, (((1,), (1,)), ((), ())), preferred_element_type=F32)


def sorter(rows, outer, inner, outer_at=lambda o: o, inner_at=lambda i: i):
    out_id = lax.broadcasted_iota(jnp.int32, (rows, rows), 0)
    in_id = lax.broadcasted_iota(jnp.int32, (rows, rows), 1)
    i = out_id // (2 * outer)
    part = (out_id // outer) % 2
    o = out_id % outer
    column = (outer_at(o) * 2 + part) * inner + inner_at(i)
    return jnp.where(in_id == column, 1.0, 0.0).astype(BF16)


def swapped_digits(value, high, low):
    return value % low * high + value // low


def part_sorter(rows, inner, back):
    first = lax.broadcasted_iota(jnp.int32, (rows, rows), 1 if back else 0)
    second = lax.broadcasted_iota(jnp.int32, (rows, rows), 0 if back else 1)
    half = rows // 2
    part = first // half
    o = (first % half) // inner
    i = first % inner
    return jnp.where(second == (o * 2 + part) * inner + i, 1.0, 0.0).astype(BF16)


def fetch(pairs, sems):
    copies = [
        pltpu.make_async_copy(source, target, sems.at[n])
        for n, (source, target) in enumerate(pairs)
    ]
    for copy in copies:
        copy.start()
    return copies


def pack_kernel(
    total_cols,
    grid_shape,
    cur_hbm,
    reflect_hbm,
    weight_hbm,
    partners_hbm,
    count_hbm,
    centres_hbm,
    out,
    cur,
    reflect,
    weight,
    partners,
    count,
    centres,
    sems,
):
    copies = fetch(
        [
            (cur_hbm, cur),
            (reflect_hbm, reflect),
            (partners_hbm, partners),
            (weight_hbm, weight),
            (count_hbm, count),
            (centres_hbm, centres),
        ],
        sems,
    )
    rows = cur.shape[0]
    local_rows, local_cols, unit_count = reflect.shape
    local = local_rows * local_cols
    half = unit_count // 2
    base_row = lax.axis_index("px") * local_rows
    base_col = lax.axis_index("py") * local_cols
    order = sorter(
        rows, local, rows // (2 * local), inner_at=lambda i: swapped_digits(i, *grid_shape)
    )
    lane = lax.broadcasted_iota(jnp.int32, (local, 128), 1)
    row = lax.broadcasted_iota(jnp.int32, (local, 128), 0)
    patch_row = base_row + row // local_cols
    patch_col = base_col + row % local_cols
    target = jnp.full((local, 128), -1, jnp.int32)
    for o, (a, b) in enumerate(OFFSETS):
        col = patch_col + b
        col = jnp.where(col < 0, col + total_cols, col)
        col = jnp.where(col >= total_cols, col - total_cols, col)
        target = jnp.where(lane == o, (patch_row + a) * total_cols + col, target)
    for copy in copies[1:]:
        copy.wait()
    ids = partners[...].reshape(local, SLOTS)
    weights = weight[...].astype(F32).reshape(local, SLOTS)
    spots = centres[...].reshape(local, 3)
    counts = count[...]
    live = jnp.zeros((local, 128), jnp.int32)
    for r in range(local_rows):
        for c in range(local_cols):
            live = jnp.where(row == r * local_cols + c, counts[r : r + 1, c : c + 1], live)
    small = jnp.zeros((local, 128), F32)
    for s in range(SLOTS):
        hit = (ids[:, s : s + 1] == target) & (live > s)
        small = small + jnp.where(hit, weights[:, s : s + 1], 0.0)
    first = len(OFFSETS)
    for d in range(3):
        spot = spots[:, d : d + 1]
        top = spot.astype(BF16).astype(F32)
        rest = spot - top
        middle = rest.astype(BF16).astype(F32)
        small = jnp.where(lane == first + 3 * d, top, small)
        small = jnp.where(lane == first + 3 * d + 1, middle, small)
        small = jnp.where(lane == first + 3 * d + 2, rest - middle, small)
    refl = reflect[...].reshape(local, unit_count)
    refl = jnp.concatenate([refl[:, :half], refl[:, half:]], axis=0)
    small = jnp.concatenate([small, jnp.zeros_like(small)], axis=0)
    tail = jnp.concatenate([refl, small], axis=1)
    tail = jnp.concatenate([tail, tail], axis=0).astype(BF16)
    step = tail.shape[0]
    for s in range(rows // step):
        out[step * s : step * (s + 1), unit_count:] = tail
    copies[0].wait()
    out[:, :unit_count] = dot(order, cur[...]).astype(BF16)


def table_kernel(rad_hbm, rad, long_table, sems):
    copies = fetch([(rad_hbm, rad)], sems)
    tile = long_table.shape[0]
    row = lax.broadcasted_iota(jnp.int32, (tile, tile), 0)
    column = lax.broadcasted_iota(jnp.int32, (tile, tile), 1)
    cosine, sine = cos_sin(((row * column) % tile).astype(F32) * (1.0 / tile))
    long_table[:, :tile] = cosine.astype(BF16)
    long_table[:, tile:] = sine.astype(BF16)
    for copy in copies:
        copy.wait()


def centres_of(small):
    first = len(OFFSETS)
    centre = []
    for d in range(3):
        at = first + 3 * d
        value = small[:, at : at + 1] + small[:, at + 1 : at + 2] + small[:, at + 2 : at + 3]
        centre.append(value * (0.5 / math.pi))
    return centre


def turns(centre, dirs):
    return centre[0] * dirs[0:1] + centre[1] * dirs[1:2] + centre[2] * dirs[2:3]


def spectrum(current, rad):
    patches = current.shape[0] // 2
    first_part = dot(current, rad[0])
    second_part = dot(current, rad[1])
    return (
        first_part[:patches] - second_part[patches:],
        second_part[:patches] + first_part[patches:],
    )


def bounce_kernel(grid_shape, local_shape, got, rad, spectral_dirs, out, last, kept):
    unit_count = rad.shape[1]
    half = unit_count // 2
    rows = got.shape[0]
    patches = rows // 2
    local_rows, local_cols = local_shape
    local = local_rows * local_cols
    n_px, n_py = grid_shape
    total_cols = n_py * local_cols
    sorted_rows = dot(part_sorter(rows, local, False), got[...])
    start = sorted_rows[:, :unit_count]
    reflect = jnp.concatenate(
        [
            sorted_rows[:patches, unit_count : unit_count + half],
            sorted_rows[patches:, unit_count : unit_count + half],
        ],
        axis=1,
    )
    small = sorted_rows[:patches, unit_count + half :]
    kept[...] = small

    def place(axis):
        ids = lax.broadcasted_iota(jnp.int32, (patches, patches), axis)
        device, within = ids // local, ids % local
        return (
            device // n_py * local_rows + within // local_cols,
            device % n_py * local_cols + within % local_cols,
        )

    (here_row, here_col), (there_row, there_col) = place(0), place(1)
    down = there_row - here_row
    across = there_col - here_col
    across = jnp.where(across > COL_REACH, across - total_cols, across)
    across = jnp.where(across < -COL_REACH, across + total_cols, across)
    near = (down >= -ROW_REACH) & (down <= ROW_REACH)
    near = near & (across >= -COL_REACH) & (across <= COL_REACH)
    offset = (down + ROW_REACH) * (2 * COL_REACH + 1) + across + COL_REACH
    offset = jnp.where(near, offset, -1)
    coef = jnp.zeros((patches, patches), F32)
    for o in range(len(OFFSETS)):
        coef = jnp.where(offset == o, small[:, o : o + 1], coef)
    coef = coef.astype(BF16)
    cosine, sine = cos_sin(turns(centres_of(small), spectral_dirs[...]))
    current = start.astype(BF16)
    for _ in range(2):
        spec_re, spec_im = spectrum(current, rad)
        outgoing = jnp.concatenate(
            [spec_re * cosine + spec_im * sine, spec_im * cosine - spec_re * sine], axis=1
        ).astype(BF16)
        collected = dot(coef, outgoing)
        width = collected.shape[1] // 2
        col_re = collected[:, :width]
        col_im = collected[:, width:]
        arriving = jnp.concatenate(
            [col_re * cosine - col_im * sine, col_re * sine + col_im * cosine], axis=0
        ).astype(BF16)
        first_part = dot_t(arriving, rad[0])
        second_part = dot_t(arriving, rad[1])
        recv_re = first_part[:patches] - second_part[patches:]
        recv_im = second_part[:patches] + first_part[patches:]
        current = jnp.concatenate(
            [start[:patches] + reflect * recv_re, start[patches:] + reflect * recv_im], axis=0
        ).astype(BF16)
    last[...] = current
    out[...] = dot(part_sorter(rows, local, True), current).astype(BF16)


def image_kernel(
    scale, last, kept, long_table, receiver_dirs, rad, far_hbm, image, far_map, cos_view, sin_view, sems
):
    copies = fetch([(far_hbm, far_map)], sems)
    splits, tile = image.shape
    patches = kept.shape[0]
    centre = centres_of(kept[...])
    cuts = [slice(tile * t, tile * (t + 1)) for t in range(splits)]
    for cut in cuts:
        cos_view[:, cut], sin_view[:, cut] = cos_sin(turns(centre, receiver_dirs[:, cut]))
    final = jnp.concatenate(spectrum(last[...], rad), axis=0).astype(BF16)
    copies[0].wait()
    far_re, far_im = [], []
    for cut in cuts:
        beams = dot(final, far_map[:, cut])
        c, s = cos_view[:, cut], sin_view[:, cut]
        beam_re = beams[:patches]
        beam_im = beams[patches:]
        far_re.append(jnp.sum(beam_re * c - beam_im * s, axis=0, keepdims=True))
        far_im.append(jnp.sum(beam_re * s + beam_im * c, axis=0, keepdims=True))
    row = lax.broadcasted_iota(jnp.int32, (splits, 128), 0)
    column = lax.broadcasted_iota(jnp.int32, (splits, 128), 1)
    short_cos, short_sin = cos_sin((row * column % splits).astype(F32) * (1.0 / splits))
    row = lax.broadcasted_iota(jnp.int32, (splits, tile), 0)
    column = lax.broadcasted_iota(jnp.int32, (splits, tile), 1)
    twist_cos, twist_sin = cos_sin((row * column).astype(F32) * (1.0 / (splits * tile)))
    mid_re = jnp.zeros((splits, tile), F32)
    mid_im = jnp.zeros((splits, tile), F32)
    for t in range(splits):
        c = short_cos[:, t : t + 1]
        s = short_sin[:, t : t + 1]
        mid_re = mid_re + (c * far_re[t] + s * far_im[t])
        mid_im = mid_im + (c * far_im[t] - s * far_re[t])
    tw_re = mid_re * twist_cos + mid_im * twist_sin
    tw_im = mid_im * twist_cos - mid_re * twist_sin
    both = jnp.concatenate([tw_re, tw_im], axis=0)
    upper = both.astype(BF16)
    lower = (both - upper.astype(F32)).astype(BF16)
    answer = dot(jnp.concatenate([upper, lower], axis=0), long_table[...])
    answer = answer[: 2 * splits] + answer[2 * splits :]
    image_re = answer[:splits, :tile] + answer[splits:, tile:]
    image_im = answer[splits:, :tile] - answer[:splits, tile:]
    power = scale * (image_re * image_re + image_im * image_im)
    each = tile // splits
    lane = lax.broadcasted_iota(jnp.int32, (splits, tile), 1)
    row = lax.broadcasted_iota(jnp.int32, (splits, tile), 0)
    fast = jnp.where(lane % splits == row, 1.0, 0.0)
    spread = lax.dot_general(
        power, fast, (((0,), (0,)), ((), ())), precision=HIGH, preferred_element_type=F32
    )
    row = lax.broadcasted_iota(jnp.int32, (tile, tile), 0)
    column = lax.broadcasted_iota(jnp.int32, (tile, tile), 1)
    spread = jnp.where(row % each == column // splits, spread, 0.0)
    image[...] = jnp.sum(spread.reshape(splits, each, tile), axis=1)


def unpack_kernel(local, grid_shape, got, *refs):
    pairs, (currents, image) = refs[:-2], refs[-2:]
    rows = currents.shape[0]
    n_px, n_py = grid_shape
    order = sorter(
        rows, rows // (2 * local), local, outer_at=lambda o: swapped_digits(o, n_py, n_px)
    )
    currents[...] = dot(order, got[...]).astype(BF16)
    me = lax.axis_index("px")
    row = lax.broadcasted_iota(jnp.int32, image.shape, 0)
    whole = jnp.zeros(image.shape, F32)
    for n in range(n_px):
        mine = pairs[n // 2][pl.ds(n % 2 * n_px + me, 1), :]
        whole = jnp.where(row == (me ^ n), mine, whole)
    image[...] = whole


def call(kernel, name, outs, operands, spaces, scratch=(), cost=None, limit=32):
    vmem = pl.BlockSpec(memory_space=pltpu.VMEM)
    operands = [
        pltpu.with_memory_space_constraint(a, pltpu.HBM) if m is pltpu.HBM else a
        for a, m in zip(operands, spaces)
    ]
    return pl.pallas_call(
        kernel,
        out_shape=outs,
        in_specs=[pl.BlockSpec(memory_space=m) for m in spaces],
        out_specs=jax.tree.map(lambda _: vmem, outs),
        scratch_shapes=list(scratch),
        compiler_params=pltpu.CompilerParams(vmem_limit_bytes=limit * MIB),
        cost_estimate=cost,
        name=name,
    )(*operands)


def illumination_sharded(
    currents_in,
    rad_pattern,
    far_map,
    reflect,
    centres,
    spectral_dirs,
    receiver_dirs,
    partners,
    partner_count,
    pair_weight,
):
    local_rows, local_cols, _, illum_count, unit_count = currents_in.shape
    n_px, n_py = lax.axis_size("px"), lax.axis_size("py")
    devices = n_px * n_py
    local = local_rows * local_cols
    rows = 2 * local * illum_count
    total_cols = local_cols * n_py
    patches = local_rows * n_px * total_cols
    rcv_count = far_map.shape[1]
    tile = rcv_count // n_px
    block = 2 * local
    axes = ("px", "py")
    vmem, hbm = pltpu.VMEM, pltpu.HBM

    def like(*arrays):
        scratch = [pltpu.VMEM(a.shape, a.dtype) for a in arrays]
        return scratch + [pltpu.SemaphoreType.DMA((len(arrays),))]

    def shape(*dims, dtype=BF16):
        return jax.ShapeDtypeStruct(dims, dtype)

    sent_width = unit_count + unit_count // 2 + 128
    sources = (
        currents_in.reshape(rows, unit_count),
        reflect,
        pair_weight,
        partners,
        partner_count,
        jnp.transpose(centres, (1, 2, 0)),
    )
    packed = call(
        functools.partial(pack_kernel, total_cols, (n_px, n_py)),
        "pack",
        shape(rows, sent_width),
        sources,
        [hbm] * 6,
        like(*sources),
    )
    got = lax.all_to_all(packed.reshape(devices, block, sent_width), axes, 0, 0, tiled=True)
    rad, long_table = call(
        table_kernel,
        "table",
        (shape(*rad_pattern.shape), shape(tile, 2 * tile)),
        (rad_pattern,),
        [hbm],
        [pltpu.SemaphoreType.DMA((1,))],
        cost=pl.CostEstimate(flops=10**7, bytes_accessed=4 * 10**6, transcendentals=0),
    )
    answer, last, kept = call(
        functools.partial(bounce_kernel, (n_px, n_py), (local_rows, local_cols)),
        "bounces",
        (shape(rows, unit_count), shape(rows, unit_count), shape(patches, 128, dtype=F32)),
        (got.reshape(rows, sent_width), rad, spectral_dirs),
        [vmem] * 3,
    )
    back = lax.all_to_all(answer.reshape(devices, block, unit_count), axes, 0, 0, tiled=True)
    part = call(
        functools.partial(image_kernel, 0.125 / (patches * rcv_count)),
        "image",
        shape(n_px, tile, dtype=F32),
        (last, kept, long_table, receiver_dirs, rad, far_map),
        [vmem] * 5 + [hbm],
        [
            pltpu.VMEM(far_map.shape, BF16),
            pltpu.VMEM((patches, rcv_count), F32),
            pltpu.VMEM((patches, rcv_count), F32),
            pltpu.SemaphoreType.DMA((1,)),
        ],
        cost=pl.CostEstimate(flops=2 * 10**9, bytes_accessed=4 * 10**6, transcendentals=0),
    )

    def swapped(array, bits):
        return lax.ppermute(array, "px", [(i, i ^ bits) for i in range(n_px)])

    pair = jnp.concatenate([part, swapped(part, 1)], axis=0)
    pairs = [pair] + [swapped(pair, bits) for bits in range(2, n_px, 2)]
    currents, image = call(
        functools.partial(unpack_kernel, local, (n_px, n_py)),
        "unpack",
        (shape(rows, unit_count), shape(illum_count // n_py, tile, dtype=F32)),
        (back.reshape(rows, unit_count), *pairs),
        [vmem] * (1 + len(pairs)),
    )
    return (currents.reshape(currents_in.shape), image)


def fits(mesh):
    def check(currents_in, far_map):
        n_px, n_py = mesh.shape["px"], mesh.shape["py"]
        total_rows, total_cols, _, illum_count, unit_count = currents_in.shape
        local = (total_rows // n_px) * (total_cols // n_py)
        return (
            illum_count == n_px * n_py
            and local == 4
            and n_px == 8
            and unit_count % 256 == 0
            and far_map.shape[1] == n_px * 256
            and total_cols > 2 * COL_REACH
        )

    return check


def solution(mesh):
    in_specs = (
        P("px", "py", None, None, None),
        P(),
        P(),
        P("px", "py", None),
        P(None, "px", "py"),
        P(),
        P(),
        P("px", "py", None),
        P("px", "py"),
        P("px", "py", None),
    )
    out_specs = (P("px", "py", None, None, None), P("py", "px"))
    check = fits(mesh)

    def run(*args):
        local = illumination_sharded if check(args[0], args[2]) else patch_sharded
        mapped = jax.shard_map(
            local, mesh=mesh, in_specs=in_specs, out_specs=out_specs, check_vma=False
        )
        return mapped(*args)

    return run
```

```python
import functools
import math

import jax
import jax.numpy as jnp
import numpy as np
from jax import lax
from jax.experimental import pallas as pl
from jax.experimental.pallas import tpu as pltpu
from jax.sharding import PartitionSpec as P

SLOTS = 12
ROW_REACH = 1
COL_REACH = 2
OFFSETS = [
    (a, b)
    for a in range(-ROW_REACH, ROW_REACH + 1)
    for b in range(-COL_REACH, COL_REACH + 1)
]
F32 = jnp.float32
BF16 = jnp.bfloat16
HIGH = lax.Precision.HIGHEST
MIB = 1024 * 1024


def padded(block, sides, width, periodic):
    for axis, dim in sides:
        count = lax.axis_size(axis)
        forward = [(i, i + 1) for i in range(count - 1)]
        if periodic:
            forward.append((count - 1, 0))
        backward = [(target, source) for source, target in forward]
        low = lax.ppermute(
            lax.slice_in_dim(block, block.shape[dim] - width, None, axis=dim), axis, forward
        )
        high = lax.ppermute(lax.slice_in_dim(block, 0, width, axis=dim), axis, backward)
        block = jnp.concatenate([low, block, high], axis=dim)
    return block


def combined(rad_pattern):
    upper = jnp.concatenate([rad_pattern[0], rad_pattern[1]], axis=1)
    lower = jnp.concatenate([-rad_pattern[1], rad_pattern[0]], axis=1)
    return jnp.concatenate([upper, lower], axis=0)


def radiate(currents, rad_big):
    row_count, col_count, _, illum_count, unit_count = currents.shape
    stacked = jnp.concatenate([currents[:, :, 0], currents[:, :, 1]], axis=-1)
    flat_rows = stacked.reshape(row_count * col_count * illum_count, 2 * unit_count)
    spectra = jnp.dot(flat_rows, rad_big, preferred_element_type=F32)
    return spectra.reshape(row_count, col_count, illum_count, -1)


def receive(arriving, rad_big):
    row_count, col_count, illum_count, double = arriving.shape
    flat_rows = arriving.reshape(-1, double)
    answer = lax.dot_general(
        flat_rows, rad_big, (((1,), (1,)), ((), ())), preferred_element_type=F32
    )
    return answer.reshape(row_count, col_count, illum_count, -1)


def partner_sum(halo_flat, slot_index, weights):
    height = halo_flat.shape[0]
    onehot = slot_index[:, :, None] == jnp.arange(height, dtype=jnp.int32)[None, None, :]
    coef = jnp.sum(jnp.where(onehot, weights[:, :, None].astype(F32), 0.0), axis=1).astype(BF16)
    return jnp.dot(coef, halo_flat, preferred_element_type=F32)


def bounce(current_now, currents_in, rad_big, reflect, cosine, sine_part, plan):
    row_count, col_count, _, illum_count, unit_count = current_now.shape
    spectra = radiate(current_now, rad_big)
    half_width = spectra.shape[-1] // 2
    spec_re = spectra[..., :half_width]
    spec_im = spectra[..., half_width:]
    out_re = spec_re * cosine + spec_im * sine_part
    out_im = spec_im * cosine - spec_re * sine_part
    outgoing = jnp.stack([out_re, out_im], axis=2).astype(BF16)
    girth_block = padded(outgoing, (("py", 1),), COL_REACH, True)
    slot_index, weights = plan
    rim_block = padded(girth_block, (("px", 0),), ROW_REACH, False)
    halo_flat = rim_block.reshape(-1, 2 * illum_count * half_width)
    collected = partner_sum(halo_flat, slot_index, weights)
    collected = collected.reshape(row_count, col_count, 2, illum_count, half_width)
    col_re = collected[:, :, 0]
    col_im = collected[:, :, 1]
    arr_re = col_re * cosine - col_im * sine_part
    arr_im = col_re * sine_part + col_im * cosine
    arriving = jnp.concatenate([arr_re, -arr_im], axis=-1).astype(BF16)
    answer = receive(arriving, rad_big)
    received = jnp.stack([answer[..., :unit_count], -answer[..., unit_count:]], axis=2)
    updated = currents_in.astype(F32) + reflect[:, :, None, None, :] * received
    return updated.astype(BF16)


def patch_sharded(
    currents_in,
    rad_pattern,
    far_map,
    reflect,
    centres,
    spectral_dirs,
    receiver_dirs,
    partners,
    partner_count,
    pair_weight,
):
    row_count, col_count = partner_count.shape
    high = HIGH
    rad_big = combined(rad_pattern)
    phi = jnp.einsum("dm,dab->abm", spectral_dirs, centres, precision=high)
    cosine = jnp.cos(phi)[:, :, None, :]
    sine_part = jnp.sin(phi)[:, :, None, :]
    total_cols = col_count * lax.axis_size("py")
    total_rows = row_count * lax.axis_size("px")
    base_row = lax.axis_index("px") * row_count
    base_col = lax.axis_index("py") * col_count
    across = col_count + 2 * COL_REACH
    local_col = jnp.arange(col_count, dtype=jnp.int32)[None, :, None]
    live = jnp.arange(SLOTS, dtype=jnp.int32)[None, None, :] < partner_count[:, :, None]
    masked_weight = jnp.where(live, pair_weight, jnp.zeros_like(pair_weight))
    part_row = partners // total_cols
    part_col = partners % total_cols
    near_row = part_row - base_row
    near_col = (part_col - base_col - local_col + COL_REACH) % total_cols + local_col
    slot_index = ((near_row + ROW_REACH) * across + near_col).reshape(row_count * col_count, SLOTS)
    weights = masked_weight.reshape(row_count * col_count, SLOTS)
    plan = (slot_index, weights)
    current_now = currents_in
    for bounce_id in range(2):
        current_now = bounce(current_now, currents_in, rad_big, reflect, cosine, sine_part, plan)
    spectra = radiate(current_now, rad_big).astype(BF16)
    illum_count = spectra.shape[2]
    dir_count = far_map.shape[0]
    rcv_count = far_map.shape[1]
    beams = jnp.dot(spectra.reshape(-1, dir_count), far_map, preferred_element_type=F32)
    beams = beams.reshape(row_count, col_count, illum_count, 2, rcv_count)
    view = jnp.einsum("dr,dab->abr", receiver_dirs, centres, precision=high)
    cos_view = jnp.cos(view)[:, :, None, :]
    sin_view = jnp.sin(view)[:, :, None, :]
    beam_re = beams[:, :, :, 0]
    beam_im = beams[:, :, :, 1]
    far_re = jnp.sum(beam_re * cos_view - beam_im * sin_view, axis=(0, 1))
    far_im = jnp.sum(beam_re * sin_view + beam_im * cos_view, axis=(0, 1))
    factor = 1.0 / math.sqrt(total_rows * total_cols)
    far_part = jnp.stack([far_re, far_im]) * factor
    owned_far = lax.psum(
        lax.psum_scatter(far_part.astype(BF16), "py", scatter_dimension=1, tiled=True), "px"
    ).astype(F32)
    bin_width = rcv_count // lax.axis_size("px")
    rcv_ids = jnp.arange(rcv_count, dtype=jnp.int32)[:, None]
    bin_ids = lax.axis_index("px") * bin_width + jnp.arange(bin_width, dtype=jnp.int32)[None, :]
    turn_angle = (rcv_ids * bin_ids % rcv_count).astype(F32) * (2.0 * math.pi / rcv_count)
    norm_factor = 1.0 / math.sqrt(rcv_count)
    cos_table = jnp.cos(turn_angle) * norm_factor
    sin_table = jnp.sin(turn_angle) * norm_factor
    image_re = jnp.dot(owned_far[0], cos_table, precision=high) + jnp.dot(
        owned_far[1], sin_table, precision=high
    )
    image_im = jnp.dot(owned_far[1], cos_table, precision=high) - jnp.dot(
        owned_far[0], sin_table, precision=high
    )
    isar_image = 0.125 * (image_re * image_re + image_im * image_im)
    return (current_now, isar_image)


def turn_polynomials():
    grid = np.linspace(0.0, 0.25, 4001)
    safe = np.where(grid > 0, np.sqrt(grid), 1.0)
    sine_over = np.where(grid > 0, np.sin(2 * np.pi * safe) / safe, 2 * np.pi)
    cosine = np.cos(2 * np.pi * np.sqrt(grid))
    make = np.polynomial.chebyshev.Chebyshev.fit
    power = np.polynomial.Polynomial
    sine_fit = make(grid, sine_over, 5).convert(kind=power).coef
    cosine_fit = make(grid, cosine, 6).convert(kind=power).coef
    return [float(c) for c in sine_fit], [float(c) for c in cosine_fit]


SINE_FIT, COSINE_FIT = turn_polynomials()


def horner(coefs, x):
    value = jnp.full_like(x, coefs[-1])
    for c in coefs[-2::-1]:
        value = value * x + c
    return value


def cos_sin(turns):
    frac = turns - jnp.floor(turns + 0.5)
    square = frac * frac
    return horner(COSINE_FIT, square), frac * horner(SINE_FIT, square)


def dot(left, right):
    return jnp.dot(left, right, preferred_element_type=F32)


def dot_t(left, right):
    return lax.dot_general(left, right, (((1,), (1,)), ((), ())), preferred_element_type=F32)


def sorter(rows, outer, inner, outer_at=lambda o: o, inner_at=lambda i: i):
    out_id = lax.broadcasted_iota(jnp.int32, (rows, rows), 0)
    in_id = lax.broadcasted_iota(jnp.int32, (rows, rows), 1)
    i = out_id // (2 * outer)
    part = (out_id // outer) % 2
    o = out_id % outer
    column = (outer_at(o) * 2 + part) * inner + inner_at(i)
    return jnp.where(in_id == column, 1.0, 0.0).astype(BF16)


def swapped_digits(value, high, low):
    return value % low * high + value // low


def part_sorter(rows, inner, back):
    first = lax.broadcasted_iota(jnp.int32, (rows, rows), 1 if back else 0)
    second = lax.broadcasted_iota(jnp.int32, (rows, rows), 0 if back else 1)
    half = rows // 2
    part = first // half
    o = (first % half) // inner
    i = first % inner
    return jnp.where(second == (o * 2 + part) * inner + i, 1.0, 0.0).astype(BF16)


def fetch(pairs, sems):
    copies = [
        pltpu.make_async_copy(source, target, sems.at[n])
        for n, (source, target) in enumerate(pairs)
    ]
    for copy in copies:
        copy.start()
    return copies


def pack_kernel(
    total_cols,
    grid_shape,
    cur_hbm,
    reflect_hbm,
    weight_hbm,
    partners_hbm,
    count_hbm,
    centres_hbm,
    out,
    cur,
    reflect,
    weight,
    partners,
    count,
    centres,
    sems,
):
    copies = fetch(
        [
            (cur_hbm, cur),
            (reflect_hbm, reflect),
            (partners_hbm, partners),
            (weight_hbm, weight),
            (count_hbm, count),
            (centres_hbm, centres),
        ],
        sems,
    )
    rows = cur.shape[0]
    local_rows, local_cols, unit_count = reflect.shape
    local = local_rows * local_cols
    half = unit_count // 2
    base_row = lax.axis_index("px") * local_rows
    base_col = lax.axis_index("py") * local_cols
    order = sorter(
        rows, local, rows // (2 * local), inner_at=lambda i: swapped_digits(i, *grid_shape)
    )
    lane = lax.broadcasted_iota(jnp.int32, (local, 128), 1)
    row = lax.broadcasted_iota(jnp.int32, (local, 128), 0)
    patch_row = base_row + row // local_cols
    patch_col = base_col + row % local_cols
    target = jnp.full((local, 128), -1, jnp.int32)
    for o, (a, b) in enumerate(OFFSETS):
        col = patch_col + b
        col = jnp.where(col < 0, col + total_cols, col)
        col = jnp.where(col >= total_cols, col - total_cols, col)
        target = jnp.where(lane == o, (patch_row + a) * total_cols + col, target)
    for copy in copies[1:]:
        copy.wait()
    ids = partners[...].reshape(local, SLOTS)
    weights = weight[...].astype(F32).reshape(local, SLOTS)
    spots = centres[...].reshape(local, 3)
    counts = count[...]
    live = jnp.zeros((local, 128), jnp.int32)
    for r in range(local_rows):
        for c in range(local_cols):
            live = jnp.where(row == r * local_cols + c, counts[r : r + 1, c : c + 1], live)
    small = jnp.zeros((local, 128), F32)
    for s in range(SLOTS):
        hit = (ids[:, s : s + 1] == target) & (live > s)
        small = small + jnp.where(hit, weights[:, s : s + 1], 0.0)
    first = len(OFFSETS)
    for d in range(3):
        spot = spots[:, d : d + 1]
        top = spot.astype(BF16).astype(F32)
        rest = spot - top
        middle = rest.astype(BF16).astype(F32)
        small = jnp.where(lane == first + 3 * d, top, small)
        small = jnp.where(lane == first + 3 * d + 1, middle, small)
        small = jnp.where(lane == first + 3 * d + 2, rest - middle, small)
    refl = reflect[...].reshape(local, unit_count)
    refl = jnp.concatenate([refl[:, :half], refl[:, half:]], axis=0)
    small = jnp.concatenate([small, jnp.zeros_like(small)], axis=0)
    tail = jnp.concatenate([refl, small], axis=1)
    tail = jnp.concatenate([tail, tail], axis=0).astype(BF16)
    step = tail.shape[0]
    for s in range(rows // step):
        out[step * s : step * (s + 1), unit_count:] = tail
    copies[0].wait()
    out[:, :unit_count] = dot(order, cur[...]).astype(BF16)


def table_kernel(rad_hbm, far_hbm, rad, far_head, long_table, sems):
    head = far_hbm.at[:, : far_head.shape[1]]
    copies = fetch([(rad_hbm, rad), (head, far_head)], sems)
    tile = long_table.shape[0]
    row = lax.broadcasted_iota(jnp.int32, (tile, tile), 0)
    column = lax.broadcasted_iota(jnp.int32, (tile, tile), 1)
    cosine, sine = cos_sin(((row * column) % tile).astype(F32) * (1.0 / tile))
    long_table[:, :tile] = cosine.astype(BF16)
    long_table[:, tile:] = sine.astype(BF16)
    for copy in copies:
        copy.wait()


def centres_of(small):
    first = len(OFFSETS)
    centre = []
    for d in range(3):
        at = first + 3 * d
        value = small[:, at : at + 1] + small[:, at + 1 : at + 2] + small[:, at + 2 : at + 3]
        centre.append(value * (0.5 / math.pi))
    return centre


def turns(centre, dirs):
    return centre[0] * dirs[0:1] + centre[1] * dirs[1:2] + centre[2] * dirs[2:3]


def spectrum(current, rad):
    patches = current.shape[0] // 2
    first_part = dot(current, rad[0])
    second_part = dot(current, rad[1])
    return (
        first_part[:patches] - second_part[patches:],
        second_part[:patches] + first_part[patches:],
    )


def bounce_kernel(
    grid_shape,
    local_shape,
    got,
    rad,
    spectral_dirs,
    far_head,
    out_hbm,
    final,
    kept,
    out,
    sems,
):
    del far_head
    unit_count = rad.shape[1]
    half = unit_count // 2
    rows = got.shape[0]
    patches = rows // 2
    local_rows, local_cols = local_shape
    local = local_rows * local_cols
    n_px, n_py = grid_shape
    total_cols = n_py * local_cols
    sorted_rows = dot(part_sorter(rows, local, False), got[...])
    start = sorted_rows[:, :unit_count]
    reflect = jnp.concatenate(
        [
            sorted_rows[:patches, unit_count : unit_count + half],
            sorted_rows[patches:, unit_count : unit_count + half],
        ],
        axis=1,
    )
    small = sorted_rows[:patches, unit_count + half :]
    kept[...] = small

    def place(axis):
        ids = lax.broadcasted_iota(jnp.int32, (patches, patches), axis)
        device, within = ids // local, ids % local
        return (
            device // n_py * local_rows + within // local_cols,
            device % n_py * local_cols + within % local_cols,
        )

    (here_row, here_col), (there_row, there_col) = place(0), place(1)
    down = there_row - here_row
    across = there_col - here_col
    across = jnp.where(across > COL_REACH, across - total_cols, across)
    across = jnp.where(across < -COL_REACH, across + total_cols, across)
    near = (down >= -ROW_REACH) & (down <= ROW_REACH)
    near = near & (across >= -COL_REACH) & (across <= COL_REACH)
    offset = (down + ROW_REACH) * (2 * COL_REACH + 1) + across + COL_REACH
    offset = jnp.where(near, offset, -1)
    coef = jnp.zeros((patches, patches), F32)
    for o in range(len(OFFSETS)):
        coef = jnp.where(offset == o, small[:, o : o + 1], coef)
    coef = coef.astype(BF16)
    cosine, sine = cos_sin(turns(centres_of(small), spectral_dirs[...]))
    current = start.astype(BF16)
    for _ in range(2):
        spec_re, spec_im = spectrum(current, rad)
        outgoing = jnp.concatenate(
            [spec_re * cosine + spec_im * sine, spec_im * cosine - spec_re * sine], axis=1
        ).astype(BF16)
        collected = dot(coef, outgoing)
        width = collected.shape[1] // 2
        col_re = collected[:, :width]
        col_im = collected[:, width:]
        arriving = jnp.concatenate(
            [col_re * cosine - col_im * sine, col_re * sine + col_im * cosine], axis=0
        ).astype(BF16)
        first_part = dot_t(arriving, rad[0])
        second_part = dot_t(arriving, rad[1])
        recv_re = first_part[:patches] - second_part[patches:]
        recv_im = second_part[:patches] + first_part[patches:]
        current = jnp.concatenate(
            [start[:patches] + reflect * recv_re, start[patches:] + reflect * recv_im], axis=0
        ).astype(BF16)
    out[...] = dot(part_sorter(rows, local, True), current).astype(BF16)
    out_copy = pltpu.make_async_copy(out, out_hbm, sems.at[0])
    out_copy.start()
    final[...] = jnp.concatenate(spectrum(current, rad), axis=0).astype(BF16)
    out_copy.wait()


def image_kernel(
    scale,
    final,
    kept,
    long_table,
    receiver_dirs,
    far_head,
    far_hbm,
    same,
    other,
    image,
    far_rest,
    sems,
):
    head = far_head.shape[1]
    rest_copy = pltpu.make_async_copy(far_hbm.at[:, head:], far_rest, sems.at[0])
    rest_copy.start()
    splits, tile = image.shape
    patches = kept.shape[0]
    centre = centres_of(kept[...])
    far_re, far_im = [], []
    for t in range(splits):
        cut = slice(tile * t, tile * (t + 1))
        if tile * t == head:
            rest_copy.wait()
        if tile * t < head:
            beams = dot(final[...], far_head[:, cut])
        else:
            beams = dot(final[...], far_rest[:, tile * t - head : tile * (t + 1) - head])
        cos_view, sin_view = cos_sin(turns(centre, receiver_dirs[:, cut]))
        beam_re = beams[:patches]
        beam_im = beams[patches:]
        far_re.append(jnp.sum(beam_re * cos_view - beam_im * sin_view, axis=0, keepdims=True))
        far_im.append(jnp.sum(beam_re * sin_view + beam_im * cos_view, axis=0, keepdims=True))
    row = lax.broadcasted_iota(jnp.int32, (splits, 128), 0)
    column = lax.broadcasted_iota(jnp.int32, (splits, 128), 1)
    short_cos, short_sin = cos_sin((row * column % splits).astype(F32) * (1.0 / splits))
    row = lax.broadcasted_iota(jnp.int32, (splits, tile), 0)
    column = lax.broadcasted_iota(jnp.int32, (splits, tile), 1)
    twist_cos, twist_sin = cos_sin((row * column).astype(F32) * (1.0 / (splits * tile)))
    mid_re = jnp.zeros((splits, tile), F32)
    mid_im = jnp.zeros((splits, tile), F32)
    for t in range(splits):
        c = short_cos[:, t : t + 1]
        s = short_sin[:, t : t + 1]
        mid_re = mid_re + (c * far_re[t] + s * far_im[t])
        mid_im = mid_im + (c * far_im[t] - s * far_re[t])
    tw_re = mid_re * twist_cos + mid_im * twist_sin
    tw_im = mid_im * twist_cos - mid_re * twist_sin
    both = jnp.concatenate([tw_re, tw_im], axis=0)
    upper = both.astype(BF16)
    lower = (both - upper.astype(F32)).astype(BF16)
    answer = dot(jnp.concatenate([upper, lower], axis=0), long_table[...])
    answer = answer[: 2 * splits] + answer[2 * splits :]
    image_re = answer[:splits, :tile] + answer[splits:, tile:]
    image_im = answer[splits:, :tile] - answer[:splits, tile:]
    power = scale * (image_re * image_re + image_im * image_im)
    each = tile // splits
    upper = power.astype(BF16)
    lower = (power - upper.astype(F32)).astype(BF16)
    lane = lax.broadcasted_iota(jnp.int32, (2 * splits, tile), 1)
    row = lax.broadcasted_iota(jnp.int32, (2 * splits, tile), 0)
    fast = jnp.where(lane % splits == row % splits, 1.0, 0.0).astype(BF16)
    spread = lax.dot_general(
        jnp.concatenate([upper, lower], axis=0),
        fast,
        (((0,), (0,)), ((), ())),
        preferred_element_type=F32,
    )
    row = lax.broadcasted_iota(jnp.int32, (tile, tile), 0)
    column = lax.broadcasted_iota(jnp.int32, (tile, tile), 1)
    spread = jnp.where(row % each == column // splits, spread, 0.0)
    image[...] = jnp.sum(spread.reshape(splits, each, tile), axis=1)
    me = lax.axis_index("px")
    for n in range(splits // 2):
        same[n : n + 1, :] = image[pl.ds(me ^ (2 * n), 1), :]
        other[n : n + 1, :] = image[pl.ds(me ^ (2 * n + 1), 1), :]


def unpack_kernel(local, grid_shape, got, *refs):
    pairs, (currents, image) = refs[:-2], refs[-2:]
    rows = currents.shape[0]
    n_px, n_py = grid_shape
    order = sorter(
        rows, rows // (2 * local), local, outer_at=lambda o: swapped_digits(o, n_py, n_px)
    )
    currents[...] = dot(order, got[...]).astype(BF16)
    me = lax.axis_index("px")
    row = lax.broadcasted_iota(jnp.int32, image.shape, 0)
    whole = jnp.zeros(image.shape, F32)
    for n in range(n_px):
        at = n // 2 + n % 2 * (n_px // 2)
        mine = pairs[n // 2][at : at + 1, :]
        whole = jnp.where(row == (me ^ n), mine, whole)
    image[...] = whole


def call(kernel, name, outs, operands, spaces, scratch=(), cost=None, limit=32, left=()):
    specs = jax.tree.map(lambda _: pl.BlockSpec(memory_space=pltpu.VMEM), outs)
    if left:
        specs = tuple(
            pl.BlockSpec(memory_space=pl.ANY) if n in left else s for n, s in enumerate(specs)
        )
    operands = [
        pltpu.with_memory_space_constraint(a, pltpu.HBM) if m is pltpu.HBM else a
        for a, m in zip(operands, spaces)
    ]
    return pl.pallas_call(
        kernel,
        out_shape=outs,
        in_specs=[pl.BlockSpec(memory_space=m) for m in spaces],
        out_specs=specs,
        scratch_shapes=list(scratch),
        compiler_params=pltpu.CompilerParams(vmem_limit_bytes=limit * MIB),
        cost_estimate=cost,
        name=name,
    )(*operands)


def illumination_sharded(
    currents_in,
    rad_pattern,
    far_map,
    reflect,
    centres,
    spectral_dirs,
    receiver_dirs,
    partners,
    partner_count,
    pair_weight,
):
    local_rows, local_cols, _, illum_count, unit_count = currents_in.shape
    n_px, n_py = lax.axis_size("px"), lax.axis_size("py")
    devices = n_px * n_py
    local = local_rows * local_cols
    rows = 2 * local * illum_count
    total_cols = local_cols * n_py
    patches = local_rows * n_px * total_cols
    rcv_count = far_map.shape[1]
    tile = rcv_count // n_px
    block = 2 * local
    axes = ("px", "py")
    vmem, hbm = pltpu.VMEM, pltpu.HBM

    def like(*arrays):
        scratch = [pltpu.VMEM(a.shape, a.dtype) for a in arrays]
        return scratch + [pltpu.SemaphoreType.DMA((len(arrays),))]

    def shape(*dims, dtype=BF16):
        return jax.ShapeDtypeStruct(dims, dtype)

    sent_width = unit_count + unit_count // 2 + 128
    sources = (
        currents_in.reshape(rows, unit_count),
        reflect,
        pair_weight,
        partners,
        partner_count,
        jnp.transpose(centres, (1, 2, 0)),
    )
    packed = call(
        functools.partial(pack_kernel, total_cols, (n_px, n_py)),
        "pack",
        shape(rows, sent_width),
        sources,
        [hbm] * 6,
        like(*sources),
    )
    got = lax.all_to_all(packed.reshape(devices, block, sent_width), axes, 0, 0, tiled=True)
    depth, head = far_map.shape[0], rcv_count // 2
    rad, far_head, long_table = call(
        table_kernel,
        "table",
        (shape(*rad_pattern.shape), shape(depth, head), shape(tile, 2 * tile)),
        (rad_pattern, far_map),
        [hbm] * 2,
        [pltpu.SemaphoreType.DMA((2,))],
        cost=pl.CostEstimate(flops=10**7, bytes_accessed=4 * 10**6, transcendentals=0),
    )
    answer, final, kept = call(
        functools.partial(bounce_kernel, (n_px, n_py), (local_rows, local_cols)),
        "bounces",
        (shape(rows, unit_count), shape(rows, unit_count), shape(patches, 128, dtype=F32)),
        (got.reshape(rows, sent_width), rad, spectral_dirs, far_head),
        [vmem] * 3 + [pl.ANY],
        [pltpu.VMEM((rows, unit_count), BF16), pltpu.SemaphoreType.DMA((1,))],
        left=(0,),
    )
    back = lax.all_to_all(answer.reshape(devices, block, unit_count), axes, 0, 0, tiled=True)
    half = n_px // 2
    same, other = call(
        functools.partial(image_kernel, 0.125 / (patches * rcv_count)),
        "image",
        (shape(half, tile, dtype=F32), shape(half, tile, dtype=F32)),
        (final, kept, long_table, receiver_dirs, far_head, far_map),
        [vmem] * 5 + [hbm],
        [
            pltpu.VMEM((n_px, tile), F32),
            pltpu.VMEM((depth, rcv_count - head), BF16),
            pltpu.SemaphoreType.DMA((1,)),
        ],
        cost=pl.CostEstimate(flops=2 * 10**9, bytes_accessed=4 * 10**6, transcendentals=0),
    )

    def swapped(array, bits):
        return lax.ppermute(array, "px", [(i, i ^ bits) for i in range(n_px)])

    pair = jnp.concatenate([same, swapped(other, 1)], axis=0)
    pairs = [pair] + [swapped(pair, bits) for bits in range(2, n_px, 2)]
    currents, image = call(
        functools.partial(unpack_kernel, local, (n_px, n_py)),
        "unpack",
        (shape(rows, unit_count), shape(illum_count // n_py, tile, dtype=F32)),
        (back.reshape(rows, unit_count), *pairs),
        [vmem] * (1 + len(pairs)),
    )
    return (currents.reshape(currents_in.shape), image)


def fits(mesh):
    def check(currents_in, far_map):
        n_px, n_py = mesh.shape["px"], mesh.shape["py"]
        total_rows, total_cols, _, illum_count, unit_count = currents_in.shape
        local = (total_rows // n_px) * (total_cols // n_py)
        return (
            illum_count == n_px * n_py
            and local == 4
            and n_px == 8
            and unit_count % 256 == 0
            and far_map.shape[1] == n_px * 256
            and total_cols > 2 * COL_REACH
        )

    return check


def solution(mesh):
    in_specs = (
        P("px", "py", None, None, None),
        P(),
        P(),
        P("px", "py", None),
        P(None, "px", "py"),
        P(),
        P(),
        P("px", "py", None),
        P("px", "py"),
        P("px", "py", None),
    )
    out_specs = (P("px", "py", None, None, None), P("py", "px"))
    check = fits(mesh)

    def run(*args):
        local = illumination_sharded if check(args[0], args[2]) else patch_sharded
        mapped = jax.shard_map(
            local, mesh=mesh, in_specs=in_specs, out_specs=out_specs, check_vma=False
        )
        return mapped(*args)

    return run
```

```python
import functools
import math

import jax
import jax.numpy as jnp
import numpy as np
from jax import lax
from jax.experimental import pallas as pl
from jax.experimental.pallas import tpu as pltpu
from jax.sharding import PartitionSpec as P

SLOTS = 12
ROW_REACH = 1
COL_REACH = 2
OFFSETS = [
    (a, b)
    for a in range(-ROW_REACH, ROW_REACH + 1)
    for b in range(-COL_REACH, COL_REACH + 1)
]
F32 = jnp.float32
BF16 = jnp.bfloat16
HIGH = lax.Precision.HIGHEST
MIB = 1024 * 1024


def padded(block, sides, width, periodic):
    for axis, dim in sides:
        count = lax.axis_size(axis)
        forward = [(i, i + 1) for i in range(count - 1)]
        if periodic:
            forward.append((count - 1, 0))
        backward = [(target, source) for source, target in forward]
        low = lax.ppermute(
            lax.slice_in_dim(block, block.shape[dim] - width, None, axis=dim), axis, forward
        )
        high = lax.ppermute(lax.slice_in_dim(block, 0, width, axis=dim), axis, backward)
        block = jnp.concatenate([low, block, high], axis=dim)
    return block


def combined(rad_pattern):
    upper = jnp.concatenate([rad_pattern[0], rad_pattern[1]], axis=1)
    lower = jnp.concatenate([-rad_pattern[1], rad_pattern[0]], axis=1)
    return jnp.concatenate([upper, lower], axis=0)


def radiate(currents, rad_big):
    row_count, col_count, _, illum_count, unit_count = currents.shape
    stacked = jnp.concatenate([currents[:, :, 0], currents[:, :, 1]], axis=-1)
    flat_rows = stacked.reshape(row_count * col_count * illum_count, 2 * unit_count)
    spectra = jnp.dot(flat_rows, rad_big, preferred_element_type=F32)
    return spectra.reshape(row_count, col_count, illum_count, -1)


def receive(arriving, rad_big):
    row_count, col_count, illum_count, double = arriving.shape
    flat_rows = arriving.reshape(-1, double)
    answer = lax.dot_general(
        flat_rows, rad_big, (((1,), (1,)), ((), ())), preferred_element_type=F32
    )
    return answer.reshape(row_count, col_count, illum_count, -1)


def partner_sum(halo_flat, slot_index, weights):
    height = halo_flat.shape[0]
    onehot = slot_index[:, :, None] == jnp.arange(height, dtype=jnp.int32)[None, None, :]
    coef = jnp.sum(jnp.where(onehot, weights[:, :, None].astype(F32), 0.0), axis=1).astype(BF16)
    return jnp.dot(coef, halo_flat, preferred_element_type=F32)


def bounce(current_now, currents_in, rad_big, reflect, cosine, sine_part, plan):
    row_count, col_count, _, illum_count, unit_count = current_now.shape
    spectra = radiate(current_now, rad_big)
    half_width = spectra.shape[-1] // 2
    spec_re = spectra[..., :half_width]
    spec_im = spectra[..., half_width:]
    out_re = spec_re * cosine + spec_im * sine_part
    out_im = spec_im * cosine - spec_re * sine_part
    outgoing = jnp.stack([out_re, out_im], axis=2).astype(BF16)
    girth_block = padded(outgoing, (("py", 1),), COL_REACH, True)
    slot_index, weights = plan
    rim_block = padded(girth_block, (("px", 0),), ROW_REACH, False)
    halo_flat = rim_block.reshape(-1, 2 * illum_count * half_width)
    collected = partner_sum(halo_flat, slot_index, weights)
    collected = collected.reshape(row_count, col_count, 2, illum_count, half_width)
    col_re = collected[:, :, 0]
    col_im = collected[:, :, 1]
    arr_re = col_re * cosine - col_im * sine_part
    arr_im = col_re * sine_part + col_im * cosine
    arriving = jnp.concatenate([arr_re, -arr_im], axis=-1).astype(BF16)
    answer = receive(arriving, rad_big)
    received = jnp.stack([answer[..., :unit_count], -answer[..., unit_count:]], axis=2)
    updated = currents_in.astype(F32) + reflect[:, :, None, None, :] * received
    return updated.astype(BF16)


def patch_sharded(
    currents_in,
    rad_pattern,
    far_map,
    reflect,
    centres,
    spectral_dirs,
    receiver_dirs,
    partners,
    partner_count,
    pair_weight,
):
    row_count, col_count = partner_count.shape
    high = HIGH
    rad_big = combined(rad_pattern)
    phi = jnp.einsum("dm,dab->abm", spectral_dirs, centres, precision=high)
    cosine = jnp.cos(phi)[:, :, None, :]
    sine_part = jnp.sin(phi)[:, :, None, :]
    total_cols = col_count * lax.axis_size("py")
    total_rows = row_count * lax.axis_size("px")
    base_row = lax.axis_index("px") * row_count
    base_col = lax.axis_index("py") * col_count
    across = col_count + 2 * COL_REACH
    local_col = jnp.arange(col_count, dtype=jnp.int32)[None, :, None]
    live = jnp.arange(SLOTS, dtype=jnp.int32)[None, None, :] < partner_count[:, :, None]
    masked_weight = jnp.where(live, pair_weight, jnp.zeros_like(pair_weight))
    part_row = partners // total_cols
    part_col = partners % total_cols
    near_row = part_row - base_row
    near_col = (part_col - base_col - local_col + COL_REACH) % total_cols + local_col
    slot_index = ((near_row + ROW_REACH) * across + near_col).reshape(row_count * col_count, SLOTS)
    weights = masked_weight.reshape(row_count * col_count, SLOTS)
    plan = (slot_index, weights)
    current_now = currents_in
    for bounce_id in range(2):
        current_now = bounce(current_now, currents_in, rad_big, reflect, cosine, sine_part, plan)
    spectra = radiate(current_now, rad_big).astype(BF16)
    illum_count = spectra.shape[2]
    dir_count = far_map.shape[0]
    rcv_count = far_map.shape[1]
    beams = jnp.dot(spectra.reshape(-1, dir_count), far_map, preferred_element_type=F32)
    beams = beams.reshape(row_count, col_count, illum_count, 2, rcv_count)
    view = jnp.einsum("dr,dab->abr", receiver_dirs, centres, precision=high)
    cos_view = jnp.cos(view)[:, :, None, :]
    sin_view = jnp.sin(view)[:, :, None, :]
    beam_re = beams[:, :, :, 0]
    beam_im = beams[:, :, :, 1]
    far_re = jnp.sum(beam_re * cos_view - beam_im * sin_view, axis=(0, 1))
    far_im = jnp.sum(beam_re * sin_view + beam_im * cos_view, axis=(0, 1))
    factor = 1.0 / math.sqrt(total_rows * total_cols)
    far_part = jnp.stack([far_re, far_im]) * factor
    owned_far = lax.psum(
        lax.psum_scatter(far_part.astype(BF16), "py", scatter_dimension=1, tiled=True), "px"
    ).astype(F32)
    bin_width = rcv_count // lax.axis_size("px")
    rcv_ids = jnp.arange(rcv_count, dtype=jnp.int32)[:, None]
    bin_ids = lax.axis_index("px") * bin_width + jnp.arange(bin_width, dtype=jnp.int32)[None, :]
    turn_angle = (rcv_ids * bin_ids % rcv_count).astype(F32) * (2.0 * math.pi / rcv_count)
    norm_factor = 1.0 / math.sqrt(rcv_count)
    cos_table = jnp.cos(turn_angle) * norm_factor
    sin_table = jnp.sin(turn_angle) * norm_factor
    image_re = jnp.dot(owned_far[0], cos_table, precision=high) + jnp.dot(
        owned_far[1], sin_table, precision=high
    )
    image_im = jnp.dot(owned_far[1], cos_table, precision=high) - jnp.dot(
        owned_far[0], sin_table, precision=high
    )
    isar_image = 0.125 * (image_re * image_re + image_im * image_im)
    return (current_now, isar_image)


def turn_polynomials():
    grid = np.linspace(0.0, 0.25, 4001)
    safe = np.where(grid > 0, np.sqrt(grid), 1.0)
    sine_over = np.where(grid > 0, np.sin(2 * np.pi * safe) / safe, 2 * np.pi)
    cosine = np.cos(2 * np.pi * np.sqrt(grid))
    make = np.polynomial.chebyshev.Chebyshev.fit
    power = np.polynomial.Polynomial
    sine_fit = make(grid, sine_over, 5).convert(kind=power).coef
    cosine_fit = make(grid, cosine, 6).convert(kind=power).coef
    return [float(c) for c in sine_fit], [float(c) for c in cosine_fit]


SINE_FIT, COSINE_FIT = turn_polynomials()


def horner(coefs, x):
    value = jnp.full_like(x, coefs[-1])
    for c in coefs[-2::-1]:
        value = value * x + c
    return value


def cos_sin(turns):
    frac = turns - jnp.floor(turns + 0.5)
    square = frac * frac
    return horner(COSINE_FIT, square), frac * horner(SINE_FIT, square)


def dot(left, right):
    return jnp.dot(left, right, preferred_element_type=F32)


def dot_t(left, right):
    return lax.dot_general(left, right, (((1,), (1,)), ((), ())), preferred_element_type=F32)


def sorter(rows, outer, inner, outer_at=lambda o: o, inner_at=lambda i: i):
    out_id = lax.broadcasted_iota(jnp.int32, (rows, rows), 0)
    in_id = lax.broadcasted_iota(jnp.int32, (rows, rows), 1)
    i = out_id // (2 * outer)
    part = (out_id // outer) % 2
    o = out_id % outer
    column = (outer_at(o) * 2 + part) * inner + inner_at(i)
    return jnp.where(in_id == column, 1.0, 0.0).astype(BF16)


def swapped_digits(value, high, low):
    return value % low * high + value // low


def part_sorter(rows, inner, back):
    first = lax.broadcasted_iota(jnp.int32, (rows, rows), 1 if back else 0)
    second = lax.broadcasted_iota(jnp.int32, (rows, rows), 0 if back else 1)
    half = rows // 2
    part = first // half
    o = (first % half) // inner
    i = first % inner
    return jnp.where(second == (o * 2 + part) * inner + i, 1.0, 0.0).astype(BF16)


def fetch(pairs, sems):
    copies = [
        pltpu.make_async_copy(source, target, sems.at[n])
        for n, (source, target) in enumerate(pairs)
    ]
    for copy in copies:
        copy.start()
    return copies


def pack_kernel(
    total_cols,
    grid_shape,
    cur_hbm,
    reflect_hbm,
    weight_hbm,
    partners_hbm,
    count_hbm,
    centres_hbm,
    out,
    cur,
    reflect,
    weight,
    partners,
    count,
    centres,
    sems,
):
    copies = fetch(
        [
            (cur_hbm, cur),
            (reflect_hbm, reflect),
            (partners_hbm, partners),
            (weight_hbm, weight),
            (count_hbm, count),
            (centres_hbm, centres),
        ],
        sems,
    )
    rows = cur.shape[0]
    local_rows, local_cols, unit_count = reflect.shape
    local = local_rows * local_cols
    base_row = lax.axis_index("px") * local_rows
    base_col = lax.axis_index("py") * local_cols
    row_id = lax.broadcasted_iota(jnp.int32, (rows, rows), 0)
    in_id = lax.broadcasted_iota(jnp.int32, (rows, rows), 1)
    illum_count = rows // (2 * local)
    part, chunk, o = row_id // (rows // 2), row_id % (rows // 2) // local, row_id % local
    column = (o * 2 + part) * illum_count + swapped_digits(chunk, *grid_shape)
    order = jnp.where(in_id == column, 1.0, 0.0).astype(BF16)
    lane = lax.broadcasted_iota(jnp.int32, (local, 128), 1)
    row = lax.broadcasted_iota(jnp.int32, (local, 128), 0)
    patch_row = base_row + row // local_cols
    patch_col = base_col + row % local_cols
    target = jnp.full((local, 128), -1, jnp.int32)
    for o, (a, b) in enumerate(OFFSETS):
        col = patch_col + b
        col = jnp.where(col < 0, col + total_cols, col)
        col = jnp.where(col >= total_cols, col - total_cols, col)
        target = jnp.where(lane == o, (patch_row + a) * total_cols + col, target)
    for copy in copies[1:]:
        copy.wait()
    ids = partners[...].reshape(local, SLOTS)
    weights = weight[...].astype(F32).reshape(local, SLOTS)
    spots = centres[...].reshape(local, 3)
    counts = count[...]
    live = jnp.zeros((local, 128), jnp.int32)
    for r in range(local_rows):
        for c in range(local_cols):
            live = jnp.where(row == r * local_cols + c, counts[r : r + 1, c : c + 1], live)
    small = jnp.zeros((local, 128), F32)
    for s in range(SLOTS):
        hit = (ids[:, s : s + 1] == target) & (live > s)
        small = small + jnp.where(hit, weights[:, s : s + 1], 0.0)
    first = len(OFFSETS)
    for d in range(3):
        spot = spots[:, d : d + 1]
        top = spot.astype(BF16).astype(F32)
        rest = spot - top
        middle = rest.astype(BF16).astype(F32)
        small = jnp.where(lane == first + 3 * d, top, small)
        small = jnp.where(lane == first + 3 * d + 1, middle, small)
        small = jnp.where(lane == first + 3 * d + 2, rest - middle, small)
    refl = reflect[...].reshape(local, unit_count)
    tail = jnp.concatenate([refl, small], axis=1).astype(BF16)
    for n in range(illum_count):
        out[n, :, 2 * unit_count :] = tail
    copies[0].wait()
    both = dot(order, cur[...])
    both = jnp.concatenate([both[: rows // 2], both[rows // 2 :]], axis=1)
    for n in range(illum_count):
        out[n, :, : 2 * unit_count] = both[local * n : local * (n + 1)].astype(BF16)


def table_kernel(rad_hbm, far_hbm, rad, far_head, long_table, sems):
    head = far_hbm.at[:, : far_head.shape[1]]
    copies = fetch([(rad_hbm, rad), (head, far_head)], sems)
    tile = long_table.shape[0]
    row = lax.broadcasted_iota(jnp.int32, (tile, tile), 0)
    column = lax.broadcasted_iota(jnp.int32, (tile, tile), 1)
    cosine, sine = cos_sin(((row * column) % tile).astype(F32) * (1.0 / tile))
    long_table[:, :tile] = cosine.astype(BF16)
    long_table[:, tile:] = sine.astype(BF16)
    for copy in copies:
        copy.wait()


def centres_of(small):
    first = len(OFFSETS)
    centre = []
    for d in range(3):
        at = first + 3 * d
        value = small[:, at : at + 1] + small[:, at + 1 : at + 2] + small[:, at + 2 : at + 3]
        centre.append(value * (0.5 / math.pi))
    return centre


def turns(centre, dirs):
    return centre[0] * dirs[0:1] + centre[1] * dirs[1:2] + centre[2] * dirs[2:3]


def spectrum(current, rad):
    patches = current.shape[0] // 2
    first_part = dot(current, rad[0])
    second_part = dot(current, rad[1])
    return (
        first_part[:patches] - second_part[patches:],
        second_part[:patches] + first_part[patches:],
    )


def bounce_kernel(
    grid_shape,
    local_shape,
    got,
    rad,
    spectral_dirs,
    far_head,
    out_hbm,
    final,
    kept,
    out,
    sems,
):
    del far_head
    unit_count = rad.shape[1]
    patches = got.shape[0] * got.shape[1]
    rows = 2 * patches
    local_rows, local_cols = local_shape
    local = local_rows * local_cols
    n_px, n_py = grid_shape
    total_cols = n_py * local_cols
    whole = jnp.concatenate([got[n].astype(F32) for n in range(got.shape[0])], axis=0)
    start = jnp.concatenate([whole[:, :unit_count], whole[:, unit_count : 2 * unit_count]], axis=0)
    reflect = whole[:, 2 * unit_count : 3 * unit_count]
    small = whole[:, 3 * unit_count :]
    kept[...] = small

    def place(axis):
        ids = lax.broadcasted_iota(jnp.int32, (patches, patches), axis)
        device, within = ids // local, ids % local
        return (
            device // n_py * local_rows + within // local_cols,
            device % n_py * local_cols + within % local_cols,
        )

    (here_row, here_col), (there_row, there_col) = place(0), place(1)
    down = there_row - here_row
    across = there_col - here_col
    across = jnp.where(across > COL_REACH, across - total_cols, across)
    across = jnp.where(across < -COL_REACH, across + total_cols, across)
    near = (down >= -ROW_REACH) & (down <= ROW_REACH)
    near = near & (across >= -COL_REACH) & (across <= COL_REACH)
    offset = (down + ROW_REACH) * (2 * COL_REACH + 1) + across + COL_REACH
    offset = jnp.where(near, offset, -1)
    coef = jnp.zeros((patches, patches), F32)
    for o in range(len(OFFSETS)):
        coef = jnp.where(offset == o, small[:, o : o + 1], coef)
    coef = coef.astype(BF16)
    cosine, sine = cos_sin(turns(centres_of(small), spectral_dirs[...]))
    current = start.astype(BF16)
    for _ in range(2):
        spec_re, spec_im = spectrum(current, rad)
        outgoing = jnp.concatenate(
            [spec_re * cosine + spec_im * sine, spec_im * cosine - spec_re * sine], axis=1
        ).astype(BF16)
        collected = dot(coef, outgoing)
        width = collected.shape[1] // 2
        col_re = collected[:, :width]
        col_im = collected[:, width:]
        arriving = jnp.concatenate(
            [col_re * cosine - col_im * sine, col_re * sine + col_im * cosine], axis=0
        ).astype(BF16)
        first_part = dot_t(arriving, rad[0])
        second_part = dot_t(arriving, rad[1])
        recv_re = first_part[:patches] - second_part[patches:]
        recv_im = second_part[:patches] + first_part[patches:]
        current = jnp.concatenate(
            [start[:patches] + reflect * recv_re, start[patches:] + reflect * recv_im], axis=0
        ).astype(BF16)
    out[...] = dot(part_sorter(rows, local, True), current).astype(BF16)
    out_copy = pltpu.make_async_copy(out, out_hbm, sems.at[0])
    out_copy.start()
    final[...] = jnp.concatenate(spectrum(current, rad), axis=0).astype(BF16)
    out_copy.wait()


def image_kernel(
    scale,
    final,
    kept,
    long_table,
    receiver_dirs,
    far_head,
    far_hbm,
    same,
    other,
    image,
    far_rest,
    sems,
):
    head = far_head.shape[1]
    rest_copy = pltpu.make_async_copy(far_hbm.at[:, head:], far_rest, sems.at[0])
    rest_copy.start()
    splits, tile = image.shape
    patches = kept.shape[0]
    centre = centres_of(kept[...])
    far_re, far_im = [], []
    for t in range(splits):
        cut = slice(tile * t, tile * (t + 1))
        if tile * t == head:
            rest_copy.wait()
        if tile * t < head:
            beams = dot(final[...], far_head[:, cut])
        else:
            beams = dot(final[...], far_rest[:, tile * t - head : tile * (t + 1) - head])
        cos_view, sin_view = cos_sin(turns(centre, receiver_dirs[:, cut]))
        beam_re = beams[:patches]
        beam_im = beams[patches:]
        far_re.append(jnp.sum(beam_re * cos_view - beam_im * sin_view, axis=0, keepdims=True))
        far_im.append(jnp.sum(beam_re * sin_view + beam_im * cos_view, axis=0, keepdims=True))
    row = lax.broadcasted_iota(jnp.int32, (splits, 128), 0)
    column = lax.broadcasted_iota(jnp.int32, (splits, 128), 1)
    short_cos, short_sin = cos_sin((row * column % splits).astype(F32) * (1.0 / splits))
    row = lax.broadcasted_iota(jnp.int32, (splits, tile), 0)
    column = lax.broadcasted_iota(jnp.int32, (splits, tile), 1)
    twist_cos, twist_sin = cos_sin((row * column).astype(F32) * (1.0 / (splits * tile)))
    mid_re = jnp.zeros((splits, tile), F32)
    mid_im = jnp.zeros((splits, tile), F32)
    for t in range(splits):
        c = short_cos[:, t : t + 1]
        s = short_sin[:, t : t + 1]
        mid_re = mid_re + (c * far_re[t] + s * far_im[t])
        mid_im = mid_im + (c * far_im[t] - s * far_re[t])
    tw_re = mid_re * twist_cos + mid_im * twist_sin
    tw_im = mid_im * twist_cos - mid_re * twist_sin
    both = jnp.concatenate([tw_re, tw_im], axis=0)
    upper = both.astype(BF16)
    lower = (both - upper.astype(F32)).astype(BF16)
    answer = dot(jnp.concatenate([upper, lower], axis=0), long_table[...])
    answer = answer[: 2 * splits] + answer[2 * splits :]
    image_re = answer[:splits, :tile] + answer[splits:, tile:]
    image_im = answer[splits:, :tile] - answer[:splits, tile:]
    power = scale * (image_re * image_re + image_im * image_im)
    each = tile // splits
    upper = power.astype(BF16)
    lower = (power - upper.astype(F32)).astype(BF16)
    lane = lax.broadcasted_iota(jnp.int32, (2 * splits, tile), 1)
    row = lax.broadcasted_iota(jnp.int32, (2 * splits, tile), 0)
    fast = jnp.where(lane % splits == row % splits, 1.0, 0.0).astype(BF16)
    spread = lax.dot_general(
        jnp.concatenate([upper, lower], axis=0),
        fast,
        (((0,), (0,)), ((), ())),
        preferred_element_type=F32,
    )
    row = lax.broadcasted_iota(jnp.int32, (tile, tile), 0)
    column = lax.broadcasted_iota(jnp.int32, (tile, tile), 1)
    spread = jnp.where(row % each == column // splits, spread, 0.0)
    image[...] = jnp.sum(spread.reshape(splits, each, tile), axis=1)
    me = lax.axis_index("px")
    for n in range(splits // 2):
        same[n : n + 1, :] = image[pl.ds(me ^ (2 * n), 1), :]
        other[n : n + 1, :] = image[pl.ds(me ^ (2 * n + 1), 1), :]


def unpack_kernel(local, grid_shape, got, *refs):
    pairs, (currents, image) = refs[:-2], refs[-2:]
    rows = currents.shape[0]
    n_px, n_py = grid_shape
    order = sorter(
        rows, rows // (2 * local), local, outer_at=lambda o: swapped_digits(o, n_py, n_px)
    )
    currents[...] = dot(order, got[...]).astype(BF16)
    me = lax.axis_index("px")
    row = lax.broadcasted_iota(jnp.int32, image.shape, 0)
    whole = jnp.zeros(image.shape, F32)
    for n in range(n_px):
        at = n // 2 + n % 2 * (n_px // 2)
        mine = pairs[n // 2][at : at + 1, :]
        whole = jnp.where(row == (me ^ n), mine, whole)
    image[...] = whole


def call(kernel, name, outs, operands, spaces, scratch=(), cost=None, limit=32, left=()):
    specs = jax.tree.map(lambda _: pl.BlockSpec(memory_space=pltpu.VMEM), outs)
    if left:
        specs = tuple(
            pl.BlockSpec(memory_space=pl.ANY) if n in left else s for n, s in enumerate(specs)
        )
    operands = [
        pltpu.with_memory_space_constraint(a, pltpu.HBM) if m is pltpu.HBM else a
        for a, m in zip(operands, spaces)
    ]
    return pl.pallas_call(
        kernel,
        out_shape=outs,
        in_specs=[pl.BlockSpec(memory_space=m) for m in spaces],
        out_specs=specs,
        scratch_shapes=list(scratch),
        compiler_params=pltpu.CompilerParams(vmem_limit_bytes=limit * MIB),
        cost_estimate=cost,
        name=name,
    )(*operands)


def illumination_sharded(
    currents_in,
    rad_pattern,
    far_map,
    reflect,
    centres,
    spectral_dirs,
    receiver_dirs,
    partners,
    partner_count,
    pair_weight,
):
    local_rows, local_cols, _, illum_count, unit_count = currents_in.shape
    n_px, n_py = lax.axis_size("px"), lax.axis_size("py")
    devices = n_px * n_py
    local = local_rows * local_cols
    rows = 2 * local * illum_count
    total_cols = local_cols * n_py
    patches = local_rows * n_px * total_cols
    rcv_count = far_map.shape[1]
    tile = rcv_count // n_px
    block = 2 * local
    axes = ("px", "py")
    vmem, hbm = pltpu.VMEM, pltpu.HBM

    def like(*arrays):
        scratch = [pltpu.VMEM(a.shape, a.dtype) for a in arrays]
        return scratch + [pltpu.SemaphoreType.DMA((len(arrays),))]

    def shape(*dims, dtype=BF16):
        return jax.ShapeDtypeStruct(dims, dtype)

    sent_width = 3 * unit_count + 128
    sources = (
        currents_in.reshape(rows, unit_count),
        reflect,
        pair_weight,
        partners,
        partner_count,
        jnp.transpose(centres, (1, 2, 0)),
    )
    packed = call(
        functools.partial(pack_kernel, total_cols, (n_px, n_py)),
        "pack",
        shape(devices, local, sent_width),
        sources,
        [hbm] * 6,
        like(*sources),
    )
    got = lax.all_to_all(packed, axes, 0, 0, tiled=True)
    depth, head = far_map.shape[0], rcv_count // 2
    rad, far_head, long_table = call(
        table_kernel,
        "table",
        (shape(*rad_pattern.shape), shape(depth, head), shape(tile, 2 * tile)),
        (rad_pattern, far_map),
        [hbm] * 2,
        [pltpu.SemaphoreType.DMA((2,))],
        cost=pl.CostEstimate(flops=10**7, bytes_accessed=4 * 10**6, transcendentals=0),
    )
    answer, final, kept = call(
        functools.partial(bounce_kernel, (n_px, n_py), (local_rows, local_cols)),
        "bounces",
        (shape(rows, unit_count), shape(rows, unit_count), shape(patches, 128, dtype=F32)),
        (got, rad, spectral_dirs, far_head),
        [vmem] * 3 + [pl.ANY],
        [pltpu.VMEM((rows, unit_count), BF16), pltpu.SemaphoreType.DMA((1,))],
        left=(0,),
    )
    back = lax.all_to_all(answer.reshape(devices, block, unit_count), axes, 0, 0, tiled=True)
    half = n_px // 2
    same, other = call(
        functools.partial(image_kernel, 0.125 / (patches * rcv_count)),
        "image",
        (shape(half, tile, dtype=F32), shape(half, tile, dtype=F32)),
        (final, kept, long_table, receiver_dirs, far_head, far_map),
        [vmem] * 5 + [hbm],
        [
            pltpu.VMEM((n_px, tile), F32),
            pltpu.VMEM((depth, rcv_count - head), BF16),
            pltpu.SemaphoreType.DMA((1,)),
        ],
        cost=pl.CostEstimate(flops=2 * 10**9, bytes_accessed=4 * 10**6, transcendentals=0),
    )

    def swapped(array, bits):
        return lax.ppermute(array, "px", [(i, i ^ bits) for i in range(n_px)])

    pair = jnp.concatenate([same, swapped(other, 1)], axis=0)
    pairs = [pair] + [swapped(pair, bits) for bits in range(2, n_px, 2)]
    currents, image = call(
        functools.partial(unpack_kernel, local, (n_px, n_py)),
        "unpack",
        (shape(rows, unit_count), shape(illum_count // n_py, tile, dtype=F32)),
        (back.reshape(rows, unit_count), *pairs),
        [vmem] * (1 + len(pairs)),
    )
    return (currents.reshape(currents_in.shape), image)


def fits(mesh):
    def check(currents_in, far_map):
        n_px, n_py = mesh.shape["px"], mesh.shape["py"]
        total_rows, total_cols, _, illum_count, unit_count = currents_in.shape
        local = (total_rows // n_px) * (total_cols // n_py)
        return (
            illum_count == n_px * n_py
            and local == 4
            and n_px == 8
            and unit_count % 256 == 0
            and far_map.shape[1] == n_px * 256
            and total_cols > 2 * COL_REACH
        )

    return check


def solution(mesh):
    in_specs = (
        P("px", "py", None, None, None),
        P(),
        P(),
        P("px", "py", None),
        P(None, "px", "py"),
        P(),
        P(),
        P("px", "py", None),
        P("px", "py"),
        P("px", "py", None),
    )
    out_specs = (P("px", "py", None, None, None), P("py", "px"))
    check = fits(mesh)

    def run(*args):
        local = illumination_sharded if check(args[0], args[2]) else patch_sharded
        mapped = jax.shard_map(
            local, mesh=mesh, in_specs=in_specs, out_specs=out_specs, check_vma=False
        )
        return mapped(*args)

    return run
```

```python
import functools
import math

import jax
import jax.numpy as jnp
import numpy as np
from jax import lax
from jax.experimental import pallas as pl
from jax.experimental.pallas import tpu as pltpu
from jax.sharding import PartitionSpec as P

SLOTS = 12
ROW_REACH = 1
COL_REACH = 2
OFFSETS = [
    (a, b)
    for a in range(-ROW_REACH, ROW_REACH + 1)
    for b in range(-COL_REACH, COL_REACH + 1)
]
F32 = jnp.float32
BF16 = jnp.bfloat16
HIGH = lax.Precision.HIGHEST
MIB = 1024 * 1024


def padded(block, sides, width, periodic):
    for axis, dim in sides:
        count = lax.axis_size(axis)
        forward = [(i, i + 1) for i in range(count - 1)]
        if periodic:
            forward.append((count - 1, 0))
        backward = [(target, source) for source, target in forward]
        low = lax.ppermute(
            lax.slice_in_dim(block, block.shape[dim] - width, None, axis=dim), axis, forward
        )
        high = lax.ppermute(lax.slice_in_dim(block, 0, width, axis=dim), axis, backward)
        block = jnp.concatenate([low, block, high], axis=dim)
    return block


def combined(rad_pattern):
    upper = jnp.concatenate([rad_pattern[0], rad_pattern[1]], axis=1)
    lower = jnp.concatenate([-rad_pattern[1], rad_pattern[0]], axis=1)
    return jnp.concatenate([upper, lower], axis=0)


def radiate(currents, rad_big):
    row_count, col_count, _, illum_count, unit_count = currents.shape
    stacked = jnp.concatenate([currents[:, :, 0], currents[:, :, 1]], axis=-1)
    flat_rows = stacked.reshape(row_count * col_count * illum_count, 2 * unit_count)
    spectra = jnp.dot(flat_rows, rad_big, preferred_element_type=F32)
    return spectra.reshape(row_count, col_count, illum_count, -1)


def receive(arriving, rad_big):
    row_count, col_count, illum_count, double = arriving.shape
    flat_rows = arriving.reshape(-1, double)
    answer = lax.dot_general(
        flat_rows, rad_big, (((1,), (1,)), ((), ())), preferred_element_type=F32
    )
    return answer.reshape(row_count, col_count, illum_count, -1)


def partner_sum(halo_flat, slot_index, weights):
    height = halo_flat.shape[0]
    onehot = slot_index[:, :, None] == jnp.arange(height, dtype=jnp.int32)[None, None, :]
    coef = jnp.sum(jnp.where(onehot, weights[:, :, None].astype(F32), 0.0), axis=1).astype(BF16)
    return jnp.dot(coef, halo_flat, preferred_element_type=F32)


def bounce(current_now, currents_in, rad_big, reflect, cosine, sine_part, plan):
    row_count, col_count, _, illum_count, unit_count = current_now.shape
    spectra = radiate(current_now, rad_big)
    half_width = spectra.shape[-1] // 2
    spec_re = spectra[..., :half_width]
    spec_im = spectra[..., half_width:]
    out_re = spec_re * cosine + spec_im * sine_part
    out_im = spec_im * cosine - spec_re * sine_part
    outgoing = jnp.stack([out_re, out_im], axis=2).astype(BF16)
    girth_block = padded(outgoing, (("py", 1),), COL_REACH, True)
    slot_index, weights = plan
    rim_block = padded(girth_block, (("px", 0),), ROW_REACH, False)
    halo_flat = rim_block.reshape(-1, 2 * illum_count * half_width)
    collected = partner_sum(halo_flat, slot_index, weights)
    collected = collected.reshape(row_count, col_count, 2, illum_count, half_width)
    col_re = collected[:, :, 0]
    col_im = collected[:, :, 1]
    arr_re = col_re * cosine - col_im * sine_part
    arr_im = col_re * sine_part + col_im * cosine
    arriving = jnp.concatenate([arr_re, -arr_im], axis=-1).astype(BF16)
    answer = receive(arriving, rad_big)
    received = jnp.stack([answer[..., :unit_count], -answer[..., unit_count:]], axis=2)
    updated = currents_in.astype(F32) + reflect[:, :, None, None, :] * received
    return updated.astype(BF16)


def patch_sharded(
    currents_in,
    rad_pattern,
    far_map,
    reflect,
    centres,
    spectral_dirs,
    receiver_dirs,
    partners,
    partner_count,
    pair_weight,
):
    row_count, col_count = partner_count.shape
    high = HIGH
    rad_big = combined(rad_pattern)
    phi = jnp.einsum("dm,dab->abm", spectral_dirs, centres, precision=high)
    cosine = jnp.cos(phi)[:, :, None, :]
    sine_part = jnp.sin(phi)[:, :, None, :]
    total_cols = col_count * lax.axis_size("py")
    total_rows = row_count * lax.axis_size("px")
    base_row = lax.axis_index("px") * row_count
    base_col = lax.axis_index("py") * col_count
    across = col_count + 2 * COL_REACH
    local_col = jnp.arange(col_count, dtype=jnp.int32)[None, :, None]
    live = jnp.arange(SLOTS, dtype=jnp.int32)[None, None, :] < partner_count[:, :, None]
    masked_weight = jnp.where(live, pair_weight, jnp.zeros_like(pair_weight))
    part_row = partners // total_cols
    part_col = partners % total_cols
    near_row = part_row - base_row
    near_col = (part_col - base_col - local_col + COL_REACH) % total_cols + local_col
    slot_index = ((near_row + ROW_REACH) * across + near_col).reshape(row_count * col_count, SLOTS)
    weights = masked_weight.reshape(row_count * col_count, SLOTS)
    plan = (slot_index, weights)
    current_now = currents_in
    for bounce_id in range(2):
        current_now = bounce(current_now, currents_in, rad_big, reflect, cosine, sine_part, plan)
    spectra = radiate(current_now, rad_big).astype(BF16)
    illum_count = spectra.shape[2]
    dir_count = far_map.shape[0]
    rcv_count = far_map.shape[1]
    beams = jnp.dot(spectra.reshape(-1, dir_count), far_map, preferred_element_type=F32)
    beams = beams.reshape(row_count, col_count, illum_count, 2, rcv_count)
    view = jnp.einsum("dr,dab->abr", receiver_dirs, centres, precision=high)
    cos_view = jnp.cos(view)[:, :, None, :]
    sin_view = jnp.sin(view)[:, :, None, :]
    beam_re = beams[:, :, :, 0]
    beam_im = beams[:, :, :, 1]
    far_re = jnp.sum(beam_re * cos_view - beam_im * sin_view, axis=(0, 1))
    far_im = jnp.sum(beam_re * sin_view + beam_im * cos_view, axis=(0, 1))
    factor = 1.0 / math.sqrt(total_rows * total_cols)
    far_part = jnp.stack([far_re, far_im]) * factor
    owned_far = lax.psum(
        lax.psum_scatter(far_part.astype(BF16), "py", scatter_dimension=1, tiled=True), "px"
    ).astype(F32)
    bin_width = rcv_count // lax.axis_size("px")
    rcv_ids = jnp.arange(rcv_count, dtype=jnp.int32)[:, None]
    bin_ids = lax.axis_index("px") * bin_width + jnp.arange(bin_width, dtype=jnp.int32)[None, :]
    turn_angle = (rcv_ids * bin_ids % rcv_count).astype(F32) * (2.0 * math.pi / rcv_count)
    norm_factor = 1.0 / math.sqrt(rcv_count)
    cos_table = jnp.cos(turn_angle) * norm_factor
    sin_table = jnp.sin(turn_angle) * norm_factor
    image_re = jnp.dot(owned_far[0], cos_table, precision=high) + jnp.dot(
        owned_far[1], sin_table, precision=high
    )
    image_im = jnp.dot(owned_far[1], cos_table, precision=high) - jnp.dot(
        owned_far[0], sin_table, precision=high
    )
    isar_image = 0.125 * (image_re * image_re + image_im * image_im)
    return (current_now, isar_image)


def turn_polynomials():
    grid = np.linspace(0.0, 0.25, 4001)
    safe = np.where(grid > 0, np.sqrt(grid), 1.0)
    sine_over = np.where(grid > 0, np.sin(2 * np.pi * safe) / safe, 2 * np.pi)
    cosine = np.cos(2 * np.pi * np.sqrt(grid))
    make = np.polynomial.chebyshev.Chebyshev.fit
    power = np.polynomial.Polynomial
    sine_fit = make(grid, sine_over, 5).convert(kind=power).coef
    cosine_fit = make(grid, cosine, 6).convert(kind=power).coef
    return [float(c) for c in sine_fit], [float(c) for c in cosine_fit]


SINE_FIT, COSINE_FIT = turn_polynomials()


def horner(coefs, x):
    value = jnp.full_like(x, coefs[-1])
    for c in coefs[-2::-1]:
        value = value * x + c
    return value


def cos_sin(turns):
    frac = turns - jnp.floor(turns + 0.5)
    square = frac * frac
    return horner(COSINE_FIT, square), frac * horner(SINE_FIT, square)


def dot(left, right):
    return jnp.dot(left, right, preferred_element_type=F32)


def dot_t(left, right):
    return lax.dot_general(left, right, (((1,), (1,)), ((), ())), preferred_element_type=F32)


def sorter(rows, outer, inner, outer_at=lambda o: o, inner_at=lambda i: i):
    out_id = lax.broadcasted_iota(jnp.int32, (rows, rows), 0)
    in_id = lax.broadcasted_iota(jnp.int32, (rows, rows), 1)
    i = out_id // (2 * outer)
    part = (out_id // outer) % 2
    o = out_id % outer
    column = (outer_at(o) * 2 + part) * inner + inner_at(i)
    return jnp.where(in_id == column, 1.0, 0.0).astype(BF16)


def swapped_digits(value, high, low):
    return value % low * high + value // low


def part_sorter(rows, inner, back):
    first = lax.broadcasted_iota(jnp.int32, (rows, rows), 1 if back else 0)
    second = lax.broadcasted_iota(jnp.int32, (rows, rows), 0 if back else 1)
    half = rows // 2
    part = first // half
    o = (first % half) // inner
    i = first % inner
    return jnp.where(second == (o * 2 + part) * inner + i, 1.0, 0.0).astype(BF16)


def fetch(pairs, sems):
    copies = [
        pltpu.make_async_copy(source, target, sems.at[n])
        for n, (source, target) in enumerate(pairs)
    ]
    for copy in copies:
        copy.start()
    return copies


def pack_kernel(
    total_cols,
    grid_shape,
    cur_hbm,
    reflect_hbm,
    weight_hbm,
    partners_hbm,
    count_hbm,
    centres_hbm,
    out,
    cur,
    reflect,
    weight,
    partners,
    count,
    centres,
    sems,
):
    copies = fetch(
        [
            (cur_hbm, cur),
            (reflect_hbm, reflect),
            (partners_hbm, partners),
            (weight_hbm, weight),
            (count_hbm, count),
            (centres_hbm, centres),
        ],
        sems,
    )
    rows = cur.shape[0]
    local_rows, local_cols, unit_count = reflect.shape
    local = local_rows * local_cols
    base_row = lax.axis_index("px") * local_rows
    base_col = lax.axis_index("py") * local_cols
    row_id = lax.broadcasted_iota(jnp.int32, (rows, rows), 0)
    in_id = lax.broadcasted_iota(jnp.int32, (rows, rows), 1)
    illum_count = rows // (2 * local)
    part, chunk, o = row_id // (rows // 2), row_id % (rows // 2) // local, row_id % local
    column = (o * 2 + part) * illum_count + swapped_digits(chunk, *grid_shape)
    order = jnp.where(in_id == column, 1.0, 0.0).astype(BF16)
    lane = lax.broadcasted_iota(jnp.int32, (local, 128), 1)
    row = lax.broadcasted_iota(jnp.int32, (local, 128), 0)
    patch_row = base_row + row // local_cols
    patch_col = base_col + row % local_cols
    target = jnp.full((local, 128), -1, jnp.int32)
    for o, (a, b) in enumerate(OFFSETS):
        col = patch_col + b
        col = jnp.where(col < 0, col + total_cols, col)
        col = jnp.where(col >= total_cols, col - total_cols, col)
        target = jnp.where(lane == o, (patch_row + a) * total_cols + col, target)
    for copy in copies[1:]:
        copy.wait()
    ids = partners[...].reshape(local, SLOTS)
    weights = weight[...].astype(F32).reshape(local, SLOTS)
    spots = centres[...].reshape(local, 3)
    counts = count[...]
    live = jnp.zeros((local, 128), jnp.int32)
    for r in range(local_rows):
        for c in range(local_cols):
            live = jnp.where(row == r * local_cols + c, counts[r : r + 1, c : c + 1], live)
    small = jnp.zeros((local, 128), F32)
    for s in range(SLOTS):
        hit = (ids[:, s : s + 1] == target) & (live > s)
        small = small + jnp.where(hit, weights[:, s : s + 1], 0.0)
    first = len(OFFSETS)
    for d in range(3):
        spot = spots[:, d : d + 1]
        top = spot.astype(BF16).astype(F32)
        rest = spot - top
        middle = rest.astype(BF16).astype(F32)
        small = jnp.where(lane == first + 3 * d, top, small)
        small = jnp.where(lane == first + 3 * d + 1, middle, small)
        small = jnp.where(lane == first + 3 * d + 2, rest - middle, small)
    refl = reflect[...].reshape(local, unit_count)
    tail = jnp.concatenate([refl, small], axis=1).astype(BF16)
    for n in range(illum_count):
        out[n, :, 2 * unit_count :] = tail
    copies[0].wait()
    both = dot(order, cur[...])
    both = jnp.concatenate([both[: rows // 2], both[rows // 2 :]], axis=1)
    for n in range(illum_count):
        out[n, :, : 2 * unit_count] = both[local * n : local * (n + 1)].astype(BF16)


def table_kernel(rad_hbm, far_hbm, rad, far_head, long_table, sems):
    head = far_hbm.at[:, : far_head.shape[1]]
    copies = fetch([(rad_hbm, rad), (head, far_head)], sems)
    tile = long_table.shape[0]
    row = lax.broadcasted_iota(jnp.int32, (tile, tile), 0)
    column = lax.broadcasted_iota(jnp.int32, (tile, tile), 1)
    cosine, sine = cos_sin(((row * column) % tile).astype(F32) * (1.0 / tile))
    long_table[:, :tile] = cosine.astype(BF16)
    long_table[:, tile:] = sine.astype(BF16)
    for copy in copies:
        copy.wait()


def centres_of(small):
    first = len(OFFSETS)
    centre = []
    for d in range(3):
        at = first + 3 * d
        value = small[:, at : at + 1] + small[:, at + 1 : at + 2] + small[:, at + 2 : at + 3]
        centre.append(value * (0.5 / math.pi))
    return centre


def turns(centre, dirs):
    return centre[0] * dirs[0:1] + centre[1] * dirs[1:2] + centre[2] * dirs[2:3]


def spectrum(current, rad):
    patches = current.shape[0] // 2
    first_part = dot(current, rad[0])
    second_part = dot(current, rad[1])
    return (
        first_part[:patches] - second_part[patches:],
        second_part[:patches] + first_part[patches:],
    )


def bounce_kernel(
    grid_shape,
    local_shape,
    got,
    rad,
    spectral_dirs,
    far_head,
    out_hbm,
    final,
    kept,
    out,
    sems,
):
    del far_head
    unit_count = rad.shape[1]
    patches = got.shape[0] * got.shape[1]
    rows = 2 * patches
    local_rows, local_cols = local_shape
    local = local_rows * local_cols
    n_px, n_py = grid_shape
    total_cols = n_py * local_cols
    whole = jnp.concatenate([got[n].astype(F32) for n in range(got.shape[0])], axis=0)
    start = jnp.concatenate([whole[:, :unit_count], whole[:, unit_count : 2 * unit_count]], axis=0)
    reflect = whole[:, 2 * unit_count : 3 * unit_count]
    small = whole[:, 3 * unit_count :]
    kept[...] = small

    def place(axis):
        ids = lax.broadcasted_iota(jnp.int32, (patches, patches), axis)
        device, within = ids // local, ids % local
        return (
            device // n_py * local_rows + within // local_cols,
            device % n_py * local_cols + within % local_cols,
        )

    (here_row, here_col), (there_row, there_col) = place(0), place(1)
    down = there_row - here_row
    across = there_col - here_col
    across = jnp.where(across > COL_REACH, across - total_cols, across)
    across = jnp.where(across < -COL_REACH, across + total_cols, across)
    near = (down >= -ROW_REACH) & (down <= ROW_REACH)
    near = near & (across >= -COL_REACH) & (across <= COL_REACH)
    offset = (down + ROW_REACH) * (2 * COL_REACH + 1) + across + COL_REACH
    offset = jnp.where(near, offset, -1)
    coef = jnp.zeros((patches, patches), F32)
    for o in range(len(OFFSETS)):
        coef = jnp.where(offset == o, small[:, o : o + 1], coef)
    coef = coef.astype(BF16)
    cosine, sine = cos_sin(turns(centres_of(small), spectral_dirs[...]))
    current = start.astype(BF16)
    for _ in range(2):
        spec_re, spec_im = spectrum(current, rad)
        outgoing = jnp.concatenate(
            [spec_re * cosine + spec_im * sine, spec_im * cosine - spec_re * sine], axis=1
        ).astype(BF16)
        collected = dot(coef, outgoing)
        width = collected.shape[1] // 2
        col_re = collected[:, :width]
        col_im = collected[:, width:]
        arriving = jnp.concatenate(
            [col_re * cosine - col_im * sine, col_re * sine + col_im * cosine], axis=0
        ).astype(BF16)
        first_part = dot_t(arriving, rad[0])
        second_part = dot_t(arriving, rad[1])
        recv_re = first_part[:patches] - second_part[patches:]
        recv_im = second_part[:patches] + first_part[patches:]
        current = jnp.concatenate(
            [start[:patches] + reflect * recv_re, start[patches:] + reflect * recv_im], axis=0
        ).astype(BF16)
    out[...] = dot(part_sorter(rows, local, True), current).astype(BF16)
    out_copy = pltpu.make_async_copy(out, out_hbm, sems.at[0])
    out_copy.start()
    final[...] = jnp.concatenate(spectrum(current, rad), axis=0).astype(BF16)
    out_copy.wait()


def image_kernel(
    root_scale,
    final,
    kept,
    long_table,
    receiver_dirs,
    far_head,
    far_hbm,
    same,
    other,
    image,
    far_rest,
    sems,
):
    head = far_head.shape[1]
    rest_copy = pltpu.make_async_copy(far_hbm.at[:, head:], far_rest, sems.at[0])
    rest_copy.start()
    splits, tile = image.shape
    patches = kept.shape[0]
    centre = centres_of(kept[...])
    far_re, far_im = [], []
    for t in range(splits):
        cut = slice(tile * t, tile * (t + 1))
        if tile * t == head:
            rest_copy.wait()
        if tile * t < head:
            beams = dot(final[...], far_head[:, cut])
        else:
            beams = dot(final[...], far_rest[:, tile * t - head : tile * (t + 1) - head])
        cos_view, sin_view = cos_sin(turns(centre, receiver_dirs[:, cut]))
        beam_re = beams[:patches]
        beam_im = beams[patches:]
        far_re.append(jnp.sum(beam_re * cos_view - beam_im * sin_view, axis=0, keepdims=True))
        far_im.append(jnp.sum(beam_re * sin_view + beam_im * cos_view, axis=0, keepdims=True))
    row = lax.broadcasted_iota(jnp.int32, (splits, 128), 0)
    column = lax.broadcasted_iota(jnp.int32, (splits, 128), 1)
    short_cos, short_sin = cos_sin((row * column % splits).astype(F32) * (1.0 / splits))
    row = lax.broadcasted_iota(jnp.int32, (splits, tile), 0)
    column = lax.broadcasted_iota(jnp.int32, (splits, tile), 1)
    twist_cos, twist_sin = cos_sin((row * column).astype(F32) * (1.0 / (splits * tile)))
    mid_re = jnp.zeros((splits, tile), F32)
    mid_im = jnp.zeros((splits, tile), F32)
    for t in range(splits):
        c = short_cos[:, t : t + 1] * root_scale
        s = short_sin[:, t : t + 1] * root_scale
        mid_re = mid_re + (c * far_re[t] + s * far_im[t])
        mid_im = mid_im + (c * far_im[t] - s * far_re[t])
    tw_re = mid_re * twist_cos + mid_im * twist_sin
    tw_im = mid_im * twist_cos - mid_re * twist_sin
    both = jnp.concatenate([tw_re, tw_im], axis=0)
    upper = both.astype(BF16)
    lower = (both - upper.astype(F32)).astype(BF16)
    answer = dot(jnp.concatenate([upper, lower], axis=0), long_table[...])
    answer = answer[: 2 * splits] + answer[2 * splits :]
    image_re = answer[:splits, :tile] + answer[splits:, tile:]
    image_im = answer[splits:, :tile] - answer[:splits, tile:]
    power = image_re * image_re + image_im * image_im
    each = tile // splits
    upper = power.astype(BF16)
    lower = (power - upper.astype(F32)).astype(BF16)
    lane = lax.broadcasted_iota(jnp.int32, (2 * splits, tile), 1)
    row = lax.broadcasted_iota(jnp.int32, (2 * splits, tile), 0)
    fast = jnp.where(lane % splits == row % splits, 1.0, 0.0).astype(BF16)
    spread = lax.dot_general(
        jnp.concatenate([upper, lower], axis=0),
        fast,
        (((0,), (0,)), ((), ())),
        preferred_element_type=F32,
    )
    row = lax.broadcasted_iota(jnp.int32, (tile, tile), 0)
    column = lax.broadcasted_iota(jnp.int32, (tile, tile), 1)
    spread = jnp.where(row % each == column // splits, spread, 0.0)
    image[...] = jnp.sum(spread.reshape(splits, each, tile), axis=1)
    me = lax.axis_index("px")
    for n in range(splits // 2):
        same[n : n + 1, :] = image[pl.ds(me ^ (2 * n), 1), :]
        other[n : n + 1, :] = image[pl.ds(me ^ (2 * n + 1), 1), :]


def unpack_kernel(local, grid_shape, got, *refs):
    pairs, (currents, image) = refs[:-2], refs[-2:]
    rows = currents.shape[0]
    n_px, n_py = grid_shape
    order = sorter(
        rows, rows // (2 * local), local, outer_at=lambda o: swapped_digits(o, n_py, n_px)
    )
    currents[...] = dot(order, got[...]).astype(BF16)
    me = lax.axis_index("px")
    row = lax.broadcasted_iota(jnp.int32, image.shape, 0)
    whole = jnp.zeros(image.shape, F32)
    for n in range(n_px):
        at = n // 2 + n % 2 * (n_px // 2)
        mine = pairs[n // 2][at : at + 1, :]
        whole = jnp.where(row == (me ^ n), mine, whole)
    image[...] = whole


def call(kernel, name, outs, operands, spaces, scratch=(), cost=None, limit=32, left=()):
    specs = jax.tree.map(lambda _: pl.BlockSpec(memory_space=pltpu.VMEM), outs)
    if left:
        specs = tuple(
            pl.BlockSpec(memory_space=pl.ANY) if n in left else s for n, s in enumerate(specs)
        )
    operands = [
        pltpu.with_memory_space_constraint(a, pltpu.HBM) if m is pltpu.HBM else a
        for a, m in zip(operands, spaces)
    ]
    return pl.pallas_call(
        kernel,
        out_shape=outs,
        in_specs=[pl.BlockSpec(memory_space=m) for m in spaces],
        out_specs=specs,
        scratch_shapes=list(scratch),
        compiler_params=pltpu.CompilerParams(vmem_limit_bytes=limit * MIB),
        cost_estimate=cost,
        name=name,
    )(*operands)


def illumination_sharded(
    currents_in,
    rad_pattern,
    far_map,
    reflect,
    centres,
    spectral_dirs,
    receiver_dirs,
    partners,
    partner_count,
    pair_weight,
):
    local_rows, local_cols, _, illum_count, unit_count = currents_in.shape
    n_px, n_py = lax.axis_size("px"), lax.axis_size("py")
    devices = n_px * n_py
    local = local_rows * local_cols
    rows = 2 * local * illum_count
    total_cols = local_cols * n_py
    patches = local_rows * n_px * total_cols
    rcv_count = far_map.shape[1]
    tile = rcv_count // n_px
    block = 2 * local
    axes = ("px", "py")
    vmem, hbm = pltpu.VMEM, pltpu.HBM

    def like(*arrays):
        scratch = [pltpu.VMEM(a.shape, a.dtype) for a in arrays]
        return scratch + [pltpu.SemaphoreType.DMA((len(arrays),))]

    def shape(*dims, dtype=BF16):
        return jax.ShapeDtypeStruct(dims, dtype)

    sent_width = 3 * unit_count + 128
    sources = (
        currents_in.reshape(rows, unit_count),
        reflect,
        pair_weight,
        partners,
        partner_count,
        jnp.transpose(centres, (1, 2, 0)),
    )
    packed = call(
        functools.partial(pack_kernel, total_cols, (n_px, n_py)),
        "pack",
        shape(devices, local, sent_width),
        sources,
        [hbm] * 6,
        like(*sources),
    )
    got = lax.all_to_all(packed, axes, 0, 0, tiled=True)
    depth, head = far_map.shape[0], rcv_count // 2
    rad, far_head, long_table = call(
        table_kernel,
        "table",
        (shape(*rad_pattern.shape), shape(depth, head), shape(tile, 2 * tile)),
        (rad_pattern, far_map),
        [hbm] * 2,
        [pltpu.SemaphoreType.DMA((2,))],
        cost=pl.CostEstimate(flops=10**7, bytes_accessed=4 * 10**6, transcendentals=0),
    )
    answer, final, kept = call(
        functools.partial(bounce_kernel, (n_px, n_py), (local_rows, local_cols)),
        "bounces",
        (shape(rows, unit_count), shape(rows, unit_count), shape(patches, 128, dtype=F32)),
        (got, rad, spectral_dirs, far_head),
        [vmem] * 3 + [pl.ANY],
        [pltpu.VMEM((rows, unit_count), BF16), pltpu.SemaphoreType.DMA((1,))],
        left=(0,),
    )
    back = lax.all_to_all(answer.reshape(devices, block, unit_count), axes, 0, 0, tiled=True)
    half = n_px // 2
    same, other = call(
        functools.partial(image_kernel, math.sqrt(0.125 / (patches * rcv_count))),
        "image",
        (shape(half, tile, dtype=F32), shape(half, tile, dtype=F32)),
        (final, kept, long_table, receiver_dirs, far_head, far_map),
        [vmem] * 5 + [hbm],
        [
            pltpu.VMEM((n_px, tile), F32),
            pltpu.VMEM((depth, rcv_count - head), BF16),
            pltpu.SemaphoreType.DMA((1,)),
        ],
        cost=pl.CostEstimate(flops=2 * 10**9, bytes_accessed=4 * 10**6, transcendentals=0),
    )

    def swapped(array, bits):
        return lax.ppermute(array, "px", [(i, i ^ bits) for i in range(n_px)])

    pair = jnp.concatenate([same, swapped(other, 1)], axis=0)
    pairs = [pair] + [swapped(pair, bits) for bits in range(2, n_px, 2)]
    currents, image = call(
        functools.partial(unpack_kernel, local, (n_px, n_py)),
        "unpack",
        (shape(rows, unit_count), shape(illum_count // n_py, tile, dtype=F32)),
        (back.reshape(rows, unit_count), *pairs),
        [vmem] * (1 + len(pairs)),
    )
    return (currents.reshape(currents_in.shape), image)


def fits(mesh):
    def check(currents_in, far_map):
        n_px, n_py = mesh.shape["px"], mesh.shape["py"]
        total_rows, total_cols, _, illum_count, unit_count = currents_in.shape
        local = (total_rows // n_px) * (total_cols // n_py)
        return (
            illum_count == n_px * n_py
            and local == 4
            and n_px == 8
            and unit_count % 256 == 0
            and far_map.shape[1] == n_px * 256
            and total_cols > 2 * COL_REACH
        )

    return check


def solution(mesh):
    in_specs = (
        P("px", "py", None, None, None),
        P(),
        P(),
        P("px", "py", None),
        P(None, "px", "py"),
        P(),
        P(),
        P("px", "py", None),
        P("px", "py"),
        P("px", "py", None),
    )
    out_specs = (P("px", "py", None, None, None), P("py", "px"))
    check = fits(mesh)

    def run(*args):
        local = illumination_sharded if check(args[0], args[2]) else patch_sharded
        mapped = jax.shard_map(
            local, mesh=mesh, in_specs=in_specs, out_specs=out_specs, check_vma=False
        )
        return mapped(*args)

    return run
```

```python
import functools
import math

import jax
import jax.numpy as jnp
import numpy as np
from jax import lax
from jax.experimental import pallas as pl
from jax.experimental.pallas import tpu as pltpu
from jax.sharding import PartitionSpec as P

SLOTS = 12
ROW_REACH = 1
COL_REACH = 2
OFFSETS = [
    (a, b)
    for a in range(-ROW_REACH, ROW_REACH + 1)
    for b in range(-COL_REACH, COL_REACH + 1)
]
F32 = jnp.float32
BF16 = jnp.bfloat16
HIGH = lax.Precision.HIGHEST
MIB = 1024 * 1024


def padded(block, sides, width, periodic):
    for axis, dim in sides:
        count = lax.axis_size(axis)
        forward = [(i, i + 1) for i in range(count - 1)]
        if periodic:
            forward.append((count - 1, 0))
        backward = [(target, source) for source, target in forward]
        low = lax.ppermute(
            lax.slice_in_dim(block, block.shape[dim] - width, None, axis=dim), axis, forward
        )
        high = lax.ppermute(lax.slice_in_dim(block, 0, width, axis=dim), axis, backward)
        block = jnp.concatenate([low, block, high], axis=dim)
    return block


def combined(rad_pattern):
    upper = jnp.concatenate([rad_pattern[0], rad_pattern[1]], axis=1)
    lower = jnp.concatenate([-rad_pattern[1], rad_pattern[0]], axis=1)
    return jnp.concatenate([upper, lower], axis=0)


def radiate(currents, rad_big):
    row_count, col_count, _, illum_count, unit_count = currents.shape
    stacked = jnp.concatenate([currents[:, :, 0], currents[:, :, 1]], axis=-1)
    flat_rows = stacked.reshape(row_count * col_count * illum_count, 2 * unit_count)
    spectra = jnp.dot(flat_rows, rad_big, preferred_element_type=F32)
    return spectra.reshape(row_count, col_count, illum_count, -1)


def receive(arriving, rad_big):
    row_count, col_count, illum_count, double = arriving.shape
    flat_rows = arriving.reshape(-1, double)
    answer = lax.dot_general(
        flat_rows, rad_big, (((1,), (1,)), ((), ())), preferred_element_type=F32
    )
    return answer.reshape(row_count, col_count, illum_count, -1)


def partner_sum(halo_flat, slot_index, weights):
    height = halo_flat.shape[0]
    onehot = slot_index[:, :, None] == jnp.arange(height, dtype=jnp.int32)[None, None, :]
    coef = jnp.sum(jnp.where(onehot, weights[:, :, None].astype(F32), 0.0), axis=1).astype(BF16)
    return jnp.dot(coef, halo_flat, preferred_element_type=F32)


def bounce(current_now, currents_in, rad_big, reflect, cosine, sine_part, plan):
    row_count, col_count, _, illum_count, unit_count = current_now.shape
    spectra = radiate(current_now, rad_big)
    half_width = spectra.shape[-1] // 2
    spec_re = spectra[..., :half_width]
    spec_im = spectra[..., half_width:]
    out_re = spec_re * cosine + spec_im * sine_part
    out_im = spec_im * cosine - spec_re * sine_part
    outgoing = jnp.stack([out_re, out_im], axis=2).astype(BF16)
    girth_block = padded(outgoing, (("py", 1),), COL_REACH, True)
    slot_index, weights = plan
    rim_block = padded(girth_block, (("px", 0),), ROW_REACH, False)
    halo_flat = rim_block.reshape(-1, 2 * illum_count * half_width)
    collected = partner_sum(halo_flat, slot_index, weights)
    collected = collected.reshape(row_count, col_count, 2, illum_count, half_width)
    col_re = collected[:, :, 0]
    col_im = collected[:, :, 1]
    arr_re = col_re * cosine - col_im * sine_part
    arr_im = col_re * sine_part + col_im * cosine
    arriving = jnp.concatenate([arr_re, -arr_im], axis=-1).astype(BF16)
    answer = receive(arriving, rad_big)
    received = jnp.stack([answer[..., :unit_count], -answer[..., unit_count:]], axis=2)
    updated = currents_in.astype(F32) + reflect[:, :, None, None, :] * received
    return updated.astype(BF16)


def patch_sharded(
    currents_in,
    rad_pattern,
    far_map,
    reflect,
    centres,
    spectral_dirs,
    receiver_dirs,
    partners,
    partner_count,
    pair_weight,
):
    row_count, col_count = partner_count.shape
    high = HIGH
    rad_big = combined(rad_pattern)
    phi = jnp.einsum("dm,dab->abm", spectral_dirs, centres, precision=high)
    cosine = jnp.cos(phi)[:, :, None, :]
    sine_part = jnp.sin(phi)[:, :, None, :]
    total_cols = col_count * lax.axis_size("py")
    total_rows = row_count * lax.axis_size("px")
    base_row = lax.axis_index("px") * row_count
    base_col = lax.axis_index("py") * col_count
    across = col_count + 2 * COL_REACH
    local_col = jnp.arange(col_count, dtype=jnp.int32)[None, :, None]
    live = jnp.arange(SLOTS, dtype=jnp.int32)[None, None, :] < partner_count[:, :, None]
    masked_weight = jnp.where(live, pair_weight, jnp.zeros_like(pair_weight))
    part_row = partners // total_cols
    part_col = partners % total_cols
    near_row = part_row - base_row
    near_col = (part_col - base_col - local_col + COL_REACH) % total_cols + local_col
    slot_index = ((near_row + ROW_REACH) * across + near_col).reshape(row_count * col_count, SLOTS)
    weights = masked_weight.reshape(row_count * col_count, SLOTS)
    plan = (slot_index, weights)
    current_now = currents_in
    for bounce_id in range(2):
        current_now = bounce(current_now, currents_in, rad_big, reflect, cosine, sine_part, plan)
    spectra = radiate(current_now, rad_big).astype(BF16)
    illum_count = spectra.shape[2]
    dir_count = far_map.shape[0]
    rcv_count = far_map.shape[1]
    beams = jnp.dot(spectra.reshape(-1, dir_count), far_map, preferred_element_type=F32)
    beams = beams.reshape(row_count, col_count, illum_count, 2, rcv_count)
    view = jnp.einsum("dr,dab->abr", receiver_dirs, centres, precision=high)
    cos_view = jnp.cos(view)[:, :, None, :]
    sin_view = jnp.sin(view)[:, :, None, :]
    beam_re = beams[:, :, :, 0]
    beam_im = beams[:, :, :, 1]
    far_re = jnp.sum(beam_re * cos_view - beam_im * sin_view, axis=(0, 1))
    far_im = jnp.sum(beam_re * sin_view + beam_im * cos_view, axis=(0, 1))
    factor = 1.0 / math.sqrt(total_rows * total_cols)
    far_part = jnp.stack([far_re, far_im]) * factor
    owned_far = lax.psum(
        lax.psum_scatter(far_part.astype(BF16), "py", scatter_dimension=1, tiled=True), "px"
    ).astype(F32)
    bin_width = rcv_count // lax.axis_size("px")
    rcv_ids = jnp.arange(rcv_count, dtype=jnp.int32)[:, None]
    bin_ids = lax.axis_index("px") * bin_width + jnp.arange(bin_width, dtype=jnp.int32)[None, :]
    turn_angle = (rcv_ids * bin_ids % rcv_count).astype(F32) * (2.0 * math.pi / rcv_count)
    norm_factor = 1.0 / math.sqrt(rcv_count)
    cos_table = jnp.cos(turn_angle) * norm_factor
    sin_table = jnp.sin(turn_angle) * norm_factor
    image_re = jnp.dot(owned_far[0], cos_table, precision=high) + jnp.dot(
        owned_far[1], sin_table, precision=high
    )
    image_im = jnp.dot(owned_far[1], cos_table, precision=high) - jnp.dot(
        owned_far[0], sin_table, precision=high
    )
    isar_image = 0.125 * (image_re * image_re + image_im * image_im)
    return (current_now, isar_image)


def turn_polynomials():
    grid = np.linspace(0.0, 0.25, 4001)
    safe = np.where(grid > 0, np.sqrt(grid), 1.0)
    sine_over = np.where(grid > 0, np.sin(2 * np.pi * safe) / safe, 2 * np.pi)
    cosine = np.cos(2 * np.pi * np.sqrt(grid))
    make = np.polynomial.chebyshev.Chebyshev.fit
    power = np.polynomial.Polynomial
    sine_fit = make(grid, sine_over, 5).convert(kind=power).coef
    cosine_fit = make(grid, cosine, 6).convert(kind=power).coef
    return [float(c) for c in sine_fit], [float(c) for c in cosine_fit]


SINE_FIT, COSINE_FIT = turn_polynomials()


def horner(coefs, x):
    value = jnp.full_like(x, coefs[-1])
    for c in coefs[-2::-1]:
        value = value * x + c
    return value


def cos_sin(turns):
    frac = turns - jnp.floor(turns + 0.5)
    square = frac * frac
    return horner(COSINE_FIT, square), frac * horner(SINE_FIT, square)


def dot(left, right):
    return jnp.dot(left, right, preferred_element_type=F32)


def dot_t(left, right):
    return lax.dot_general(left, right, (((1,), (1,)), ((), ())), preferred_element_type=F32)


def sorter(rows, outer, inner, outer_at=lambda o: o, inner_at=lambda i: i):
    out_id = lax.broadcasted_iota(jnp.int32, (rows, rows), 0)
    in_id = lax.broadcasted_iota(jnp.int32, (rows, rows), 1)
    i = out_id // (2 * outer)
    part = (out_id // outer) % 2
    o = out_id % outer
    column = (outer_at(o) * 2 + part) * inner + inner_at(i)
    return jnp.where(in_id == column, 1.0, 0.0).astype(BF16)


def swapped_digits(value, high, low):
    return value % low * high + value // low


def part_sorter(rows, inner, back):
    first = lax.broadcasted_iota(jnp.int32, (rows, rows), 1 if back else 0)
    second = lax.broadcasted_iota(jnp.int32, (rows, rows), 0 if back else 1)
    half = rows // 2
    part = first // half
    o = (first % half) // inner
    i = first % inner
    return jnp.where(second == (o * 2 + part) * inner + i, 1.0, 0.0).astype(BF16)


def fetch(pairs, sems):
    copies = [
        pltpu.make_async_copy(source, target, sems.at[n])
        for n, (source, target) in enumerate(pairs)
    ]
    for copy in copies:
        copy.start()
    return copies


def pack_kernel(
    total_cols,
    grid_shape,
    cur_hbm,
    reflect_hbm,
    weight_hbm,
    partners_hbm,
    count_hbm,
    centres_hbm,
    out,
    cur,
    reflect,
    weight,
    partners,
    count,
    centres,
    sems,
):
    copies = fetch(
        [
            (cur_hbm, cur),
            (reflect_hbm, reflect),
            (partners_hbm, partners),
            (weight_hbm, weight),
            (count_hbm, count),
            (centres_hbm, centres),
        ],
        sems,
    )
    rows = cur.shape[0]
    local_rows, local_cols, unit_count = reflect.shape
    local = local_rows * local_cols
    base_row = lax.axis_index("px") * local_rows
    base_col = lax.axis_index("py") * local_cols
    row_id = lax.broadcasted_iota(jnp.int32, (rows, rows), 0)
    in_id = lax.broadcasted_iota(jnp.int32, (rows, rows), 1)
    illum_count = rows // (2 * local)
    part, chunk, o = row_id // (rows // 2), row_id % (rows // 2) // local, row_id % local
    column = (o * 2 + part) * illum_count + swapped_digits(chunk, *grid_shape)
    order = jnp.where(in_id == column, 1.0, 0.0).astype(BF16)
    lane = lax.broadcasted_iota(jnp.int32, (local, 128), 1)
    row = lax.broadcasted_iota(jnp.int32, (local, 128), 0)
    patch_row = base_row + row // local_cols
    patch_col = base_col + row % local_cols
    target = jnp.full((local, 128), -1, jnp.int32)
    for o, (a, b) in enumerate(OFFSETS):
        col = patch_col + b
        col = jnp.where(col < 0, col + total_cols, col)
        col = jnp.where(col >= total_cols, col - total_cols, col)
        target = jnp.where(lane == o, (patch_row + a) * total_cols + col, target)
    for copy in copies[1:]:
        copy.wait()
    ids = partners[...].reshape(local, SLOTS)
    weights = weight[...].astype(F32).reshape(local, SLOTS)
    spots = centres[...].reshape(local, 3)
    counts = count[...]
    live = jnp.zeros((local, 128), jnp.int32)
    for r in range(local_rows):
        for c in range(local_cols):
            live = jnp.where(row == r * local_cols + c, counts[r : r + 1, c : c + 1], live)
    small = jnp.zeros((local, 128), F32)
    for s in range(SLOTS):
        hit = (ids[:, s : s + 1] == target) & (live > s)
        small = small + jnp.where(hit, weights[:, s : s + 1], 0.0)
    first = len(OFFSETS)
    for d in range(3):
        spot = spots[:, d : d + 1]
        top = spot.astype(BF16).astype(F32)
        rest = spot - top
        middle = rest.astype(BF16).astype(F32)
        small = jnp.where(lane == first + 3 * d, top, small)
        small = jnp.where(lane == first + 3 * d + 1, middle, small)
        small = jnp.where(lane == first + 3 * d + 2, rest - middle, small)
    refl = reflect[...].reshape(local, unit_count)
    tail = jnp.concatenate([refl, small], axis=1).astype(BF16)
    for n in range(illum_count):
        out[n, :, 2 * unit_count :] = tail
    copies[0].wait()
    both = dot(order, cur[...])
    both = jnp.concatenate([both[: rows // 2], both[rows // 2 :]], axis=1)
    for n in range(illum_count):
        out[n, :, : 2 * unit_count] = both[local * n : local * (n + 1)].astype(BF16)


def table_kernel(rad_hbm, far_hbm, rad, far_head, long_table, sems):
    head = far_hbm.at[:, : far_head.shape[1]]
    copies = fetch([(rad_hbm, rad), (head, far_head)], sems)
    tile = long_table.shape[0]
    row = lax.broadcasted_iota(jnp.int32, (tile, tile), 0)
    column = lax.broadcasted_iota(jnp.int32, (tile, tile), 1)
    cosine, sine = cos_sin(((row * column) % tile).astype(F32) * (1.0 / tile))
    long_table[:, :tile] = cosine.astype(BF16)
    long_table[:, tile:] = sine.astype(BF16)
    for copy in copies:
        copy.wait()


def centres_of(small):
    first = len(OFFSETS)
    centre = []
    for d in range(3):
        at = first + 3 * d
        value = small[:, at : at + 1] + small[:, at + 1 : at + 2] + small[:, at + 2 : at + 3]
        centre.append(value * (0.5 / math.pi))
    return centre


def turns(centre, dirs):
    return centre[0] * dirs[0:1] + centre[1] * dirs[1:2] + centre[2] * dirs[2:3]


def spectrum(current, rad):
    patches = current.shape[0] // 2
    first_part = dot(current, rad[0])
    second_part = dot(current, rad[1])
    return (
        first_part[:patches] - second_part[patches:],
        second_part[:patches] + first_part[patches:],
    )


def bounce_kernel(
    grid_shape,
    local_shape,
    got,
    rad,
    spectral_dirs,
    far_head,
    out_hbm,
    final,
    kept,
    out,
    sems,
):
    del far_head
    unit_count = rad.shape[1]
    patches = got.shape[0] * got.shape[1]
    rows = 2 * patches
    local_rows, local_cols = local_shape
    local = local_rows * local_cols
    n_px, n_py = grid_shape
    total_cols = n_py * local_cols
    whole = jnp.concatenate([got[n].astype(F32) for n in range(got.shape[0])], axis=0)
    start = jnp.concatenate([whole[:, :unit_count], whole[:, unit_count : 2 * unit_count]], axis=0)
    reflect = whole[:, 2 * unit_count : 3 * unit_count]
    small = whole[:, 3 * unit_count :]
    kept[...] = small

    def place(axis):
        ids = lax.broadcasted_iota(jnp.int32, (patches, patches), axis)
        device, within = ids // local, ids % local
        return (
            device // n_py * local_rows + within // local_cols,
            device % n_py * local_cols + within % local_cols,
        )

    (here_row, here_col), (there_row, there_col) = place(0), place(1)
    down = there_row - here_row
    across = there_col - here_col
    across = jnp.where(across > COL_REACH, across - total_cols, across)
    across = jnp.where(across < -COL_REACH, across + total_cols, across)
    near = (down >= -ROW_REACH) & (down <= ROW_REACH)
    near = near & (across >= -COL_REACH) & (across <= COL_REACH)
    offset = (down + ROW_REACH) * (2 * COL_REACH + 1) + across + COL_REACH
    offset = jnp.where(near, offset, -1)
    coef = jnp.zeros((patches, patches), F32)
    for o in range(len(OFFSETS)):
        coef = jnp.where(offset == o, small[:, o : o + 1], coef)
    coef = coef.astype(BF16)
    cosine, sine = cos_sin(turns(centres_of(small), spectral_dirs[...]))
    current = start.astype(BF16)
    for _ in range(2):
        spec_re, spec_im = spectrum(current, rad)
        outgoing = jnp.concatenate(
            [spec_re * cosine + spec_im * sine, spec_im * cosine - spec_re * sine], axis=1
        ).astype(BF16)
        collected = dot(coef, outgoing)
        width = collected.shape[1] // 2
        col_re = collected[:, :width]
        col_im = collected[:, width:]
        arriving = jnp.concatenate(
            [col_re * cosine - col_im * sine, col_re * sine + col_im * cosine], axis=0
        ).astype(BF16)
        first_part = dot_t(arriving, rad[0])
        second_part = dot_t(arriving, rad[1])
        recv_re = first_part[:patches] - second_part[patches:]
        recv_im = second_part[:patches] + first_part[patches:]
        current = jnp.concatenate(
            [start[:patches] + reflect * recv_re, start[patches:] + reflect * recv_im], axis=0
        ).astype(BF16)
    out[...] = dot(part_sorter(rows, local, True), current).astype(BF16)
    out_copy = pltpu.make_async_copy(out, out_hbm, sems.at[0])
    out_copy.start()
    final[...] = jnp.concatenate(spectrum(current, rad), axis=0).astype(BF16)
    out_copy.wait()


def image_kernel(
    root_scale,
    final,
    kept,
    long_table,
    receiver_dirs,
    far_head,
    far_hbm,
    same,
    other,
    image,
    far_rest,
    cos_rest,
    sin_rest,
    sems,
):
    head = far_head.shape[1]
    rest_copy = pltpu.make_async_copy(far_hbm.at[:, head:], far_rest, sems.at[0])
    rest_copy.start()
    splits, tile = image.shape
    patches = kept.shape[0]
    centre = centres_of(kept[...])
    far_re, far_im = [], []
    for t in range(splits):
        cut = slice(tile * t, tile * (t + 1))
        if tile * t == head:
            for n in range(t, splits):
                at = slice(tile * n, tile * (n + 1))
                to = slice(tile * (n - t), tile * (n - t + 1))
                cos_rest[:, to], sin_rest[:, to] = cos_sin(turns(centre, receiver_dirs[:, at]))
            rest_copy.wait()
        if tile * t < head:
            beams = dot(final[...], far_head[:, cut])
        else:
            beams = dot(final[...], far_rest[:, tile * t - head : tile * (t + 1) - head])
        if tile * t < head:
            cos_view, sin_view = cos_sin(turns(centre, receiver_dirs[:, cut]))
        else:
            to = slice(tile * t - head, tile * (t + 1) - head)
            cos_view, sin_view = cos_rest[:, to], sin_rest[:, to]
        beam_re = beams[:patches]
        beam_im = beams[patches:]
        far_re.append(jnp.sum(beam_re * cos_view - beam_im * sin_view, axis=0, keepdims=True))
        far_im.append(jnp.sum(beam_re * sin_view + beam_im * cos_view, axis=0, keepdims=True))
    row = lax.broadcasted_iota(jnp.int32, (splits, 128), 0)
    column = lax.broadcasted_iota(jnp.int32, (splits, 128), 1)
    short_cos, short_sin = cos_sin((row * column % splits).astype(F32) * (1.0 / splits))
    row = lax.broadcasted_iota(jnp.int32, (splits, tile), 0)
    column = lax.broadcasted_iota(jnp.int32, (splits, tile), 1)
    twist_cos, twist_sin = cos_sin((row * column).astype(F32) * (1.0 / (splits * tile)))
    mid_re = jnp.zeros((splits, tile), F32)
    mid_im = jnp.zeros((splits, tile), F32)
    for t in range(splits):
        c = short_cos[:, t : t + 1] * root_scale
        s = short_sin[:, t : t + 1] * root_scale
        mid_re = mid_re + (c * far_re[t] + s * far_im[t])
        mid_im = mid_im + (c * far_im[t] - s * far_re[t])
    tw_re = mid_re * twist_cos + mid_im * twist_sin
    tw_im = mid_im * twist_cos - mid_re * twist_sin
    both = jnp.concatenate([tw_re, tw_im], axis=0)
    upper = both.astype(BF16)
    lower = (both - upper.astype(F32)).astype(BF16)
    answer = dot(jnp.concatenate([upper, lower], axis=0), long_table[...])
    answer = answer[: 2 * splits] + answer[2 * splits :]
    image_re = answer[:splits, :tile] + answer[splits:, tile:]
    image_im = answer[splits:, :tile] - answer[:splits, tile:]
    power = image_re * image_re + image_im * image_im
    each = tile // splits
    upper = power.astype(BF16)
    lower = (power - upper.astype(F32)).astype(BF16)
    lane = lax.broadcasted_iota(jnp.int32, (2 * splits, tile), 1)
    row = lax.broadcasted_iota(jnp.int32, (2 * splits, tile), 0)
    fast = jnp.where(lane % splits == row % splits, 1.0, 0.0).astype(BF16)
    spread = lax.dot_general(
        jnp.concatenate([upper, lower], axis=0),
        fast,
        (((0,), (0,)), ((), ())),
        preferred_element_type=F32,
    )
    row = lax.broadcasted_iota(jnp.int32, (tile, tile), 0)
    column = lax.broadcasted_iota(jnp.int32, (tile, tile), 1)
    spread = jnp.where(row % each == column // splits, spread, 0.0)
    image[...] = jnp.sum(spread.reshape(splits, each, tile), axis=1)
    me = lax.axis_index("px")
    for n in range(splits // 2):
        same[n : n + 1, :] = image[pl.ds(me ^ (2 * n), 1), :]
        other[n : n + 1, :] = image[pl.ds(me ^ (2 * n + 1), 1), :]


def unpack_kernel(local, grid_shape, got, *refs):
    pairs, (currents, image) = refs[:-2], refs[-2:]
    rows = currents.shape[0]
    n_px, n_py = grid_shape
    order = sorter(
        rows, rows // (2 * local), local, outer_at=lambda o: swapped_digits(o, n_py, n_px)
    )
    currents[...] = dot(order, got[...]).astype(BF16)
    me = lax.axis_index("px")
    row = lax.broadcasted_iota(jnp.int32, image.shape, 0)
    whole = jnp.zeros(image.shape, F32)
    for n in range(n_px):
        at = n // 2 + n % 2 * (n_px // 2)
        mine = pairs[n // 2][at : at + 1, :]
        whole = jnp.where(row == (me ^ n), mine, whole)
    image[...] = whole


def call(kernel, name, outs, operands, spaces, scratch=(), cost=None, limit=32, left=()):
    specs = jax.tree.map(lambda _: pl.BlockSpec(memory_space=pltpu.VMEM), outs)
    if left:
        specs = tuple(
            pl.BlockSpec(memory_space=pl.ANY) if n in left else s for n, s in enumerate(specs)
        )
    operands = [
        pltpu.with_memory_space_constraint(a, pltpu.HBM) if m is pltpu.HBM else a
        for a, m in zip(operands, spaces)
    ]
    return pl.pallas_call(
        kernel,
        out_shape=outs,
        in_specs=[pl.BlockSpec(memory_space=m) for m in spaces],
        out_specs=specs,
        scratch_shapes=list(scratch),
        compiler_params=pltpu.CompilerParams(vmem_limit_bytes=limit * MIB),
        cost_estimate=cost,
        name=name,
    )(*operands)


def illumination_sharded(
    currents_in,
    rad_pattern,
    far_map,
    reflect,
    centres,
    spectral_dirs,
    receiver_dirs,
    partners,
    partner_count,
    pair_weight,
):
    local_rows, local_cols, _, illum_count, unit_count = currents_in.shape
    n_px, n_py = lax.axis_size("px"), lax.axis_size("py")
    devices = n_px * n_py
    local = local_rows * local_cols
    rows = 2 * local * illum_count
    total_cols = local_cols * n_py
    patches = local_rows * n_px * total_cols
    rcv_count = far_map.shape[1]
    tile = rcv_count // n_px
    block = 2 * local
    axes = ("px", "py")
    vmem, hbm = pltpu.VMEM, pltpu.HBM

    def like(*arrays):
        scratch = [pltpu.VMEM(a.shape, a.dtype) for a in arrays]
        return scratch + [pltpu.SemaphoreType.DMA((len(arrays),))]

    def shape(*dims, dtype=BF16):
        return jax.ShapeDtypeStruct(dims, dtype)

    sent_width = 3 * unit_count + 128
    sources = (
        currents_in.reshape(rows, unit_count),
        reflect,
        pair_weight,
        partners,
        partner_count,
        jnp.transpose(centres, (1, 2, 0)),
    )
    packed = call(
        functools.partial(pack_kernel, total_cols, (n_px, n_py)),
        "pack",
        shape(devices, local, sent_width),
        sources,
        [hbm] * 6,
        like(*sources),
    )
    got = lax.all_to_all(packed, axes, 0, 0, tiled=True)
    depth, head = far_map.shape[0], rcv_count // 2
    rad, far_head, long_table = call(
        table_kernel,
        "table",
        (shape(*rad_pattern.shape), shape(depth, head), shape(tile, 2 * tile)),
        (rad_pattern, far_map),
        [hbm] * 2,
        [pltpu.SemaphoreType.DMA((2,))],
        cost=pl.CostEstimate(flops=10**7, bytes_accessed=4 * 10**6, transcendentals=0),
    )
    answer, final, kept = call(
        functools.partial(bounce_kernel, (n_px, n_py), (local_rows, local_cols)),
        "bounces",
        (shape(rows, unit_count), shape(rows, unit_count), shape(patches, 128, dtype=F32)),
        (got, rad, spectral_dirs, far_head),
        [vmem] * 3 + [pl.ANY],
        [pltpu.VMEM((rows, unit_count), BF16), pltpu.SemaphoreType.DMA((1,))],
        left=(0,),
    )
    back = lax.all_to_all(answer.reshape(devices, block, unit_count), axes, 0, 0, tiled=True)
    half = n_px // 2
    same, other = call(
        functools.partial(image_kernel, math.sqrt(0.125 / (patches * rcv_count))),
        "image",
        (shape(half, tile, dtype=F32), shape(half, tile, dtype=F32)),
        (final, kept, long_table, receiver_dirs, far_head, far_map),
        [vmem] * 5 + [hbm],
        [
            pltpu.VMEM((n_px, tile), F32),
            pltpu.VMEM((depth, rcv_count - head), BF16),
            pltpu.VMEM((patches, rcv_count - head), F32),
            pltpu.VMEM((patches, rcv_count - head), F32),
            pltpu.SemaphoreType.DMA((1,)),
        ],
        cost=pl.CostEstimate(flops=2 * 10**9, bytes_accessed=4 * 10**6, transcendentals=0),
    )

    def swapped(array, bits):
        return lax.ppermute(array, "px", [(i, i ^ bits) for i in range(n_px)])

    pair = jnp.concatenate([same, swapped(other, 1)], axis=0)
    pairs = [pair] + [swapped(pair, bits) for bits in range(2, n_px, 2)]
    currents, image = call(
        functools.partial(unpack_kernel, local, (n_px, n_py)),
        "unpack",
        (shape(rows, unit_count), shape(illum_count // n_py, tile, dtype=F32)),
        (back.reshape(rows, unit_count), *pairs),
        [vmem] * (1 + len(pairs)),
    )
    return (currents.reshape(currents_in.shape), image)


def fits(mesh):
    def check(currents_in, far_map):
        n_px, n_py = mesh.shape["px"], mesh.shape["py"]
        total_rows, total_cols, _, illum_count, unit_count = currents_in.shape
        local = (total_rows // n_px) * (total_cols // n_py)
        return (
            illum_count == n_px * n_py
            and local == 4
            and n_px == 8
            and unit_count % 256 == 0
            and far_map.shape[1] == n_px * 256
            and total_cols > 2 * COL_REACH
        )

    return check


def solution(mesh):
    in_specs = (
        P("px", "py", None, None, None),
        P(),
        P(),
        P("px", "py", None),
        P(None, "px", "py"),
        P(),
        P(),
        P("px", "py", None),
        P("px", "py"),
        P("px", "py", None),
    )
    out_specs = (P("px", "py", None, None, None), P("py", "px"))
    check = fits(mesh)

    def run(*args):
        local = illumination_sharded if check(args[0], args[2]) else patch_sharded
        mapped = jax.shard_map(
            local, mesh=mesh, in_specs=in_specs, out_specs=out_specs, check_vma=False
        )
        return mapped(*args)

    return run
```

```python
import functools
import math

import jax
import jax.numpy as jnp
import numpy as np
from jax import lax
from jax.experimental import pallas as pl
from jax.experimental.pallas import tpu as pltpu
from jax.sharding import PartitionSpec as P

SLOTS = 12
ROW_REACH = 1
COL_REACH = 2
OFFSETS = [
    (a, b)
    for a in range(-ROW_REACH, ROW_REACH + 1)
    for b in range(-COL_REACH, COL_REACH + 1)
]
F32 = jnp.float32
BF16 = jnp.bfloat16
HIGH = lax.Precision.HIGHEST
MIB = 1024 * 1024


def padded(block, sides, width, periodic):
    for axis, dim in sides:
        count = lax.axis_size(axis)
        forward = [(i, i + 1) for i in range(count - 1)]
        if periodic:
            forward.append((count - 1, 0))
        backward = [(target, source) for source, target in forward]
        low = lax.ppermute(
            lax.slice_in_dim(block, block.shape[dim] - width, None, axis=dim), axis, forward
        )
        high = lax.ppermute(lax.slice_in_dim(block, 0, width, axis=dim), axis, backward)
        block = jnp.concatenate([low, block, high], axis=dim)
    return block


def combined(rad_pattern):
    upper = jnp.concatenate([rad_pattern[0], rad_pattern[1]], axis=1)
    lower = jnp.concatenate([-rad_pattern[1], rad_pattern[0]], axis=1)
    return jnp.concatenate([upper, lower], axis=0)


def radiate(currents, rad_big):
    row_count, col_count, _, illum_count, unit_count = currents.shape
    stacked = jnp.concatenate([currents[:, :, 0], currents[:, :, 1]], axis=-1)
    flat_rows = stacked.reshape(row_count * col_count * illum_count, 2 * unit_count)
    spectra = jnp.dot(flat_rows, rad_big, preferred_element_type=F32)
    return spectra.reshape(row_count, col_count, illum_count, -1)


def receive(arriving, rad_big):
    row_count, col_count, illum_count, double = arriving.shape
    flat_rows = arriving.reshape(-1, double)
    answer = lax.dot_general(
        flat_rows, rad_big, (((1,), (1,)), ((), ())), preferred_element_type=F32
    )
    return answer.reshape(row_count, col_count, illum_count, -1)


def partner_sum(halo_flat, slot_index, weights):
    height = halo_flat.shape[0]
    onehot = slot_index[:, :, None] == jnp.arange(height, dtype=jnp.int32)[None, None, :]
    coef = jnp.sum(jnp.where(onehot, weights[:, :, None].astype(F32), 0.0), axis=1).astype(BF16)
    return jnp.dot(coef, halo_flat, preferred_element_type=F32)


def bounce(current_now, currents_in, rad_big, reflect, cosine, sine_part, plan):
    row_count, col_count, _, illum_count, unit_count = current_now.shape
    spectra = radiate(current_now, rad_big)
    half_width = spectra.shape[-1] // 2
    spec_re = spectra[..., :half_width]
    spec_im = spectra[..., half_width:]
    out_re = spec_re * cosine + spec_im * sine_part
    out_im = spec_im * cosine - spec_re * sine_part
    outgoing = jnp.stack([out_re, out_im], axis=2).astype(BF16)
    girth_block = padded(outgoing, (("py", 1),), COL_REACH, True)
    slot_index, weights = plan
    rim_block = padded(girth_block, (("px", 0),), ROW_REACH, False)
    halo_flat = rim_block.reshape(-1, 2 * illum_count * half_width)
    collected = partner_sum(halo_flat, slot_index, weights)
    collected = collected.reshape(row_count, col_count, 2, illum_count, half_width)
    col_re = collected[:, :, 0]
    col_im = collected[:, :, 1]
    arr_re = col_re * cosine - col_im * sine_part
    arr_im = col_re * sine_part + col_im * cosine
    arriving = jnp.concatenate([arr_re, -arr_im], axis=-1).astype(BF16)
    answer = receive(arriving, rad_big)
    received = jnp.stack([answer[..., :unit_count], -answer[..., unit_count:]], axis=2)
    updated = currents_in.astype(F32) + reflect[:, :, None, None, :] * received
    return updated.astype(BF16)


def patch_sharded(
    currents_in,
    rad_pattern,
    far_map,
    reflect,
    centres,
    spectral_dirs,
    receiver_dirs,
    partners,
    partner_count,
    pair_weight,
):
    row_count, col_count = partner_count.shape
    high = HIGH
    rad_big = combined(rad_pattern)
    phi = jnp.einsum("dm,dab->abm", spectral_dirs, centres, precision=high)
    cosine = jnp.cos(phi)[:, :, None, :]
    sine_part = jnp.sin(phi)[:, :, None, :]
    total_cols = col_count * lax.axis_size("py")
    total_rows = row_count * lax.axis_size("px")
    base_row = lax.axis_index("px") * row_count
    base_col = lax.axis_index("py") * col_count
    across = col_count + 2 * COL_REACH
    local_col = jnp.arange(col_count, dtype=jnp.int32)[None, :, None]
    live = jnp.arange(SLOTS, dtype=jnp.int32)[None, None, :] < partner_count[:, :, None]
    masked_weight = jnp.where(live, pair_weight, jnp.zeros_like(pair_weight))
    part_row = partners // total_cols
    part_col = partners % total_cols
    near_row = part_row - base_row
    near_col = (part_col - base_col - local_col + COL_REACH) % total_cols + local_col
    slot_index = ((near_row + ROW_REACH) * across + near_col).reshape(row_count * col_count, SLOTS)
    weights = masked_weight.reshape(row_count * col_count, SLOTS)
    plan = (slot_index, weights)
    current_now = currents_in
    for bounce_id in range(2):
        current_now = bounce(current_now, currents_in, rad_big, reflect, cosine, sine_part, plan)
    spectra = radiate(current_now, rad_big).astype(BF16)
    illum_count = spectra.shape[2]
    dir_count = far_map.shape[0]
    rcv_count = far_map.shape[1]
    beams = jnp.dot(spectra.reshape(-1, dir_count), far_map, preferred_element_type=F32)
    beams = beams.reshape(row_count, col_count, illum_count, 2, rcv_count)
    view = jnp.einsum("dr,dab->abr", receiver_dirs, centres, precision=high)
    cos_view = jnp.cos(view)[:, :, None, :]
    sin_view = jnp.sin(view)[:, :, None, :]
    beam_re = beams[:, :, :, 0]
    beam_im = beams[:, :, :, 1]
    far_re = jnp.sum(beam_re * cos_view - beam_im * sin_view, axis=(0, 1))
    far_im = jnp.sum(beam_re * sin_view + beam_im * cos_view, axis=(0, 1))
    factor = 1.0 / math.sqrt(total_rows * total_cols)
    far_part = jnp.stack([far_re, far_im]) * factor
    owned_far = lax.psum(
        lax.psum_scatter(far_part.astype(BF16), "py", scatter_dimension=1, tiled=True), "px"
    ).astype(F32)
    bin_width = rcv_count // lax.axis_size("px")
    rcv_ids = jnp.arange(rcv_count, dtype=jnp.int32)[:, None]
    bin_ids = lax.axis_index("px") * bin_width + jnp.arange(bin_width, dtype=jnp.int32)[None, :]
    turn_angle = (rcv_ids * bin_ids % rcv_count).astype(F32) * (2.0 * math.pi / rcv_count)
    norm_factor = 1.0 / math.sqrt(rcv_count)
    cos_table = jnp.cos(turn_angle) * norm_factor
    sin_table = jnp.sin(turn_angle) * norm_factor
    image_re = jnp.dot(owned_far[0], cos_table, precision=high) + jnp.dot(
        owned_far[1], sin_table, precision=high
    )
    image_im = jnp.dot(owned_far[1], cos_table, precision=high) - jnp.dot(
        owned_far[0], sin_table, precision=high
    )
    isar_image = 0.125 * (image_re * image_re + image_im * image_im)
    return (current_now, isar_image)


def turn_polynomials():
    grid = np.linspace(0.0, 0.25, 4001)
    safe = np.where(grid > 0, np.sqrt(grid), 1.0)
    sine_over = np.where(grid > 0, np.sin(2 * np.pi * safe) / safe, 2 * np.pi)
    cosine = np.cos(2 * np.pi * np.sqrt(grid))
    make = np.polynomial.chebyshev.Chebyshev.fit
    power = np.polynomial.Polynomial
    sine_fit = make(grid, sine_over, 5).convert(kind=power).coef
    cosine_fit = make(grid, cosine, 5).convert(kind=power).coef
    return [float(c) for c in sine_fit], [float(c) for c in cosine_fit]


SINE_FIT, COSINE_FIT = turn_polynomials()


def horner(coefs, x):
    value = jnp.full_like(x, coefs[-1])
    for c in coefs[-2::-1]:
        value = value * x + c
    return value


def cos_sin(turns):
    frac = turns - jnp.floor(turns + 0.5)
    square = frac * frac
    return horner(COSINE_FIT, square), frac * horner(SINE_FIT, square)


def dot(left, right):
    return jnp.dot(left, right, preferred_element_type=F32)


def dot_t(left, right):
    return lax.dot_general(left, right, (((1,), (1,)), ((), ())), preferred_element_type=F32)


def sorter(rows, outer, inner, outer_at=lambda o: o, inner_at=lambda i: i):
    out_id = lax.broadcasted_iota(jnp.int32, (rows, rows), 0)
    in_id = lax.broadcasted_iota(jnp.int32, (rows, rows), 1)
    i = out_id // (2 * outer)
    part = (out_id // outer) % 2
    o = out_id % outer
    column = (outer_at(o) * 2 + part) * inner + inner_at(i)
    return jnp.where(in_id == column, 1.0, 0.0).astype(BF16)


def swapped_digits(value, high, low):
    return value % low * high + value // low


def part_sorter(rows, inner, back):
    first = lax.broadcasted_iota(jnp.int32, (rows, rows), 1 if back else 0)
    second = lax.broadcasted_iota(jnp.int32, (rows, rows), 0 if back else 1)
    half = rows // 2
    part = first // half
    o = (first % half) // inner
    i = first % inner
    return jnp.where(second == (o * 2 + part) * inner + i, 1.0, 0.0).astype(BF16)


def fetch(pairs, sems):
    copies = [
        pltpu.make_async_copy(source, target, sems.at[n])
        for n, (source, target) in enumerate(pairs)
    ]
    for copy in copies:
        copy.start()
    return copies


def pack_kernel(
    total_cols,
    grid_shape,
    cur_hbm,
    reflect_hbm,
    weight_hbm,
    partners_hbm,
    count_hbm,
    centres_hbm,
    out,
    cur,
    reflect,
    weight,
    partners,
    count,
    centres,
    sems,
):
    copies = fetch(
        [
            (cur_hbm, cur),
            (reflect_hbm, reflect),
            (partners_hbm, partners),
            (weight_hbm, weight),
            (count_hbm, count),
            (centres_hbm, centres),
        ],
        sems,
    )
    rows = cur.shape[0]
    local_rows, local_cols, unit_count = reflect.shape
    local = local_rows * local_cols
    base_row = lax.axis_index("px") * local_rows
    base_col = lax.axis_index("py") * local_cols
    row_id = lax.broadcasted_iota(jnp.int32, (rows, rows), 0)
    in_id = lax.broadcasted_iota(jnp.int32, (rows, rows), 1)
    illum_count = rows // (2 * local)
    part, chunk, o = row_id // (rows // 2), row_id % (rows // 2) // local, row_id % local
    column = (o * 2 + part) * illum_count + swapped_digits(chunk, *grid_shape)
    order = jnp.where(in_id == column, 1.0, 0.0).astype(BF16)
    lane = lax.broadcasted_iota(jnp.int32, (local, 128), 1)
    row = lax.broadcasted_iota(jnp.int32, (local, 128), 0)
    patch_row = base_row + row // local_cols
    patch_col = base_col + row % local_cols
    target = jnp.full((local, 128), -1, jnp.int32)
    for o, (a, b) in enumerate(OFFSETS):
        col = patch_col + b
        col = jnp.where(col < 0, col + total_cols, col)
        col = jnp.where(col >= total_cols, col - total_cols, col)
        target = jnp.where(lane == o, (patch_row + a) * total_cols + col, target)
    for copy in copies[1:]:
        copy.wait()
    ids = partners[...].reshape(local, SLOTS)
    weights = weight[...].astype(F32).reshape(local, SLOTS)
    spots = centres[...].reshape(local, 3)
    counts = count[...]
    live = jnp.zeros((local, 128), jnp.int32)
    for r in range(local_rows):
        for c in range(local_cols):
            live = jnp.where(row == r * local_cols + c, counts[r : r + 1, c : c + 1], live)
    small = jnp.zeros((local, 128), F32)
    for s in range(SLOTS):
        hit = (ids[:, s : s + 1] == target) & (live > s)
        small = small + jnp.where(hit, weights[:, s : s + 1], 0.0)
    first = len(OFFSETS)
    for d in range(3):
        spot = spots[:, d : d + 1]
        top = spot.astype(BF16).astype(F32)
        rest = spot - top
        middle = rest.astype(BF16).astype(F32)
        small = jnp.where(lane == first + 3 * d, top, small)
        small = jnp.where(lane == first + 3 * d + 1, middle, small)
        small = jnp.where(lane == first + 3 * d + 2, rest - middle, small)
    refl = reflect[...].reshape(local, unit_count)
    tail = jnp.concatenate([refl, small], axis=1).astype(BF16)
    for n in range(illum_count):
        out[n, :, 2 * unit_count :] = tail
    copies[0].wait()
    both = dot(order, cur[...])
    both = jnp.concatenate([both[: rows // 2], both[rows // 2 :]], axis=1)
    for n in range(illum_count):
        out[n, :, : 2 * unit_count] = both[local * n : local * (n + 1)].astype(BF16)


def table_kernel(
    local, grid_shape, rad_hbm, far_hbm, rad, far_head, long_table, to_blocks, to_rows, sems
):
    head = far_hbm.at[:, : far_head.shape[1]]
    copies = fetch([(rad_hbm, rad), (head, far_head)], sems)
    tile = long_table.shape[0]
    row = lax.broadcasted_iota(jnp.int32, (tile, tile), 0)
    column = lax.broadcasted_iota(jnp.int32, (tile, tile), 1)
    cosine, sine = cos_sin(((row * column) % tile).astype(F32) * (1.0 / tile))
    long_table[:, :tile] = cosine.astype(BF16)
    long_table[:, tile:] = sine.astype(BF16)
    rows = to_rows.shape[0]
    n_px, n_py = grid_shape
    to_blocks[...] = part_sorter(rows, local, True)
    to_rows[...] = sorter(
        rows, rows // (2 * local), local, outer_at=lambda o: swapped_digits(o, n_py, n_px)
    )
    for copy in copies:
        copy.wait()


def centres_of(small):
    first = len(OFFSETS)
    centre = []
    for d in range(3):
        at = first + 3 * d
        value = small[:, at : at + 1] + small[:, at + 1 : at + 2] + small[:, at + 2 : at + 3]
        centre.append(value * (0.5 / math.pi))
    return centre


def turns(centre, dirs):
    return centre[0] * dirs[0:1] + centre[1] * dirs[1:2] + centre[2] * dirs[2:3]


def spectrum(current, rad):
    patches = current.shape[0] // 2
    first_part = dot(current, rad[0])
    second_part = dot(current, rad[1])
    return (
        first_part[:patches] - second_part[patches:],
        second_part[:patches] + first_part[patches:],
    )


def bounce_kernel(
    grid_shape,
    local_shape,
    got,
    rad,
    spectral_dirs,
    to_blocks,
    far_head,
    out_hbm,
    final,
    kept,
    out,
    sems,
):
    del far_head
    unit_count = rad.shape[1]
    patches = got.shape[0] * got.shape[1]
    rows = 2 * patches
    local_rows, local_cols = local_shape
    local = local_rows * local_cols
    n_px, n_py = grid_shape
    total_cols = n_py * local_cols
    whole = jnp.concatenate([got[n].astype(F32) for n in range(got.shape[0])], axis=0)
    start = jnp.concatenate([whole[:, :unit_count], whole[:, unit_count : 2 * unit_count]], axis=0)
    reflect = whole[:, 2 * unit_count : 3 * unit_count]
    small = whole[:, 3 * unit_count :]
    kept[...] = small

    def place(axis):
        ids = lax.broadcasted_iota(jnp.int32, (patches, patches), axis)
        device, within = ids // local, ids % local
        return (
            device // n_py * local_rows + within // local_cols,
            device % n_py * local_cols + within % local_cols,
        )

    (here_row, here_col), (there_row, there_col) = place(0), place(1)
    down = there_row - here_row
    across = there_col - here_col
    across = jnp.where(across > COL_REACH, across - total_cols, across)
    across = jnp.where(across < -COL_REACH, across + total_cols, across)
    near = (down >= -ROW_REACH) & (down <= ROW_REACH)
    near = near & (across >= -COL_REACH) & (across <= COL_REACH)
    offset = (down + ROW_REACH) * (2 * COL_REACH + 1) + across + COL_REACH
    offset = jnp.where(near, offset, -1)
    coef = jnp.zeros((patches, patches), F32)
    for o in range(len(OFFSETS)):
        coef = jnp.where(offset == o, small[:, o : o + 1], coef)
    coef = coef.astype(BF16)
    cosine, sine = cos_sin(turns(centres_of(small), spectral_dirs[...]))
    current = start.astype(BF16)
    for _ in range(2):
        spec_re, spec_im = spectrum(current, rad)
        outgoing = jnp.concatenate(
            [spec_re * cosine + spec_im * sine, spec_im * cosine - spec_re * sine], axis=1
        ).astype(BF16)
        collected = dot(coef, outgoing)
        width = collected.shape[1] // 2
        col_re = collected[:, :width]
        col_im = collected[:, width:]
        arriving = jnp.concatenate(
            [col_re * cosine - col_im * sine, col_re * sine + col_im * cosine], axis=0
        ).astype(BF16)
        first_part = dot_t(arriving, rad[0])
        second_part = dot_t(arriving, rad[1])
        recv_re = first_part[:patches] - second_part[patches:]
        recv_im = second_part[:patches] + first_part[patches:]
        current = jnp.concatenate(
            [start[:patches] + reflect * recv_re, start[patches:] + reflect * recv_im], axis=0
        ).astype(BF16)
    out[...] = dot(to_blocks[...], current).astype(BF16)
    out_copy = pltpu.make_async_copy(out, out_hbm, sems.at[0])
    out_copy.start()
    final[...] = jnp.concatenate(spectrum(current, rad), axis=0).astype(BF16)
    out_copy.wait()


def image_kernel(
    root_scale,
    final,
    kept,
    long_table,
    receiver_dirs,
    far_head,
    far_hbm,
    same,
    other,
    image,
    far_rest,
    cos_rest,
    sin_rest,
    sems,
):
    head = far_head.shape[1]
    rest_copy = pltpu.make_async_copy(far_hbm.at[:, head:], far_rest, sems.at[0])
    rest_copy.start()
    splits, tile = image.shape
    patches = kept.shape[0]
    centre = centres_of(kept[...])
    far_re, far_im = [], []
    for t in range(splits):
        cut = slice(tile * t, tile * (t + 1))
        if tile * t == head:
            for n in range(t, splits):
                at = slice(tile * n, tile * (n + 1))
                to = slice(tile * (n - t), tile * (n - t + 1))
                cos_rest[:, to], sin_rest[:, to] = cos_sin(turns(centre, receiver_dirs[:, at]))
            rest_copy.wait()
        if tile * t < head:
            beams = dot(final[...], far_head[:, cut])
        else:
            beams = dot(final[...], far_rest[:, tile * t - head : tile * (t + 1) - head])
        if tile * t < head:
            cos_view, sin_view = cos_sin(turns(centre, receiver_dirs[:, cut]))
        else:
            to = slice(tile * t - head, tile * (t + 1) - head)
            cos_view, sin_view = cos_rest[:, to], sin_rest[:, to]
        beam_re = beams[:patches]
        beam_im = beams[patches:]
        far_re.append(jnp.sum(beam_re * cos_view - beam_im * sin_view, axis=0, keepdims=True))
        far_im.append(jnp.sum(beam_re * sin_view + beam_im * cos_view, axis=0, keepdims=True))
    row = lax.broadcasted_iota(jnp.int32, (splits, 128), 0)
    column = lax.broadcasted_iota(jnp.int32, (splits, 128), 1)
    short_cos, short_sin = cos_sin((row * column % splits).astype(F32) * (1.0 / splits))
    row = lax.broadcasted_iota(jnp.int32, (splits, tile), 0)
    column = lax.broadcasted_iota(jnp.int32, (splits, tile), 1)
    twist_cos, twist_sin = cos_sin((row * column).astype(F32) * (1.0 / (splits * tile)))
    mid_re = jnp.zeros((splits, tile), F32)
    mid_im = jnp.zeros((splits, tile), F32)
    for t in range(splits):
        c = short_cos[:, t : t + 1] * root_scale
        s = short_sin[:, t : t + 1] * root_scale
        mid_re = mid_re + (c * far_re[t] + s * far_im[t])
        mid_im = mid_im + (c * far_im[t] - s * far_re[t])
    tw_re = mid_re * twist_cos + mid_im * twist_sin
    tw_im = mid_im * twist_cos - mid_re * twist_sin
    both = jnp.concatenate([tw_re, tw_im], axis=0)
    upper = both.astype(BF16)
    lower = (both - upper.astype(F32)).astype(BF16)
    answer = dot(jnp.concatenate([upper, lower], axis=0), long_table[...])
    answer = answer[: 2 * splits] + answer[2 * splits :]
    image_re = answer[:splits, :tile] + answer[splits:, tile:]
    image_im = answer[splits:, :tile] - answer[:splits, tile:]
    power = image_re * image_re + image_im * image_im
    each = tile // splits
    upper = power.astype(BF16)
    lower = (power - upper.astype(F32)).astype(BF16)
    lane = lax.broadcasted_iota(jnp.int32, (2 * splits, tile), 1)
    row = lax.broadcasted_iota(jnp.int32, (2 * splits, tile), 0)
    fast = jnp.where(lane % splits == row % splits, 1.0, 0.0).astype(BF16)
    spread = lax.dot_general(
        jnp.concatenate([upper, lower], axis=0),
        fast,
        (((0,), (0,)), ((), ())),
        preferred_element_type=F32,
    )
    row = lax.broadcasted_iota(jnp.int32, (tile, tile), 0)
    column = lax.broadcasted_iota(jnp.int32, (tile, tile), 1)
    spread = jnp.where(row % each == column // splits, spread, 0.0)
    image[...] = jnp.sum(spread.reshape(splits, each, tile), axis=1)
    me = lax.axis_index("px")
    for n in range(splits // 2):
        same[n : n + 1, :] = image[pl.ds(me ^ (2 * n), 1), :]
        other[n : n + 1, :] = image[pl.ds(me ^ (2 * n + 1), 1), :]


def unpack_kernel(n_px, got, order, *refs):
    pairs, (currents, image) = refs[:-2], refs[-2:]
    currents[...] = dot(order[...], got[...]).astype(BF16)
    me = lax.axis_index("px")
    row = lax.broadcasted_iota(jnp.int32, image.shape, 0)
    whole = jnp.zeros(image.shape, F32)
    for n in range(n_px):
        at = n // 2 + n % 2 * (n_px // 2)
        mine = pairs[n // 2][at : at + 1, :]
        whole = jnp.where(row == (me ^ n), mine, whole)
    image[...] = whole


def call(kernel, name, outs, operands, spaces, scratch=(), cost=None, limit=32, left=()):
    specs = jax.tree.map(lambda _: pl.BlockSpec(memory_space=pltpu.VMEM), outs)
    if left:
        specs = tuple(
            pl.BlockSpec(memory_space=pl.ANY) if n in left else s for n, s in enumerate(specs)
        )
    operands = [
        pltpu.with_memory_space_constraint(a, pltpu.HBM) if m is pltpu.HBM else a
        for a, m in zip(operands, spaces)
    ]
    return pl.pallas_call(
        kernel,
        out_shape=outs,
        in_specs=[pl.BlockSpec(memory_space=m) for m in spaces],
        out_specs=specs,
        scratch_shapes=list(scratch),
        compiler_params=pltpu.CompilerParams(vmem_limit_bytes=limit * MIB),
        cost_estimate=cost,
        name=name,
    )(*operands)


def illumination_sharded(
    currents_in,
    rad_pattern,
    far_map,
    reflect,
    centres,
    spectral_dirs,
    receiver_dirs,
    partners,
    partner_count,
    pair_weight,
):
    local_rows, local_cols, _, illum_count, unit_count = currents_in.shape
    n_px, n_py = lax.axis_size("px"), lax.axis_size("py")
    devices = n_px * n_py
    local = local_rows * local_cols
    rows = 2 * local * illum_count
    total_cols = local_cols * n_py
    patches = local_rows * n_px * total_cols
    rcv_count = far_map.shape[1]
    tile = rcv_count // n_px
    block = 2 * local
    axes = ("px", "py")
    vmem, hbm = pltpu.VMEM, pltpu.HBM

    def like(*arrays):
        scratch = [pltpu.VMEM(a.shape, a.dtype) for a in arrays]
        return scratch + [pltpu.SemaphoreType.DMA((len(arrays),))]

    def shape(*dims, dtype=BF16):
        return jax.ShapeDtypeStruct(dims, dtype)

    sent_width = 3 * unit_count + 128
    sources = (
        currents_in.reshape(rows, unit_count),
        reflect,
        pair_weight,
        partners,
        partner_count,
        jnp.transpose(centres, (1, 2, 0)),
    )
    packed = call(
        functools.partial(pack_kernel, total_cols, (n_px, n_py)),
        "pack",
        shape(devices, local, sent_width),
        sources,
        [hbm] * 6,
        like(*sources),
    )
    got = lax.all_to_all(packed, axes, 0, 0, tiled=True)
    depth, head = far_map.shape[0], rcv_count // 2
    rad, far_head, long_table, to_blocks, to_rows = call(
        functools.partial(table_kernel, local, (n_px, n_py)),
        "table",
        (
            shape(*rad_pattern.shape),
            shape(depth, head),
            shape(tile, 2 * tile),
            shape(rows, rows),
            shape(rows, rows),
        ),
        (rad_pattern, far_map),
        [hbm] * 2,
        [pltpu.SemaphoreType.DMA((2,))],
        cost=pl.CostEstimate(flops=10**7, bytes_accessed=4 * 10**6, transcendentals=0),
    )
    answer, final, kept = call(
        functools.partial(bounce_kernel, (n_px, n_py), (local_rows, local_cols)),
        "bounces",
        (shape(rows, unit_count), shape(rows, unit_count), shape(patches, 128, dtype=F32)),
        (got, rad, spectral_dirs, to_blocks, far_head),
        [vmem] * 4 + [pl.ANY],
        [pltpu.VMEM((rows, unit_count), BF16), pltpu.SemaphoreType.DMA((1,))],
        left=(0,),
    )
    back = lax.all_to_all(answer.reshape(devices, block, unit_count), axes, 0, 0, tiled=True)
    half = n_px // 2
    same, other = call(
        functools.partial(image_kernel, math.sqrt(0.125 / (patches * rcv_count))),
        "image",
        (shape(half, tile, dtype=F32), shape(half, tile, dtype=F32)),
        (final, kept, long_table, receiver_dirs, far_head, far_map),
        [vmem] * 5 + [hbm],
        [
            pltpu.VMEM((n_px, tile), F32),
            pltpu.VMEM((depth, rcv_count - head), BF16),
            pltpu.VMEM((patches, rcv_count - head), F32),
            pltpu.VMEM((patches, rcv_count - head), F32),
            pltpu.SemaphoreType.DMA((1,)),
        ],
        cost=pl.CostEstimate(flops=2 * 10**9, bytes_accessed=4 * 10**6, transcendentals=0),
    )

    def swapped(array, bits):
        return lax.ppermute(array, "px", [(i, i ^ bits) for i in range(n_px)])

    pair = jnp.concatenate([same, swapped(other, 1)], axis=0)
    pairs = [pair] + [swapped(pair, bits) for bits in range(2, n_px, 2)]
    currents, image = call(
        functools.partial(unpack_kernel, n_px),
        "unpack",
        (shape(rows, unit_count), shape(illum_count // n_py, tile, dtype=F32)),
        (back.reshape(rows, unit_count), to_rows, *pairs),
        [vmem] * (2 + len(pairs)),
    )
    return (currents.reshape(currents_in.shape), image)


def fits(mesh):
    def check(currents_in, far_map):
        n_px, n_py = mesh.shape["px"], mesh.shape["py"]
        total_rows, total_cols, _, illum_count, unit_count = currents_in.shape
        local = (total_rows // n_px) * (total_cols // n_py)
        return (
            illum_count == n_px * n_py
            and local == 4
            and n_px == 8
            and unit_count % 256 == 0
            and far_map.shape[1] == n_px * 256
            and total_cols > 2 * COL_REACH
        )

    return check


def solution(mesh):
    in_specs = (
        P("px", "py", None, None, None),
        P(),
        P(),
        P("px", "py", None),
        P(None, "px", "py"),
        P(),
        P(),
        P("px", "py", None),
        P("px", "py"),
        P("px", "py", None),
    )
    out_specs = (P("px", "py", None, None, None), P("py", "px"))
    check = fits(mesh)

    def run(*args):
        local = illumination_sharded if check(args[0], args[2]) else patch_sharded
        mapped = jax.shard_map(
            local, mesh=mesh, in_specs=in_specs, out_specs=out_specs, check_vma=False
        )
        return mapped(*args)

    return run
```
